32 devices in a mesh: section: 2 (over x), dp: 16 (over z, y, core).
Axes of the slice: x: 2, y: 2, z: 4, core: 2. Of those that a mesh axis runs over, the one named last changes fastest.
Arguments:
- tokens: bfloat16 [2, 16, 512, 1024], P(None, 'dp'), may hold values from -6 to 6
- doc_lengths: int32 [2, 16, 4], P(None, 'dp'), may hold values from 1 to 256, 512 in all within a row
- cotangent: bfloat16 [2, 16, 512, 1024], P(None, 'dp'), may hold values from -6 to 6
- qkv_weight: bfloat16 [2, 1024, 3072], P('section'), may hold values from -0.1875 to 0.1875
- out_weight: bfloat16 [2, 1024, 1024], P('section'), may hold values from -1 to 1
- ff1_weight: bfloat16 [2, 1024, 4096], P('section'), may hold values from -0.1875 to 0.1875
- ff2_weight: bfloat16 [2, 4096, 1024], P('section'), may hold values from -0.09375 to 0.09375
- first_gain: float32 [2, 1024], P('section'), may hold values from 0.5 to 1.5
- second_gain: float32 [2, 1024], P('section'), may hold values from 0.5 to 1.5
- qv_bias: float32 [2, 2048], P('section'), may hold values from -3 to 3
- out_bias: float32 [2, 1024], P('section'), may hold values from -3 to 3
- first_shift: float32 [2, 1024], P('section'), may hold values from -3 to 3
- ff1_bias: float32 [2, 4096], P('section'), may hold values from -3 to 3
- ff2_bias: float32 [2, 1024], P('section'), may hold values from -3 to 3
- second_shift: float32 [2, 1024], P('section'), may hold values from -3 to 3
Outputs:
- layer_out: bfloat16 [2, 2, 16, 512, 1024], P('section', None, 'dp')
- layer_in_grad: bfloat16 [2, 2, 16, 512, 1024], P('section', None, 'dp')
- qv_bias_grad: float32 [2, 2048], P('section')
- out_bias_grad: float32 [2, 1024], P('section')
- first_shift_grad: float32 [2, 1024], P('section')
- ff1_bias_grad: float32 [2, 4096], P('section')
- ff2_bias_grad: float32 [2, 1024], P('section')
- second_shift_grad: float32 [2, 1024], P('section')
The draws below stay inside these ranges and needn't reach their ends.
Inputs may be any that keep to these rules, and one draw needn't show every extreme that they name: `doc_lengths`: the 4 lengths of one packed row sum to 512.
All inputs are finite; a program needn't handle non-finite values.
Results may differ from the reference program's by a relative error of at most 0.02.
Values may be sent and summed in bfloat16 or wider, within the bound.
No kernel may reach another device: no remote copies, remote signals or barrier semaphores. Data moves between devices by JAX's collectives and lax.ppermute only.
A program may use at most 320 MiB of HBM per device.

```python
import math
import jax
import jax.numpy as jnp
import numpy as np
from jax import lax

D = 1024
HEADS = 16
HEAD_DIM = 64
FF = 4096
SEQ = 512
SEGS = 4
LONGEST = 256
MICRO = 2
BATCH = 16


def block_scale(own_key, extent, shards, least, high):
    loudness = 1.0
    for axis_at, blocks in shards:
        draws = jax.random.uniform(jax.random.fold_in(jax.random.fold_in(own_key, 6), axis_at), (blocks,), jnp.float32, least / len(shards), high / len(shards))
        loudness = loudness * jnp.repeat(jnp.exp(draws), extent[axis_at] // blocks).reshape((-1,) + (1,) * (len(extent) - 1 - axis_at))
    return loudness


def profile(count, total, reach, lean):
    weights = [(1 << 20) // math.isqrt(grade ** lean) + 1 for grade in range(2, count + 1)]
    spare, given = total - reach - (count - 1), [1] * (count - 1)
    while spare > 0:
        movable = [i for i in range(count - 1) if given[i] < reach]
        mass, left = sum([weights[i] for i in movable]), spare
        for i in movable:
            more = min(reach - given[i], max(1, left * weights[i] // mass), spare)
            given[i] = given[i] + more
            spare = spare - more
    return np.array([reach] + given)


def ragged_sizes(stream_key, count, total, bound, slope):
    if count == 2:
        one = jax.random.randint(stream_key, (), max(1, total - bound), min(bound, total - 1) + 1)
        return jnp.stack([one, total - one])
    sizes = jnp.asarray(profile(count, total, bound, slope), jnp.int32)
    twos = (count - 1) // 2
    giver, receiver = sizes[1:1 + 2 * twos:2], sizes[2:2 + 2 * twos:2]
    margin = jnp.minimum(giver - 1, bound - receiver)
    passed = jax.random.randint(jax.random.fold_in(stream_key, 1), (twos,), 0, 1 << 20) % (margin + 1)
    sizes = sizes.at[1:1 + 2 * twos:2].set(giver - passed).at[2:2 + 2 * twos:2].set(receiver + passed)
    return sizes[jax.random.permutation(jax.random.fold_in(stream_key, 2), count)]


def normal_values(own_key, dims, scale, most, pieces=(), held_as=jnp.bfloat16):
    loudness = block_scale(own_key, dims, pieces, -0.22, 0.18) if pieces else 1.0
    values = jax.random.normal(own_key, dims, jnp.float32) * scale * loudness
    return jnp.minimum(jnp.maximum(values, -most), most).astype(held_as)


def setup_inputs(seed: int = 0) -> dict:
    splits = jax.random.split(jax.random.key(seed), 16)
    tokens = normal_values(splits[0], (MICRO, BATCH, SEQ, D), 1.0, 6.0, ((1, 16),))
    doc_lengths = jax.vmap(lambda own: ragged_sizes(own, SEGS, SEQ, LONGEST, 2))(jax.random.split(splits[1], MICRO * BATCH)).reshape((MICRO, BATCH, SEGS)).astype(jnp.int32)
    cotangent = normal_values(splits[2], (MICRO, BATCH, SEQ, D), 1.0, 6.0, ((1, 16),))
    qkv_weight = normal_values(splits[3], (2, D, 3 * D), D ** -0.5, 0.1875, ((0, 2),))
    out_weight = normal_values(splits[4], (2, D, D), (D // 32) ** -0.5, 1.0, ((0, 2),))
    ff1_weight = normal_values(splits[5], (2, D, FF), D ** -0.5, 0.1875, ((0, 2),))
    ff2_weight = normal_values(splits[6], (2, FF, D), FF ** -0.5, 0.09375, ((0, 2),))
    first_gain = jnp.clip(1.0 + 0.1 * jax.random.normal(splits[7], (2, D), jnp.float32), 0.5, 1.5)
    second_gain = jnp.clip(1.0 + 0.1 * jax.random.normal(splits[8], (2, D), jnp.float32), 0.5, 1.5)
    qv_bias = normal_values(splits[9], (2, 2 * D), 0.5, 3.0, ((0, 2),), jnp.float32)
    out_bias = normal_values(splits[10], (2, D), 0.5, 3.0, ((0, 2),), jnp.float32)
    first_shift = normal_values(splits[11], (2, D), 0.5, 3.0, ((0, 2),), jnp.float32)
    ff1_bias = normal_values(splits[12], (2, FF), 0.5, 3.0, ((0, 2),), jnp.float32)
    ff2_bias = normal_values(splits[13], (2, D), 0.5, 3.0, ((0, 2),), jnp.float32)
    second_shift = normal_values(splits[14], (2, D), 0.5, 3.0, ((0, 2),), jnp.float32)
    return {"tokens": tokens, "doc_lengths": doc_lengths, "cotangent": cotangent, "qkv_weight": qkv_weight, "out_weight": out_weight, "ff1_weight": ff1_weight, "ff2_weight": ff2_weight, "first_gain": first_gain, "second_gain": second_gain, "qv_bias": qv_bias, "out_bias": out_bias, "first_shift": first_shift, "ff1_bias": ff1_bias, "ff2_bias": ff2_bias, "second_shift": second_shift}


@jax.custom_vjp
def low(v):
    return lax.optimization_barrier(v.astype(jnp.bfloat16)).astype(jnp.float32)

@jax.custom_vjp
def low_back(v):
    return v

def low_keep(v):
    return (low(v), None)

def low_pass(kept, grad):
    return (grad,)

def back_keep(v):
    return (v, None)

def back_low(kept, grad):
    return (low(grad),)
low.defvjp(low_keep, low_pass)
low_back.defvjp(back_keep, back_low)

def matmul(left, right):
    return jnp.einsum('bsk,kn->bsn', left, right, precision=lax.Precision.HIGHEST)

def norm_rows(summed, gain, shift):
    middle = lax.optimization_barrier(jnp.mean(summed, axis=-1, keepdims=True))
    centered = summed - middle
    variance = lax.optimization_barrier(jnp.mean(centered * centered, axis=-1, keepdims=True))
    return centered * lax.rsqrt(variance + 1e-05) * gain + shift

def segment_mask(lengths):
    ends = jnp.cumsum(lengths, axis=-1).astype(jnp.int32)
    places = jnp.arange(SEQ, dtype=jnp.int32)
    labels = lax.optimization_barrier(jnp.sum((places[None, :, None] >= ends[:, None, :]).astype(jnp.int32), axis=-1))
    return labels[:, :, None] == labels[:, None, :]

def layer(inputs, frozen, trained, which, allowed):
    qkv_weight, out_weight, ff1_weight, ff2_weight, first_gain, second_gain = [item[which] for item in frozen]
    qv_bias, out_bias, first_shift, ff1_bias, ff2_bias, second_shift = [item[which] for item in trained]
    rows = inputs.shape[0]
    mixed = matmul(low(inputs), qkv_weight)
    query = low_back(low(mixed[..., :D] + qv_bias[:D])).reshape(rows, SEQ, HEADS, HEAD_DIM)
    keys = low_back(low(mixed[..., D:2 * D])).reshape(rows, SEQ, HEADS, HEAD_DIM)
    states = low_back(low(mixed[..., 2 * D:] + qv_bias[D:])).reshape(rows, SEQ, HEADS, HEAD_DIM)
    scores = jnp.einsum('bqhd,bkhd->bhqk', query, keys, precision=lax.Precision.HIGHEST) * HEAD_DIM ** (-0.5)
    scores = low_back(scores)
    scores = jnp.where(allowed[:, None], scores, -1000000000.0)
    probs = jax.nn.softmax(scores, axis=-1)
    context = jnp.einsum('bhqk,bkhd->bqhd', low(probs), states, precision=lax.Precision.HIGHEST)
    context = low_back(low(context.reshape(rows, SEQ, D)))
    attended = low_back(matmul(context, out_weight) + out_bias)
    first = norm_rows(inputs + attended, first_gain, first_shift)
    hidden = low_back(matmul(low(first), ff1_weight) + ff1_bias)
    activated = low(jax.nn.gelu(hidden, approximate=False))
    branch = low_back(matmul(activated, ff2_weight) + ff2_bias)
    return norm_rows(first + branch, second_gain, second_shift)

def reference(tokens, doc_lengths, cotangent, qkv_weight, out_weight, ff1_weight, ff2_weight, first_gain, second_gain, qv_bias, out_bias, first_shift, ff1_bias, ff2_bias, second_shift):
    frozen = tuple((item.astype(jnp.float32) for item in (qkv_weight, out_weight, ff1_weight, ff2_weight, first_gain, second_gain)))
    trained = tuple((item.astype(jnp.float32) for item in (qv_bias, out_bias, first_shift, ff1_bias, ff2_bias, second_shift)))
    total_rows = MICRO * BATCH
    limit = max(1, 4096 // SEQ)
    block = 1
    for candidate in range(1, min(limit, total_rows) + 1):
        if total_rows % candidate == 0:
            block = candidate
    blocks = total_rows // block
    inputs = tokens.astype(jnp.float32).reshape(blocks, block, SEQ, D)
    lengths = doc_lengths.reshape(blocks, block, SEGS).astype(jnp.int32)
    upstream = cotangent.astype(jnp.float32).reshape(blocks, block, SEQ, D)
    offsets = jnp.zeros_like(inputs)

    def forward(params, values, extra):

        def one_block(carry, items):
            rows_in, row_lengths, offset = items
            allowed = segment_mask(row_lengths)
            first_out = layer(rows_in, frozen, params, 0, allowed)
            sent = low_back(low(first_out)) + offset
            second_out = layer(sent, frozen, params, 1, allowed)
            return (carry, (first_out, second_out))
        unused, outputs = lax.scan(jax.checkpoint(one_block), jnp.zeros((), jnp.float32), (values, lengths, extra))
        return outputs
    outputs, pullback = jax.vjp(forward, trained, inputs, offsets)
    first_all, second_all = outputs
    trained_grad, input_grad, offset_grad = pullback((jnp.zeros_like(first_all), upstream))
    shape = (MICRO, BATCH, SEQ, D)
    layer_out = jnp.stack([first_all.reshape(shape), second_all.reshape(shape)]).astype(jnp.bfloat16)
    layer_in_grad = jnp.stack([input_grad.reshape(shape), offset_grad.reshape(shape)]).astype(jnp.bfloat16)
    return (layer_out, layer_in_grad, trained_grad[0], trained_grad[1], trained_grad[2], trained_grad[3], trained_grad[4], trained_grad[5])
```

```python
import functools
import jax
import jax.numpy as jnp
from jax import lax
from jax.experimental import pallas as pl
from jax.experimental.pallas import tpu as pltpu
from jax.sharding import PartitionSpec as P

HEAD_DIM = 64
LANES = 128
GROUP = 256
TILE = 1024
VMEM_BYTES = 62 * 2**20
epsilon = 1e-05
masked_score = -1000000000.0
root_half = 0.7071067811865476
inverse_root_tau = 0.3989422804014327
f32 = jnp.float32
bf16 = jnp.bfloat16


def dot(left, right):
    return jnp.dot(left, right, preferred_element_type=f32)


def dot_back(left, right):
    return lax.dot_general(left, right, (((1,), (1,)), ((), ())), preferred_element_type=f32)


def beside(*parts):
    return jnp.concatenate(parts, axis=1)


def above(*parts):
    return jnp.concatenate(parts, axis=0)


def column_sum(value):
    return jnp.sum(value, axis=0, keepdims=True)


def row_norm(summed):
    middle = jnp.mean(summed, axis=-1, keepdims=True)
    centered = summed - middle
    inverse = lax.rsqrt(jnp.mean(centered * centered, axis=-1, keepdims=True) + epsilon)
    return centered * inverse, inverse


def row_norm_back(upstream, normed, inverse, gain):
    scaled = upstream * gain
    centered = scaled - jnp.mean(scaled, axis=-1, keepdims=True)
    return inverse * (centered - normed * jnp.mean(scaled * normed, axis=-1, keepdims=True))


def split_three(value):
    high = value.astype(bf16).astype(f32)
    rest = value - high
    middle = rest.astype(bf16).astype(f32)
    return high, middle, rest - middle


class Copies:
    def __init__(self, semaphores):
        self.semaphores = semaphores
        self.used = 0

    def make(self, source, target):
        copy = pltpu.make_async_copy(source, target, self.semaphores.at[self.used])
        self.used += 1
        return copy

    def start(self, source, target):
        copy = self.make(source, target)
        copy.start()
        return copy


def either(condition, yes, no):
    pl.when(condition)(yes)
    pl.when(jnp.logical_not(condition))(no)


def forward_kernel(
    info, lengths, tokens, received, qkv_hbm, out_hbm, ff1_hbm, ff2_hbm,
    first_gain_hbm, second_gain_hbm, qv_bias_hbm, out_bias_hbm, first_shift_hbm, ff1_bias_hbm,
    ff2_bias_hbm, second_shift_hbm, *rest,
):
    kept_in, rest = rest[:KEPT], rest[KEPT:]
    (sent_hbm, layer_hbm, qkv_keep, context_keep, marks_keep, one_keep, one_inverse_keep, slope_keep,
     two_keep, two_inverse_keep) = rest[: KEPT + 1]
    (x, qkv, out, ff1, ff2, first_gain, second_gain, qv_bias, out_bias, first_shift, ff1_bias,
     ff2_bias, second_shift, acc, first, heads, context, marks, normed, inverse, slope, sent, semaphores) = rest[KEPT + 1 :]
    rows, width = x.shape
    hidden = ff1_bias.shape[1]
    groups = width // GROUP
    tiles = hidden // TILE

    @pl.when(info[0] == 1)
    def _():
        slot = info[2]
        copies = Copies(semaphores)
        x_token = copies.make(tokens.at[slot, 0], x)
        x_received = pltpu.make_async_copy(received, x, semaphores.at[0])
        either(info[1] == 1, x_token.start, x_received.start)
        qkv_copies = [
            [copies.make(qkv_hbm.at[:, pl.ds(part * width + g * GROUP, GROUP)], qkv.at[g, :, pl.ds(part * GROUP, GROUP)]) for part in range(3)]
            for g in range(groups)
        ]
        for copy in qkv_copies[0]:
            copy.start()
        small = [
            copies.start(source, target)
            for source, target in (
                (qv_bias_hbm, qv_bias), (out_bias_hbm, out_bias), (first_gain_hbm, first_gain),
                (first_shift_hbm, first_shift), (ff1_bias_hbm, ff1_bias), (ff2_bias_hbm, ff2_bias),
                (second_gain_hbm, second_gain), (second_shift_hbm, second_shift),
            )
        ]
        lane = lax.broadcasted_iota(jnp.int32, (rows, LANES), 1)
        place = lax.broadcasted_iota(jnp.int32, (rows, LANES), 0)
        label = jnp.zeros((rows, LANES), jnp.int32)
        end = jnp.int32(0)
        for index in range(lengths.shape[2]):
            end = end + lengths[slot, 0, index]
            label = label + jnp.where(place >= end, 1, 0)
        own = jnp.where(lane == label, 1.0, 0.0)
        query_mark = own.astype(bf16)
        key_mark = jnp.where(lane < lengths.shape[2], (1.0 - own) * masked_score, 0.0).astype(bf16)
        half = lane < HEAD_DIM
        zero = jnp.zeros((rows, LANES), bf16)
        ones = jnp.ones((rows, LANES), bf16)
        keep = own
        for copy in small:
            copy.wait()
        x_token.wait()
        for copy in qkv_copies[0]:
            copy.wait()
        for g in range(1, groups):
            for copy in qkv_copies[g]:
                copy.start()
        out_copy = copies.start(out_hbm, out)
        ff1_copies = []
        ff2_copies = []
        for t in range(tiles):
            ff1_copies.append(copies.start(ff1_hbm.at[:, pl.ds(t * TILE, TILE)], ff1.at[t]))
            ff2_copies.append(copies.start(ff2_hbm.at[pl.ds(t * TILE, TILE)], ff2.at[pl.ds(t * TILE, TILE)]))
        value = x[...]
        for g in range(groups):
            columns = slice(g * GROUP, (g + 1) * GROUP)
            if g > 0:
                for copy in qkv_copies[g]:
                    copy.wait()
            found = dot(value, qkv[g])
            query = (found[:, :GROUP] + qv_bias[:, columns]).astype(bf16)
            keys = found[:, GROUP : 2 * GROUP].astype(bf16)
            values = (found[:, 2 * GROUP :] + qv_bias[:, width + g * GROUP : width + (g + 1) * GROUP]).astype(bf16)
            heads[0, :, columns] = query
            heads[1, :, columns] = keys
            heads[2, :, columns] = values
            parts = []
            for pair in range(GROUP // LANES):
                chosen = slice(pair * LANES, (pair + 1) * LANES)
                scaled = query[:, chosen] * jnp.asarray(HEAD_DIM**-0.5, bf16)
                right = beside(keys[:, chosen], key_mark)
                carried = beside(values[:, chosen], ones)
                found = []
                for side in range(2):
                    left = jnp.where(half if side == 0 else ~half, scaled, zero)
                    scores = dot_back(beside(left, query_mark), right)
                    top = jnp.max(scores, axis=-1, keepdims=True)
                    weights = jnp.exp(scores - top).astype(bf16)
                    mixed = dot(weights, carried)
                    total = mixed[:, LANES:]
                    found.append(mixed[:, :LANES] / total)
                    head = g * (GROUP // HEAD_DIM) + pair * 2 + side
                    keep = jnp.where((lane % 16 == head) & (lane >= 16) & (lane < 64), top + jnp.log(total), keep)
                parts.append(jnp.where(half, found[0], found[1]))
            context[:, columns] = beside(*parts).astype(bf16)
            if g == 0:
                out_copy.wait()
                acc[...] = value.astype(f32) + out_bias[...] + dot(context[:, columns], out[columns, :])
            else:
                acc[...] += dot(context[:, columns], out[columns, :])
        high, middle, low = split_three(keep)
        marks[...] = jnp.where(lane < 32, high, jnp.where(lane < 48, middle, low)).astype(bf16)
        stores = [copies.start(heads, qkv_keep.at[slot]), copies.start(context, context_keep.at[slot]), copies.start(marks, marks_keep.at[slot])]
        one, one_inverse = row_norm(acc[...])
        normed[...] = one
        inverse[0] = jnp.broadcast_to(one_inverse, (rows, LANES))
        stores.append(copies.start(normed, one_keep.at[slot]))
        stores.append(copies.start(inverse.at[0], one_inverse_keep.at[slot]))
        value = one * first_gain[...] + first_shift[...]
        first[...] = value.astype(bf16)
        acc[...] = value + ff2_bias[...]
        for t in range(tiles):
            ff1_copies[t].wait()
            ff2_copies[t].wait()
            acts = []
            for c in range(TILE // GROUP):
                columns = slice(c * GROUP, (c + 1) * GROUP)
                far = slice(t * TILE + c * GROUP, t * TILE + (c + 1) * GROUP)
                h = dot(first[...], ff1[t, :, columns]) + ff1_bias[:, far]
                share = 0.5 + 0.5 * lax.erf(h * root_half)
                slope[:, far] = (share + h * jnp.exp(h * h * -0.5) * inverse_root_tau).astype(bf16)
                acts.append((h * share).astype(bf16))
            acc[...] += dot(beside(*acts), ff2[t * TILE : (t + 1) * TILE, :])
            cut = pl.ds(t * TILE, TILE)
            stores.append(copies.start(slope.at[:, cut], slope_keep.at[slot, :, cut]))
        two, two_inverse = row_norm(acc[...])
        sent[0] = (two * second_gain[...] + second_shift[...]).astype(bf16)
        sent[1] = two.astype(bf16)
        inverse[1] = jnp.broadcast_to(two_inverse, (rows, LANES))
        stores.append(copies.start(sent.at[0], sent_hbm))
        stores.append(copies.start(sent.at[0], layer_hbm.at[slot]))
        stores.append(copies.start(sent.at[1], two_keep.at[slot]))
        stores.append(copies.start(inverse.at[1], two_inverse_keep.at[slot]))
        for copy in stores:
            copy.wait()


KEPT = 9


def any_space(count):
    return [pl.BlockSpec(memory_space=pl.ANY)] * count


def forward(info, lengths, tokens, received, params, kept):
    micro, _, rows, width = tokens.shape
    hidden = params[2].shape[1]
    count = micro
    shapes = [
        ((count, rows, width), bf16), ((count, 3, rows, width), bf16), ((count, rows, width), bf16),
        ((count, rows, LANES), bf16), ((count, rows, width), f32), ((count, rows, LANES), f32),
        ((count, rows, hidden), bf16), ((count, rows, width), bf16), ((count, rows, LANES), f32),
    ]
    kept = () if kept is None else tuple(kept)
    first_kept = 4 + len(params)
    kernel = forward_kernel if kept else functools.partial(without_kept, first_kept)
    outs = pl.pallas_call(
        kernel,
        in_specs=[pl.BlockSpec(memory_space=pltpu.SMEM)] * 2 + any_space(2 + len(params) + len(kept)),
        out_specs=any_space(1 + KEPT),
        out_shape=[jax.ShapeDtypeStruct((rows, width), bf16)] + [jax.ShapeDtypeStruct(*shape) for shape in shapes],
        input_output_aliases={first_kept + i: 1 + i for i in range(len(kept))},
        scratch_shapes=[
            pltpu.VMEM((rows, width), bf16),
            pltpu.VMEM((width // GROUP, width, 3 * GROUP), bf16),
            pltpu.VMEM((width, width), bf16),
            pltpu.VMEM((hidden // TILE, width, TILE), bf16),
            pltpu.VMEM((hidden, width), bf16),
            pltpu.VMEM((1, width), f32), pltpu.VMEM((1, width), f32), pltpu.VMEM((1, 2 * width), f32),
            pltpu.VMEM((1, width), f32), pltpu.VMEM((1, width), f32), pltpu.VMEM((1, hidden), f32),
            pltpu.VMEM((1, width), f32), pltpu.VMEM((1, width), f32),
            pltpu.VMEM((rows, width), f32),
            pltpu.VMEM((rows, width), bf16),
            pltpu.VMEM((3, rows, width), bf16),
            pltpu.VMEM((rows, width), bf16),
            pltpu.VMEM((rows, LANES), bf16),
            pltpu.VMEM((rows, width), f32),
            pltpu.VMEM((2, rows, LANES), f32),
            pltpu.VMEM((rows, hidden), bf16),
            pltpu.VMEM((2, rows, width), bf16),
            pltpu.SemaphoreType.DMA((64,)),
        ],
        compiler_params=pltpu.CompilerParams(vmem_limit_bytes=VMEM_BYTES),
        cost_estimate=pl.CostEstimate(flops=2 * rows * width * (12 * width + 2 * rows), bytes_accessed=40 * 2**20, transcendentals=0),
        name="forward",
    )(info, lengths, tokens, received, *params, *kept)
    return outs[0], list(outs[1:])


def without_kept(position, *refs):
    refs = list(refs)
    forward_kernel(*refs[:position], *([None] * KEPT), *refs[position:])


def backward_kernel(
    info, cotangent, received, qkv_hbm, out_hbm, ff1_hbm, ff2_hbm, first_gain_hbm, second_gain_hbm,
    qkv_keep, context_keep, marks_keep, one_keep, one_inverse_keep, slope_keep, two_keep, two_inverse_keep,
    grad_in, totals_in, sent_hbm, grad_hbm, totals_hbm,
    up, two, two_inverse, slope, one, one_inverse, heads, context, marks, qkv, out, ff1, ff2, first_gain, second_gain,
    acc, low, totals, sent, semaphores,
):
    rows, width = up.shape
    hidden = slope.shape[1]
    groups = width // GROUP
    tiles = hidden // TILE
    at_query, at_value, at_out, at_first, at_ff1 = 0, width, 2 * width, 3 * width, 4 * width
    at_ff2 = at_ff1 + hidden
    at_second = at_ff2 + width

    @pl.when(info[0] == 1)
    def _():
        slot = info[2]
        copies = Copies(semaphores)
        up_own = copies.make(cotangent.at[slot, 0], up)
        up_received = pltpu.make_async_copy(received, up, semaphores.at[0])
        either(info[1] == 1, up_own.start, up_received.start)
        early = [
            copies.start(two_keep.at[slot], two),
            copies.start(two_inverse_keep.at[slot], two_inverse),
            copies.start(second_gain_hbm, second_gain),
            copies.start(first_gain_hbm, first_gain),
        ]
        before = copies.make(totals_hbm, totals)

        def clear():
            totals[...] = jnp.zeros_like(totals)

        def fetch():
            before.start()
            before.wait()

        ff_copies = []
        for t in range(tiles):
            cut = pl.ds(t * TILE, TILE)
            ff_copies.append([
                copies.make(ff2_hbm.at[cut], ff2.at[cut]),
                copies.make(slope_keep.at[slot, :, cut], slope.at[:, cut]),
                copies.make(ff1_hbm.at[:, cut], ff1.at[t]),
            ])
        for copy in ff_copies[0]:
            copy.start()
        either(info[3] == 1, clear, fetch)
        up_own.wait()
        for copy in early:
            copy.wait()
        for t in range(1, tiles):
            for copy in ff_copies[t]:
                copy.start()
        one_copies = [copies.start(one_keep.at[slot], one), copies.start(one_inverse_keep.at[slot], one_inverse)]
        head_copies = [
            copies.start(out_hbm, out),
            copies.start(qkv_keep.at[slot], heads),
            copies.start(context_keep.at[slot], context),
            copies.start(marks_keep.at[slot], marks),
        ]
        qkv_copies = [
            [copies.start(qkv_hbm.at[:, pl.ds(part * width + g * GROUP, GROUP)], qkv.at[g, :, pl.ds(part * GROUP, GROUP)]) for part in range(3)]
            for g in range(groups)
        ]
        upstream = up[...].astype(f32)
        grad = row_norm_back(upstream, two[...].astype(f32), two_inverse[:, :1], second_gain[...])
        low[...] = grad.astype(bf16)
        acc[...] = grad
        totals[:, at_second : at_second + width] += column_sum(upstream)
        totals[:, at_ff2 : at_ff2 + width] += column_sum(grad.astype(bf16).astype(f32))
        for t in range(tiles):
            for copy in ff_copies[t]:
                copy.wait()
            grads = []
            for c in range(TILE // GROUP):
                far = slice(t * TILE + c * GROUP, t * TILE + (c + 1) * GROUP)
                h = (dot_back(low[...], ff2[far, :]) * slope[:, far].astype(f32)).astype(bf16)
                there = slice(at_ff1 + t * TILE + c * GROUP, at_ff1 + t * TILE + (c + 1) * GROUP)
                totals[:, there] += column_sum(h.astype(f32))
                grads.append(h)
            acc[...] += dot_back(beside(*grads), ff1[t])
        for copy in one_copies:
            copy.wait()
        first_grad = acc[...]
        totals[:, at_first : at_first + width] += column_sum(first_grad)
        summed = row_norm_back(first_grad, one[...], one_inverse[:, :1], first_gain[...])
        acc[...] = summed
        low[...] = summed.astype(bf16)
        totals[:, at_out : at_out + width] += column_sum(summed.astype(bf16).astype(f32))
        for copy in head_copies:
            copy.wait()
        lane = lax.broadcasted_iota(jnp.int32, (rows, LANES), 1)
        half = lane < HEAD_DIM
        zero = jnp.zeros((rows, LANES), bf16)
        query_mark = marks[...]
        key_mark = jnp.where(lane < 16, (1.0 - query_mark.astype(f32)) * masked_score, 0.0)
        key_mark = jnp.where(lane < info[4], key_mark, 0.0)
        which = lax.broadcasted_iota(jnp.int32, (GROUP, LANES), 0) // HEAD_DIM
        spot = lax.broadcasted_iota(jnp.int32, (GROUP, LANES), 1)
        pick = jnp.where((spot % 16 == which) & (spot < 48), 1.0, 0.0).astype(bf16)
        scale = HEAD_DIM**-0.5
        for g in range(groups):
            columns = slice(g * GROUP, (g + 1) * GROUP)
            context_grad = dot_back(low[...], out[columns, :]).astype(bf16)
            product = context_grad.astype(f32) * context[:, columns].astype(f32)
            upper = product.astype(bf16)
            inner = dot(upper, pick) + dot((product - upper.astype(f32)).astype(bf16), pick)
            high, middle, rest = split_three(inner)
            grad_mark = jnp.where(lane < 16, high, jnp.where(lane < 32, middle, rest)).astype(bf16)
            query_grads, key_grads, value_grads = [], [], []
            for pair in range(GROUP // LANES):
                chosen = slice(g * GROUP + pair * LANES, g * GROUP + (pair + 1) * LANES)
                query = heads[0, :, chosen] * jnp.asarray(scale, bf16)
                keys = heads[1, :, chosen]
                values = heads[2, :, chosen]
                upper_grad = context_grad[:, pair * LANES : (pair + 1) * LANES]
                query_turned = query.T
                grad_turned = upper_grad.T
                score_grads, keys_kept = [], []
                for side in range(2):
                    ours = half if side == 0 else ~half
                    mine = slice(side * HEAD_DIM, (side + 1) * HEAD_DIM)
                    local = pair * 2 + side
                    head = g * (GROUP // HEAD_DIM) + local
                    right = beside(keys, jnp.where((lane % 16 == head) & (lane >= 16) & (lane < 64), -1.0, key_mark).astype(bf16))
                    probs = jnp.exp(dot_back(beside(jnp.where(ours, query, zero), query_mark), right))
                    right = beside(values, jnp.where((lane % 16 == local) & (lane < 48), -1.0, 0.0).astype(bf16))
                    score_grad = (probs * dot_back(beside(jnp.where(ours, upper_grad, zero), grad_mark), right)).astype(bf16)
                    value_grads.append(dot(grad_turned[mine], probs.astype(bf16)))
                    key_grads.append(dot(query_turned[mine], score_grad))
                    score_grads.append(score_grad)
                    keys_kept.append(jnp.where(ours, keys, zero))
                query_grads.append(dot(beside(*score_grads), above(*keys_kept)) * scale)
            query_grad = beside(*query_grads).astype(bf16)
            key_grad = above(*key_grads).T.astype(bf16)
            value_grad = above(*value_grads).T.astype(bf16)
            totals[:, at_query + g * GROUP : at_query + (g + 1) * GROUP] += column_sum(query_grad.astype(f32))
            totals[:, at_value + g * GROUP : at_value + (g + 1) * GROUP] += column_sum(value_grad.astype(f32))
            for copy in qkv_copies[g]:
                copy.wait()
            acc[...] += dot_back(beside(query_grad, key_grad, value_grad), qkv[g])
        sent[...] = acc[...].astype(bf16)
        stores = [
            copies.start(sent, sent_hbm), copies.start(sent, grad_hbm.at[slot]), copies.start(totals, totals_hbm),
        ]
        for copy in stores:
            copy.wait()


def backward_fresh(*refs):
    backward_kernel(*refs[:17], None, None, *refs[17:])


def backward(info, cotangent, received, params, kept, before):
    micro, _, rows, width = cotangent.shape
    hidden = params[2].shape[1]
    total = 6 * width + hidden
    kernel = backward_fresh if before is None else backward_kernel
    before = () if before is None else tuple(before)
    outs = pl.pallas_call(
        kernel,
        in_specs=[pl.BlockSpec(memory_space=pltpu.SMEM)] + any_space(16 + len(before)),
        out_specs=any_space(3),
        out_shape=[
            jax.ShapeDtypeStruct((rows, width), bf16),
            jax.ShapeDtypeStruct((micro, rows, width), bf16),
            jax.ShapeDtypeStruct((1, total), f32),
        ],
        input_output_aliases={17 + i: 1 + i for i in range(len(before))},
        scratch_shapes=[
            pltpu.VMEM((rows, width), bf16),
            pltpu.VMEM((rows, width), bf16),
            pltpu.VMEM((rows, LANES), f32),
            pltpu.VMEM((rows, hidden), bf16),
            pltpu.VMEM((rows, width), f32),
            pltpu.VMEM((rows, LANES), f32),
            pltpu.VMEM((3, rows, width), bf16),
            pltpu.VMEM((rows, width), bf16),
            pltpu.VMEM((rows, LANES), bf16),
            pltpu.VMEM((width // GROUP, width, 3 * GROUP), bf16),
            pltpu.VMEM((width, width), bf16),
            pltpu.VMEM((hidden // TILE, width, TILE), bf16),
            pltpu.VMEM((hidden, width), bf16),
            pltpu.VMEM((1, width), f32),
            pltpu.VMEM((1, width), f32),
            pltpu.VMEM((rows, width), f32),
            pltpu.VMEM((rows, width), bf16),
            pltpu.VMEM((1, total), f32),
            pltpu.VMEM((rows, width), bf16),
            pltpu.SemaphoreType.DMA((64,)),
        ],
        compiler_params=pltpu.CompilerParams(vmem_limit_bytes=VMEM_BYTES),
        cost_estimate=pl.CostEstimate(flops=2 * rows * width * (12 * width + 5 * rows), bytes_accessed=40 * 2**20, transcendentals=0),
        name="backward",
    )(info, cotangent, received, *params[:6], *kept[1:], *before)
    return outs[0], list(outs[1:])


def shift(value, axis, steps):
    count = lax.axis_size(axis)
    pairs = [(place, place + steps) for place in range(max(0, -steps), min(count, count - steps))]
    return lax.ppermute(value, axis, pairs)


def add_over(value, axis):
    count = lax.axis_size(axis)
    if count & (count - 1):
        return lax.psum(value, axis)
    step = 1
    while step < count:
        value = value + lax.ppermute(value, axis, [(place, place ^ step) for place in range(count)])
        step *= 2
    return value


def body(tokens, doc_lengths, cotangent, *params):
    params = tuple(item[0] if item.ndim == 3 else item for item in params)
    section = lax.axis_index("section")
    first = (section == 0).astype(jnp.int32)
    second = 1 - first
    one = jnp.int32(1)
    zero = jnp.int32(0)
    segments = jnp.int32(doc_lengths.shape[2])

    def info(active, own, slot, fresh):
        return jnp.stack([active, own, slot, fresh, segments])

    blank = tokens[0, 0]
    sent, kept = forward(info(first, one, zero, zero), doc_lengths, tokens, blank, params, None)
    received = shift(sent, "section", 1)
    sent, kept = forward(info(one, first, first, zero), doc_lengths, tokens, received, params, kept)
    received = shift(sent, "section", 1)
    returned, state = backward(info(second, one, zero, one), cotangent, blank, params, kept, None)
    returned = shift(returned, "section", -1)
    sent, kept = forward(info(second, zero, one, zero), doc_lengths, tokens, received, params, kept)
    sent, state = backward(info(one, second, second, first), cotangent, returned, params, kept, state)
    returned = shift(sent, "section", -1)
    sent, state = backward(info(first, zero, one, zero), cotangent, returned, params, kept, state)
    layer_out = kept[0][None, :, None]
    layer_in_grad = state[0][None, :, None]
    totals = add_over(state[1], "dp")
    width = tokens.shape[3]
    hidden = params[2].shape[1]
    places = [0, 2 * width, 3 * width, 4 * width, 4 * width + hidden, 5 * width + hidden, 6 * width + hidden]
    return (layer_out, layer_in_grad) + tuple(totals[:, low:high] for low, high in zip(places[:-1], places[1:]))


def solution(mesh):
    in_specs = (
        P(None, "dp", None, None), P(None, "dp", None), P(None, "dp", None, None),
        P("section", None, None), P("section", None, None), P("section", None, None), P("section", None, None),
    ) + (P("section", None),) * 8
    out_specs = (P("section", None, "dp", None, None),) * 2 + (P("section", None),) * 6
    return jax.shard_map(body, mesh=mesh, in_specs=in_specs, out_specs=out_specs, check_vma=False)
```

```python
import functools
import types
import jax
import jax.numpy as jnp
from jax import lax
from jax.experimental import pallas as pl
from jax.experimental.pallas import tpu as pltpu
from jax.sharding import PartitionSpec as P

HEAD_DIM = 64
LANES = 128
GROUP = 256
TILE = 1024
BLOCK = 256
ROWS = 128
PAIRS = 4
VMEM_BYTES = 36 * 2**20
epsilon = 1e-05
masked_score = -1000000000.0
root_half = 0.7071067811865476
inverse_root_tau = 0.3989422804014327
f32 = jnp.float32
bf16 = jnp.bfloat16


def dot(left, right):
    return jnp.dot(left, right, preferred_element_type=f32)


def dot_back(left, right):
    return lax.dot_general(left, right, (((1,), (1,)), ((), ())), preferred_element_type=f32)


def beside(*parts):
    return jnp.concatenate(parts, axis=1)


def above(*parts):
    return jnp.concatenate(parts, axis=0)


def column_sum(value):
    return jnp.sum(value, axis=0, keepdims=True)


def row_norm(summed):
    middle = jnp.mean(summed, axis=-1, keepdims=True)
    centered = summed - middle
    inverse = lax.rsqrt(jnp.mean(centered * centered, axis=-1, keepdims=True) + epsilon)
    return centered * inverse, inverse


def row_norm_back(upstream, normed, inverse, gain):
    scaled = upstream * gain
    centered = scaled - jnp.mean(scaled, axis=-1, keepdims=True)
    return inverse * (centered - normed * jnp.mean(scaled * normed, axis=-1, keepdims=True))


def split_three(value):
    high = value.astype(bf16).astype(f32)
    rest = value - high
    middle = rest.astype(bf16).astype(f32)
    return high, middle, rest - middle


def strip(index, size):
    return pl.ds(pl.multiple_of(index * size, size), size)


class Copies:
    def __init__(self, semaphores):
        self.semaphores = semaphores
        self.used = 0

    def take(self, count=1):
        self.used += count
        return self.used - count

    def make(self, source, target, place=None):
        place = self.take() if place is None else place
        return pltpu.make_async_copy(source, target, self.semaphores.at[place])

    def start(self, source, target):
        return self.start_at(source, target, self.take())

    def start_at(self, source, target, place):
        copy = self.make(source, target, place)
        copy.start()
        return copy


def any_space(count):
    return [pl.BlockSpec(memory_space=pl.ANY)] * count


PARAMS = (
    "qkv", "out", "ff1", "ff2", "first_gain", "second_gain", "qv_bias", "out_bias", "first_shift", "ff1_bias", "ff2_bias",
    "second_shift",
)
KEPT = ("heads", "context", "marks", "one", "one_inverse", "slope", "two", "two_inverse")


def resident_of(width, hidden):
    groups, tiles = width // GROUP, hidden // TILE
    shapes = {
        "qkv": ((groups, width, 3 * width // groups), bf16),
        "out": ((width, width), bf16),
        "ff1": ((tiles, width, TILE), bf16),
        "ff2": ((tiles, TILE, width), bf16),
    }
    lengths = {"qv_bias": 3 * width, "ff1_bias": hidden}
    return shapes | {name: ((1, lengths.get(name, width)), f32) for name in PARAMS[4:]}


def scratch_of(rows, width, hidden):
    tiles = hidden // TILE
    return {
        "acc": ((rows, width), f32),
        "low": ((rows, width), bf16),
        "heads": ((rows, 3 * width), bf16),
        "context": ((rows, width), bf16),
        "marks": ((rows, LANES), bf16),
        "logsums": ((rows, LANES), f32),
        "one": ((rows, width), f32),
        "one_inverse": ((rows, LANES), f32),
        "slope": ((tiles, rows, TILE), bf16),
        "two": ((rows, width), bf16),
        "two_inverse": ((rows, LANES), f32),
        "grad_marks": ((rows, LANES), bf16),
        "totals": ((1, 6 * width + hidden), f32),
    }


class Layer:
    def __init__(self, hbm, vmem, semaphores):
        self.hbm, self.vmem = hbm, vmem
        self.copies = Copies(semaphores)
        self.rows, self.width = vmem.acc.shape
        self.groups = vmem.qkv.shape[0]
        self.tiles = vmem.slope.shape[0]
        self.segments = hbm.lengths.shape[2]
        self.qkv_place = self.copies.take(self.groups)
        self.out_place = self.copies.take()
        self.ff_place = self.copies.take(2 * self.tiles)
        self.small_place = self.copies.take(9)
        self.loading = hasattr(hbm, "qkv")
        self.kept_place = self.copies.take(len(KEPT))
        self.slope_place = self.copies.take(self.tiles)
        self.row_place = self.copies.take(2 * (self.rows // ROWS))

    def qkv_copy(self, g):
        part = self.vmem.qkv.shape[2]
        return self.copies.make(self.hbm.qkv.at[:, strip(g, part)], self.vmem.qkv.at[g], self.qkv_place + g)

    def out_copy(self):
        return self.copies.make(self.hbm.out, self.vmem.out, self.out_place)

    def ff1_copy(self, t):
        return self.copies.make(self.hbm.ff1.at[:, strip(t, TILE)], self.vmem.ff1.at[t], self.ff_place + 2 * t)

    def ff2_copy(self, t):
        return self.copies.make(self.hbm.ff2.at[strip(t, TILE)], self.vmem.ff2.at[t], self.ff_place + 2 * t + 1)

    def small_copies(self):
        copies = []
        for name in PARAMS[4:]:
            source, target = getattr(self.hbm, name), getattr(self.vmem, name)
            if name == "qv_bias":
                copies.append((source.at[:, : self.width], target.at[:, : self.width]))
                copies.append((source.at[:, self.width :], target.at[:, 2 * self.width :]))
            else:
                copies.append((source, target))
        return [self.copies.make(*pair, self.small_place + index) for index, pair in enumerate(copies)]

    def start_weights(self):
        for g in range(self.groups):
            self.qkv_copy(g).start()
            if g == 0:
                for copy in self.small_copies():
                    copy.start()
        self.out_copy().start()
        for t in range(self.tiles):
            self.ff1_copy(t).start()
            self.ff2_copy(t).start()
        self.vmem.qv_bias[:, self.width : 2 * self.width] = jnp.zeros((1, self.width), f32)

    def wait_qkv(self, g):
        if self.loading:
            self.qkv_copy(g).wait()

    def wait_out(self):
        if self.loading:
            self.out_copy().wait()

    def wait_feed(self, t):
        if self.loading:
            self.ff1_copy(t).wait()
            self.ff2_copy(t).wait()

    def wait_small(self):
        if self.loading:
            for copy in self.small_copies():
                copy.wait()

    def wait_weights(self):
        self.wait_small()
        self.wait_out()
        for g in range(self.groups):
            self.wait_qkv(g)
        for t in range(self.tiles):
            self.wait_feed(t)

    def by_rows(self, work, size=ROWS):
        def step(index, carry):
            work(strip(index, size))
            return carry

        lax.fori_loop(0, self.rows // size, step, 0)

    def kept_copy(self, name, slot, back):
        there, here = getattr(self.hbm, "kept_" + name).at[slot], getattr(self.vmem, name)
        place = self.kept_place + KEPT.index(name)
        return self.copies.make(there, here, place) if back else self.copies.make(here, there, place)

    def slope_copy(self, t, slot, back):
        there, here = self.hbm.kept_slope.at[slot, t], self.vmem.slope.at[t]
        return self.copies.make(there, here, self.slope_place + t) if back else self.copies.make(here, there, self.slope_place + t)

    def layer_copy(self, index, slot):
        rows = strip(index, ROWS)
        return self.copies.make(self.vmem.sent.at[rows], self.hbm.layer.at[slot, rows], self.row_place + 2 * index)

    def grad_copy(self, index, slot):
        rows = strip(index, BLOCK)
        return self.copies.make(self.vmem.sent.at[rows], self.hbm.grad.at[slot, rows], self.row_place + 2 * index)

    def two_copy(self, index, slot):
        rows = strip(index, ROWS)
        return self.copies.make(self.vmem.two.at[rows], self.hbm.kept_two.at[slot, rows], self.row_place + 2 * index + 1)

    def keep(self, name, slot, keeping):
        if name == "slope":
            return
        if keeping:
            self.kept_copy(name, slot, False).start()

    def forward(self, slot, keeping):
        hbm, vmem = self.hbm, self.vmem
        rows, width, groups, tiles, segments = self.rows, self.width, self.groups, self.tiles, self.segments
        lane = lax.broadcasted_iota(jnp.int32, (rows, LANES), 1)
        place = lax.broadcasted_iota(jnp.int32, (rows, LANES), 0)
        label = jnp.zeros((rows, LANES), jnp.int32)
        end = jnp.int32(0)
        for index in range(segments):
            end = end + hbm.lengths[slot, 0, index]
            label = label + jnp.where(place >= end, 1, 0)
        own = jnp.where(lane == label, 1.0, 0.0)
        query_mark = own.astype(bf16)
        key_mark = jnp.where(lane < segments, (1.0 - own) * masked_score, 0.0).astype(bf16)
        vmem.logsums[...] = own
        half = lane < HEAD_DIM
        zero = jnp.zeros((rows, LANES), bf16)
        ones = jnp.ones((rows, LANES), bf16)
        head_lane = jnp.where((lane >= 16) & (lane < 64), lane & 15, -1)
        self.wait_small()
        if self.x_copy is not None:
            self.x_copy.wait()

        part = vmem.qkv.shape[2]

        def project(g, carry):
            self.wait_qkv(g)
            columns = strip(g, part)
            vmem.heads[:, columns] = (dot(vmem.x[...], vmem.qkv[g]) + vmem.qv_bias[:, columns]).astype(bf16)
            return carry

        lax.fori_loop(0, groups, project, 0)

        def head_step(step, carry):
            count = 2 * PAIRS
            queries, keys, values = (
                vmem.heads[:, pl.ds(pl.multiple_of(at * width + step * PAIRS * LANES, LANES), PAIRS * LANES)] for at in range(3)
            )
            mixes, tops = [], []

            def score(local):
                pair, side = divmod(local, 2)
                chosen = slice(pair * LANES, (pair + 1) * LANES)
                scaled = queries[:, chosen] * jnp.asarray(HEAD_DIM**-0.5, bf16)
                left = jnp.where(half if side == 0 else ~half, scaled, zero)
                return dot_back(beside(left, query_mark), beside(keys[:, chosen], key_mark))

            scores = score(0)
            for local in range(count):
                following = score(local + 1) if local + 1 < count else None
                chosen = slice(local // 2 * LANES, (local // 2 + 1) * LANES)
                top = jnp.max(scores, axis=-1, keepdims=True)
                weights = jnp.exp(scores - top).astype(bf16)
                mixes.append(dot(weights, beside(values[:, chosen], ones)))
                tops.append(top)
                scores = following
            keep = vmem.logsums[...]
            parts = []
            for local in range(count):
                total = mixes[local][:, LANES:]
                parts.append(mixes[local][:, :LANES] / total)
                keep = jnp.where(head_lane == step * count + local, tops[local] + jnp.log(total), keep)
            vmem.logsums[...] = keep
            mixed = beside(*[jnp.where(half, parts[2 * p], parts[2 * p + 1]) for p in range(PAIRS)])
            vmem.context[:, strip(step, PAIRS * LANES)] = mixed.astype(bf16)
            return carry

        lax.fori_loop(0, width // (PAIRS * LANES), head_step, 0)
        high, middle, rest = split_three(vmem.logsums[...])
        vmem.marks[...] = jnp.where(lane < 32, high, jnp.where(lane < 48, middle, rest)).astype(bf16)
        for name in ("heads", "context", "marks"):
            self.keep(name, slot, keeping)
        self.wait_out()

        def first_norm(rows_):
            summed = vmem.x[rows_, :].astype(f32) + vmem.out_bias[...] + dot(vmem.context[rows_, :], vmem.out[...])
            one, one_inverse = row_norm(summed)
            vmem.one[rows_, :] = one
            vmem.one_inverse[rows_, :] = jnp.broadcast_to(one_inverse, (one.shape[0], LANES))
            value = one * vmem.first_gain[...] + vmem.first_shift[...]
            vmem.low[rows_, :] = value.astype(bf16)
            vmem.acc[rows_, :] = value + vmem.ff2_bias[...]

        self.by_rows(first_norm, BLOCK)
        for name in ("one", "one_inverse"):
            self.keep(name, slot, keeping)

        def tile_step(t, carry):
            self.wait_feed(t)
            bias = vmem.ff1_bias[:, strip(t, TILE)]
            acts = []
            for c in range(TILE // BLOCK):
                columns = slice(c * BLOCK, (c + 1) * BLOCK)
                h = dot(vmem.low[...], vmem.ff1[t, :, columns]) + bias[:, columns]
                share = 0.5 + 0.5 * lax.erf(h * root_half)
                vmem.slope[t, :, columns] = (share + h * jnp.exp(h * h * -0.5) * inverse_root_tau).astype(bf16)
                acts.append((h * share).astype(bf16))
            vmem.acc[...] += dot(beside(*acts), vmem.ff2[t])
            if keeping:
                self.slope_copy(t, slot, False).start()
            return carry

        lax.fori_loop(0, tiles, tile_step, 0)

        def second_norm(rows_):
            two, two_inverse = row_norm(vmem.acc[rows_, :])
            vmem.sent[rows_, :] = (two * vmem.second_gain[...] + vmem.second_shift[...]).astype(bf16)
            vmem.two[rows_, :] = two.astype(bf16)
            vmem.two_inverse[rows_, :] = jnp.broadcast_to(two_inverse, (two.shape[0], LANES))

        def second_step(index, carry):
            second_norm(strip(index, ROWS))
            self.layer_copy(index, slot).start()
            if keeping:
                self.two_copy(index, slot).start()
            return carry

        lax.fori_loop(0, rows // ROWS, second_step, 0)
        self.keep("two_inverse", slot, keeping)

    def finish_kept(self, slot):
        for name in KEPT:
            if name not in ("slope", "two"):
                self.kept_copy(name, slot, False).wait()
        for index in range(self.rows // ROWS):
            self.two_copy(index, slot).wait()
        for t in range(self.tiles):
            self.slope_copy(t, slot, False).wait()

    def fetch_kept(self, slot):
        for name in ("two", "two_inverse"):
            self.kept_copy(name, slot, True).start()
        for t in range(self.tiles):
            self.slope_copy(t, slot, True).start()
        for name in ("one", "one_inverse", "heads", "context", "marks"):
            self.kept_copy(name, slot, True).start()

    def backward(self, slot, fetched):
        hbm, vmem = self.hbm, self.vmem
        rows, width, groups, tiles, segments = self.rows, self.width, self.groups, self.tiles, self.segments
        hidden = tiles * TILE
        at_out, at_first, at_ff1 = 2 * width, 3 * width, 4 * width
        at_ff2 = at_ff1 + hidden
        at_second = at_ff2 + width
        totals, acc, low = vmem.totals, vmem.acc, vmem.low
        if fetched:
            for name in ("two", "two_inverse"):
                self.kept_copy(name, slot, True).wait()

        def second_back(rows_):
            upstream = vmem.up[rows_, :].astype(f32)
            grad = row_norm_back(upstream, vmem.two[rows_, :].astype(f32), vmem.two_inverse[rows_, :1], vmem.second_gain[...])
            low[rows_, :] = grad.astype(bf16)
            acc[rows_, :] = grad
            totals[:, at_second : at_second + width] += column_sum(upstream)
            totals[:, at_ff2 : at_ff2 + width] += column_sum(grad.astype(bf16).astype(f32))

        self.by_rows(second_back)

        def tile_step(t, carry):
            if fetched:
                self.slope_copy(t, slot, True).wait()
            grads, sums = [], []
            for c in range(TILE // BLOCK):
                columns = slice(c * BLOCK, (c + 1) * BLOCK)
                h = (dot_back(low[...], vmem.ff2[t, columns, :]) * vmem.slope[t, :, columns].astype(f32)).astype(bf16)
                sums.append(column_sum(h.astype(f32)))
                grads.append(h)
            totals[:, pl.ds(pl.multiple_of(at_ff1 + t * TILE, TILE), TILE)] += beside(*sums)
            acc[...] += dot_back(beside(*grads), vmem.ff1[t])
            return carry

        lax.fori_loop(0, tiles, tile_step, 0)
        if fetched:
            for name in ("one", "one_inverse", "heads", "context", "marks"):
                self.kept_copy(name, slot, True).wait()

        def first_back(rows_):
            first_grad = acc[rows_, :]
            totals[:, at_first : at_first + width] += column_sum(first_grad)
            summed = row_norm_back(first_grad, vmem.one[rows_, :], vmem.one_inverse[rows_, :1], vmem.first_gain[...])
            acc[rows_, :] = summed
            attend_grad = summed.astype(bf16)
            totals[:, at_out : at_out + width] += column_sum(attend_grad.astype(f32))
            context_grad = dot_back(attend_grad, vmem.out[...]).astype(bf16)
            product = context_grad.astype(f32) * vmem.context[rows_, :].astype(f32)
            upper = product.astype(bf16)
            inner = dot(upper, pick) + dot((product - upper.astype(f32)).astype(bf16), pick)
            high, middle, rest = split_three(inner)
            place = lax.broadcasted_iota(jnp.int32, inner.shape, 1)
            vmem.grad_marks[rows_, :] = jnp.where(place < 16, high, jnp.where(place < 32, middle, rest)).astype(bf16)
            vmem.context[rows_, :] = context_grad

        which = lax.broadcasted_iota(jnp.int32, (width, LANES), 0) // HEAD_DIM
        spot = lax.broadcasted_iota(jnp.int32, (width, LANES), 1)
        pick = jnp.where(((spot & 15) == which) & (spot < 48), 1.0, 0.0).astype(bf16)
        self.by_rows(first_back, BLOCK)
        lane = lax.broadcasted_iota(jnp.int32, (rows, LANES), 1)
        half = lane < HEAD_DIM
        zero = jnp.zeros((rows, LANES), bf16)
        query_mark = vmem.marks[...]
        key_mark = jnp.where(lane < segments, (1.0 - query_mark.astype(f32)) * masked_score, 0.0)
        head_lane = jnp.where((lane >= 16) & (lane < 64), lane & 15, -1)
        local_lane = jnp.where(lane < 48, lane & 15, -1)
        scale = HEAD_DIM**-0.5
        grad_mark = vmem.grad_marks[...]

        def head_step(step, carry):
            size = PAIRS * LANES
            spans = [pl.ds(pl.multiple_of(at * width + step * size, LANES), size) for at in range(3)]
            queries, all_keys, all_values = (vmem.heads[:, span] for span in spans)
            grads = vmem.context[:, strip(step, size)]
            query_grads, key_grads, value_grads = [], [], []
            for pair in range(PAIRS):
                chosen = slice(pair * LANES, (pair + 1) * LANES)
                query = queries[:, chosen] * jnp.asarray(scale, bf16)
                keys = all_keys[:, chosen]
                values = all_values[:, chosen]
                upper_grad = grads[:, chosen]
                query_turned = query.T
                grad_turned = upper_grad.T
                score_grads, keys_kept, key_turned, value_turned = [], [], [], []
                for side in range(2):
                    ours = half if side == 0 else ~half
                    mine = slice(side * HEAD_DIM, (side + 1) * HEAD_DIM)
                    head = step * 2 * PAIRS + pair * 2 + side
                    right = beside(keys, jnp.where(head_lane == head, -1.0, key_mark).astype(bf16))
                    probs = jnp.exp(dot_back(beside(jnp.where(ours, query, zero), query_mark), right))
                    right = beside(values, jnp.where(local_lane == head, -1.0, 0.0).astype(bf16))
                    score_grad = (probs * dot_back(beside(jnp.where(ours, upper_grad, zero), grad_mark), right)).astype(bf16)
                    value_turned.append(dot(grad_turned[mine], probs.astype(bf16)).astype(bf16))
                    key_turned.append(dot(query_turned[mine], score_grad).astype(bf16))
                    score_grads.append(score_grad)
                    keys_kept.append(jnp.where(ours, keys, zero))
                key_grads.append(above(*key_turned).T)
                value_grads.append(above(*value_turned).T)
                query_grads.append((dot(beside(*score_grads), above(*keys_kept)) * scale).astype(bf16))
            query_grad, key_grad, value_grad = beside(*query_grads), beside(*key_grads), beside(*value_grads)
            for span, grad in zip(spans, (query_grad, key_grad, value_grad)):
                vmem.heads[:, span] = grad
            totals[:, strip(step, size)] += column_sum(query_grad.astype(f32))
            totals[:, pl.ds(pl.multiple_of(width + step * size, LANES), size)] += column_sum(value_grad.astype(f32))
            return carry

        lax.fori_loop(0, width // (PAIRS * LANES), head_step, 0)
        part = vmem.qkv.shape[2]

        def input_step(index, carry):
            rows_ = strip(index, BLOCK)
            found = acc[rows_, :]
            for g in range(groups):
                found = found + dot_back(vmem.heads[rows_, g * part : (g + 1) * part], vmem.qkv[g])
            vmem.sent[rows_, :] = found.astype(bf16)
            self.grad_copy(index, slot).start()
            return carry

        lax.fori_loop(0, rows // BLOCK, input_step, 0)


def clear(ref):
    ref[...] = jnp.zeros_like(ref)


EVERY = False


def step_kernel(stage, slot, names, *refs):
    refs = dict(zip(names, refs))
    hbm = types.SimpleNamespace(**{name[4:]: ref for name, ref in refs.items() if name.startswith("hbm ")})
    vmem = types.SimpleNamespace(**{name[5:]: ref for name, ref in refs.items() if name.startswith("vmem ")})
    in_first = lax.axis_index("section") == 0
    working = jnp.logical_not(in_first) if stage in ("enter", "leave") and not EVERY else in_first
    layer = Layer(hbm, vmem, refs["semaphores"])
    copies = layer.copies

    @pl.when(working)
    def _():
        if stage in ("ahead", "enter"):
            layer.x_copy = copies.start(hbm.tokens.at[slot, 0], vmem.x) if stage == "ahead" else None
            if layer.loading:
                layer.start_weights()
            layer.forward(slot, True)
            layer.finish_kept(slot)
            stores = [layer.layer_copy(index, slot) for index in range(layer.rows // ROWS)]
        else:
            totals_copy = copies.start(hbm.totals, vmem.totals) if slot > 0 else None
            up_copy = copies.start(hbm.cotangent.at[slot, 0], vmem.up) if stage == "leave" else None
            layer.fetch_kept(slot)
            if slot > 0:
                totals_copy.wait()
            else:
                clear(vmem.totals)
            if stage == "leave":
                up_copy.wait()
            layer.backward(slot, True)
            stores = [copies.start(vmem.totals, hbm.totals)] + [layer.grad_copy(index, slot) for index in range(layer.rows // BLOCK)]
        for copy in stores:
            copy.wait()

    if layer.loading:
        @pl.when(jnp.logical_not(working))
        def _():
            layer.start_weights()
            layer.wait_weights()


def run(stage, slot, inputs, near, outputs, near_outputs, changed, rows, width, hidden):
    scratch = scratch_of(rows, width, hidden)
    if stage == "ahead":
        scratch["x"] = ((rows, width), bf16)
    if stage == "leave":
        scratch["up"] = ((rows, width), bf16)
    if stage in ("enter", "back"):
        scratch["sent"] = ((rows, width), bf16)
    names = ["hbm " + name for name in inputs] + ["vmem " + name for name in near]
    names += ["hbm " + name + "_before" for name in changed]
    names += ["hbm " + name for name in outputs] + ["vmem " + name for name in near_outputs]
    names += ["hbm " + name for name in changed] + ["vmem " + name for name in scratch] + ["semaphores"]
    close = pl.BlockSpec(memory_space=pltpu.VMEM)
    specs = [pl.BlockSpec(memory_space=pltpu.SMEM if name == "lengths" else pl.ANY) for name in inputs]
    held = [pltpu.with_memory_space_constraint(item, pltpu.VMEM) for item in near.values()]
    first_changed, first_out = len(inputs) + len(near), len(outputs) + len(near_outputs)
    outs = pl.pallas_call(
        functools.partial(step_kernel, stage, slot, names),
        in_specs=specs + [close] * len(near) + any_space(len(changed)),
        out_specs=any_space(len(outputs)) + [close] * len(near_outputs) + any_space(len(changed)),
        out_shape=[jax.ShapeDtypeStruct(*shape) for shape in outputs.values()]
        + [pltpu.VMEM(*shape) for shape in near_outputs.values()]
        + [jax.ShapeDtypeStruct(item.shape, item.dtype) for item in changed.values()],
        input_output_aliases={first_changed + i: first_out + i for i in range(len(changed))},
        scratch_shapes=[pltpu.VMEM(*shape) for shape in scratch.values()] + [pltpu.SemaphoreType.DMA((96,))],
        compiler_params=pltpu.CompilerParams(vmem_limit_bytes=VMEM_BYTES),
        cost_estimate=pl.CostEstimate(
            flops=(2 if stage == "turn" else 1) * 2 * rows * width * (12 * width + 4 * rows), bytes_accessed=20 * 2**20, transcendentals=0
        ),
        name=f"{stage}_{slot}",
    )(*inputs.values(), *held, *changed.values())
    return dict(zip([*outputs, *near_outputs, *changed], outs))


def shift(value, axis, steps):
    count = lax.axis_size(axis)
    pairs = [(place, place + steps) for place in range(max(0, -steps), min(count, count - steps))]
    return lax.ppermute(value, axis, pairs)


def add_over(value, axis):
    count = lax.axis_size(axis)
    if count & (count - 1):
        return lax.psum(value, axis)
    step = 1
    while step < count:
        value = value + lax.ppermute(value, axis, [(place, place ^ step) for place in range(count)])
        step *= 2
    return value


def body(tokens, doc_lengths, cotangent, *params):
    params = dict(zip(PARAMS, (item[0] if item.ndim == 3 else item for item in params)))
    micro, _, rows, width = tokens.shape
    hidden = params["ff1"].shape[1]
    scratch = scratch_of(rows, width, hidden)
    step = functools.partial(run, rows=rows, width=width, hidden=hidden)
    sheet = ((rows, width), bf16)
    sheets = ((micro, rows, width), bf16)
    kept_shapes = {"kept_" + name: ((micro,) + scratch[name][0], scratch[name][1]) for name in KEPT}
    common = dict(lengths=doc_lengths)
    resident = resident_of(width, hidden)

    done = step(
        "ahead", 0, dict(common, tokens=tokens, **params), {}, dict(kept_shapes, layer=sheets), dict(resident, sent=sheet), {}
    )
    near = {name: done[name] for name in PARAMS}
    to_second = [shift(done["sent"], "section", 1)]
    done = step(
        "ahead", 1, dict(common, tokens=tokens), near, {}, dict(sent=sheet), {name: done[name] for name in [*kept_shapes, "layer"]}
    )
    to_second.append(shift(done["sent"], "section", 1))
    kept = {name: done[name] for name in kept_shapes}
    sums = ((1, 6 * width + hidden), f32)
    layer_out, state = done["layer"], None
    to_first = []
    back = {name: near[name] for name in PARAMS[:6]}
    for slot in range(2):
        done = step("enter", slot, dict(common), dict(near, x=to_second[slot]), {}, {}, dict(kept, layer=layer_out))
        kept = {name: done[name] for name in kept_shapes}
        layer_out = done["layer"]
        fresh = dict(grad=sheets, totals=sums) if state is None else {}
        state = step("leave", slot, dict(common, cotangent=cotangent, **kept), back, fresh, dict(sent=sheet), state or {})
        to_first.append(shift(state.pop("sent"), "section", -1))
    for slot in range(2):
        state = step("back", slot, dict(common, **kept), dict(back, up=to_first[slot]), {}, {}, state)
    totals = add_over(state["totals"], "dp")
    places = [0, 2 * width, 3 * width, 4 * width, 4 * width + hidden, 5 * width + hidden, 6 * width + hidden]
    return (layer_out[None, :, None], state["grad"][None, :, None]) + tuple(
        totals[:, low:high] for low, high in zip(places[:-1], places[1:])
    )


def solution(mesh):
    in_specs = (
        P(None, "dp", None, None), P(None, "dp", None), P(None, "dp", None, None),
        P("section", None, None), P("section", None, None), P("section", None, None), P("section", None, None),
    ) + (P("section", None),) * 8
    out_specs = (P("section", None, "dp", None, None),) * 2 + (P("section", None),) * 6
    return jax.shard_map(body, mesh=mesh, in_specs=in_specs, out_specs=out_specs, check_vma=False)
```

```python
import functools
import math
import types
import jax
import jax.numpy as jnp
from jax import lax
from jax.experimental import pallas as pl
from jax.experimental.pallas import tpu as pltpu
from jax.sharding import PartitionSpec as P

HEAD_DIM = 64
LANES = 128
GROUP = 256
TILE = 1024
BLOCK = 256
ROWS = 128
PAIRS = 4
LIMITS = {}
LIMIT = 35
epsilon = 1e-05
masked_score = -1000000000.0
root_half = 0.7071067811865476
inverse_root_tau = 0.3989422804014327
f32 = jnp.float32
bf16 = jnp.bfloat16


def dot(left, right):
    return jnp.dot(left, right, preferred_element_type=f32)


def dot_back(left, right):
    return lax.dot_general(left, right, (((1,), (1,)), ((), ())), preferred_element_type=f32)


def beside(*parts):
    return jnp.concatenate(parts, axis=1)


def above(*parts):
    return jnp.concatenate(parts, axis=0)


def column_sum(value):
    return jnp.sum(value, axis=0, keepdims=True)


def row_norm(summed):
    middle = jnp.mean(summed, axis=-1, keepdims=True)
    centered = summed - middle
    inverse = lax.rsqrt(jnp.mean(centered * centered, axis=-1, keepdims=True) + epsilon)
    return centered * inverse, inverse


def row_norm_back(upstream, normed, inverse, gain):
    scaled = upstream * gain
    centered = scaled - jnp.mean(scaled, axis=-1, keepdims=True)
    return inverse * (centered - normed * jnp.mean(scaled * normed, axis=-1, keepdims=True))


def split_three(value):
    high = value.astype(bf16).astype(f32)
    rest = value - high
    middle = rest.astype(bf16).astype(f32)
    return high, middle, rest - middle


def strip(index, size):
    return pl.ds(pl.multiple_of(index * size, size), size)


class Copies:
    def __init__(self, semaphores):
        self.semaphores = semaphores
        self.used = 0

    def take(self, count=1):
        self.used += count
        return self.used - count

    def make(self, source, target, place=None):
        place = self.take() if place is None else place
        return pltpu.make_async_copy(source, target, self.semaphores.at[place])

    def start(self, source, target):
        return self.start_at(source, target, self.take())

    def start_at(self, source, target, place):
        copy = self.make(source, target, place)
        copy.start()
        return copy


def any_space(count):
    return [pl.BlockSpec(memory_space=pl.ANY)] * count


PARAMS = (
    "qkv", "out", "ff1", "ff2", "first_gain", "second_gain", "qv_bias", "out_bias", "first_shift", "ff1_bias", "ff2_bias",
    "second_shift",
)
KEPT = ("heads", "context", "marks", "one", "one_inverse", "slope", "two", "two_inverse")


def resident_of(width, hidden):
    groups, tiles = width // GROUP, hidden // TILE
    shapes = {
        "qkv": ((groups, width, 3 * width // groups), bf16),
        "out": ((width, width), bf16),
        "ff1": ((tiles, width, TILE), bf16),
        "ff2": ((tiles, TILE, width), bf16),
    }
    lengths = {"qv_bias": 3 * width, "ff1_bias": hidden}
    return shapes | {name: ((1, lengths.get(name, width)), f32) for name in PARAMS[4:]}


def scratch_of(rows, width, hidden):
    tiles = hidden // TILE
    return {
        "acc": ((rows, width), f32),
        "low": ((rows, width), bf16),
        "heads": ((rows, 3 * width), bf16),
        "context": ((rows, width), bf16),
        "marks": ((rows, LANES), bf16),
        "logsums": ((rows, LANES), f32),
        "one": ((rows, width), f32),
        "one_inverse": ((rows, LANES), f32),
        "slope": ((tiles, rows, TILE), bf16),
        "two": ((rows, width), bf16),
        "two_inverse": ((rows, LANES), f32),
        "grad_marks": ((rows, LANES), bf16),
        "totals": ((1, 6 * width + hidden), f32),
    }


class Layer:
    def __init__(self, hbm, vmem, semaphores, slot, base, span, keeping):
        self.hbm, self.vmem = hbm, vmem
        self.slot, self.base, self.span = slot, base, span
        self.keeping = keeping
        self.value = vmem.value if hasattr(vmem, "value") else getattr(vmem, "sent", None)
        self.copies = Copies(semaphores)
        self.groups, self.width, self.part = vmem.qkv.shape
        self.tiles = vmem.ff1.shape[0] if hasattr(vmem, "ff1") else 0
        self.qkv_place = self.copies.take(self.groups)
        self.out_place = self.copies.take()
        self.ff_place = self.copies.take(2 * self.tiles)
        self.small_place = self.copies.take(9)
        self.loading = hasattr(hbm, "qkv")
        self.kept_place = self.copies.take(len(KEPT))
        self.slope_place = self.copies.take(self.tiles)
        self.row_place = self.copies.take(2 * (span // ROWS))

    def qkv_copy(self, g):
        part = self.vmem.qkv.shape[2]
        return self.copies.make(self.hbm.qkv.at[:, strip(g, part)], self.vmem.qkv.at[g], self.qkv_place + g)

    def out_copy(self):
        return self.copies.make(self.hbm.out, self.vmem.out, self.out_place)

    def ff1_copy(self, t):
        return self.copies.make(self.hbm.ff1.at[:, strip(t, TILE)], self.vmem.ff1.at[t], self.ff_place + 2 * t)

    def ff2_copy(self, t):
        return self.copies.make(self.hbm.ff2.at[strip(t, TILE)], self.vmem.ff2.at[t], self.ff_place + 2 * t + 1)

    def small_copies(self):
        copies = []
        for name in PARAMS[4:]:
            source, target = getattr(self.hbm, name), getattr(self.vmem, name)
            if name == "qv_bias":
                copies.append((source.at[:, : self.width], target.at[:, : self.width]))
                copies.append((source.at[:, self.width :], target.at[:, 2 * self.width :]))
            else:
                copies.append((source, target))
        return [self.copies.make(*pair, self.small_place + index) for index, pair in enumerate(copies)]

    def start_weights(self):
        for g in range(self.groups):
            self.qkv_copy(g).start()
            if g == 0:
                for copy in self.small_copies():
                    copy.start()
        self.out_copy().start()
        for t in range(self.tiles):
            self.ff1_copy(t).start()
            self.ff2_copy(t).start()
        self.vmem.qv_bias[:, self.width : 2 * self.width] = jnp.zeros((1, self.width), f32)

    def wait_qkv(self, g):
        if self.loading:
            self.qkv_copy(g).wait()

    def wait_out(self):
        if self.loading:
            self.out_copy().wait()

    def wait_feed(self, t):
        if self.loading:
            self.ff1_copy(t).wait()
            self.ff2_copy(t).wait()

    def wait_small(self):
        if self.loading:
            for copy in self.small_copies():
                copy.wait()

    def wait_weights(self):
        self.wait_small()
        self.wait_out()
        for g in range(self.groups):
            self.wait_qkv(g)
        for t in range(self.tiles):
            self.wait_feed(t)

    def kept_copy(self, name, back):
        there, here = getattr(self.hbm, "kept_" + name).at[self.slot], getattr(self.vmem, name)
        if here.shape[0] == self.span:
            there = there.at[pl.ds(self.base, self.span)]
        place = self.kept_place + KEPT.index(name)
        return self.copies.make(there, here, place) if back else self.copies.make(here, there, place)

    def slope_copy(self, t, back):
        there, here = self.hbm.kept_slope.at[self.slot, t, pl.ds(self.base, self.span)], self.vmem.slope.at[t]
        return self.copies.make(there, here, self.slope_place + t) if back else self.copies.make(here, there, self.slope_place + t)

    def row_copy(self, name, target, index, size, part):
        here = (self.value if name == "sent" else getattr(self.vmem, name)).at[strip(index, size)]
        there = getattr(self.hbm, target).at[self.slot, pl.ds(self.base + pl.multiple_of(index * size, size), size)]
        return self.copies.make(here, there, self.row_place + 2 * index + part)

    def layer_copy(self, index):
        return self.row_copy("sent", "layer", index, ROWS, 0)

    def two_copy(self, index):
        return self.row_copy("two", "kept_two", index, ROWS, 1)

    def grad_copy(self, index):
        return self.row_copy("sent", "grad", index, BLOCK, 0)

    def keep(self, *names):
        if self.keeping:
            for name in names:
                self.kept_copy(name, False).start()

    def await_kept(self, back, *names):
        if self.keeping:
            for name in names:
                self.kept_copy(name, back).wait()

    def some_rows(self, ref):
        return ref if ref.shape[0] == self.span else ref.at[pl.ds(self.base, self.span)]

    def attend_forward(self):
        hbm, vmem, slot = self.hbm, self.vmem, self.slot
        width, groups, part = self.width, self.groups, self.part
        rows = vmem.heads.shape[0]
        segments = hbm.lengths.shape[2]

        def own_marks(start, count):
            place = start + lax.broadcasted_iota(jnp.int32, (count, LANES), 0)
            label = jnp.zeros((count, LANES), jnp.int32)
            end = jnp.int32(0)
            for index in range(segments):
                end = end + hbm.lengths[slot, 0, index]
                label = label + jnp.where(place >= end, 1, 0)
            lane = lax.broadcasted_iota(jnp.int32, (count, LANES), 1)
            return jnp.where(lane == label, 1.0, 0.0), lane

        own, lane = own_marks(0, rows)
        key_mark = jnp.where(lane < segments, (1.0 - own) * masked_score, 0.0).astype(bf16)
        query_mark = own.astype(bf16)
        vmem.logsums[...] = own
        half = lane < HEAD_DIM
        zero = jnp.zeros((rows, LANES), bf16)
        ones = jnp.ones((rows, LANES), bf16)
        head_lane = jnp.where((lane >= 16) & (lane < 64), lane & 15, -1)
        self.wait_small()
        if self.x_copy is not None:
            self.x_copy.wait()

        def project(g, carry):
            self.wait_qkv(g)
            columns = strip(g, part)
            vmem.heads[:, columns] = (dot(vmem.x[...], vmem.qkv[g]) + vmem.qv_bias[:, columns]).astype(bf16)
            return carry

        lax.fori_loop(0, groups, project, 0)
        self.keep("heads")

        def head_step(step, carry):
            count = 2 * PAIRS
            queries, keys, values = (
                vmem.heads[:, pl.ds(pl.multiple_of(at * width + step * PAIRS * LANES, LANES), PAIRS * LANES)] for at in range(3)
            )
            mixes, tops = [], []

            def score(local):
                pair, side = divmod(local, 2)
                chosen = slice(pair * LANES, (pair + 1) * LANES)
                scaled = queries[:, chosen] * jnp.asarray(HEAD_DIM**-0.5, bf16)
                left = jnp.where(half if side == 0 else ~half, scaled, zero)
                return dot_back(beside(left, query_mark), beside(keys[:, chosen], key_mark))

            scores = score(0)
            for local in range(count):
                following = score(local + 1) if local + 1 < count else None
                chosen = slice(local // 2 * LANES, (local // 2 + 1) * LANES)
                top = jnp.max(scores, axis=-1, keepdims=True)
                weights = jnp.exp(scores - top).astype(bf16)
                mixes.append(dot(weights, beside(values[:, chosen], ones)))
                tops.append(top)
                scores = following
            keep = vmem.logsums[...]
            parts = []
            for local in range(count):
                total = mixes[local][:, LANES:]
                parts.append(mixes[local][:, :LANES] / total)
                keep = jnp.where(head_lane == step * count + local, tops[local] + jnp.log(total), keep)
            vmem.logsums[...] = keep
            mixed = beside(*[jnp.where(half, parts[2 * p], parts[2 * p + 1]) for p in range(PAIRS)])
            vmem.context[:, strip(step, PAIRS * LANES)] = mixed.astype(bf16)
            return carry

        lax.fori_loop(0, width // (PAIRS * LANES), head_step, 0)
        high, middle, rest = split_three(vmem.logsums[...])
        vmem.marks[...] = jnp.where(lane < 32, high, jnp.where(lane < 48, middle, rest)).astype(bf16)
        self.keep("context", "marks")
        self.wait_out()

        def first_norm(index, carry):
            rows_ = strip(index, BLOCK)
            summed = vmem.x[rows_, :].astype(f32) + vmem.out_bias[...] + dot(vmem.context[rows_, :], vmem.out[...])
            one, one_inverse = row_norm(summed)
            vmem.one[rows_, :] = one
            vmem.one_inverse[rows_, :] = jnp.broadcast_to(one_inverse, (one.shape[0], LANES))
            value = one * vmem.first_gain[...] + vmem.first_shift[...]
            vmem.low[rows_, :] = value.astype(bf16)
            vmem.acc[rows_, :] = value + vmem.ff2_bias[...]
            return carry

        lax.fori_loop(0, rows // BLOCK, first_norm, 0)
        self.keep("one", "one_inverse")

    def feed_forward(self):
        vmem, span, tiles = self.vmem, self.span, self.tiles
        low, acc = self.some_rows(vmem.low), self.some_rows(vmem.acc)

        def tile_step(t, carry):
            self.wait_feed(t)
            bias = vmem.ff1_bias[:, strip(t, TILE)]
            acts = []
            for c in range(TILE // BLOCK):
                columns = slice(c * BLOCK, (c + 1) * BLOCK)
                h = dot(low[...], vmem.ff1[t, :, columns]) + bias[:, columns]
                share = 0.5 + 0.5 * lax.erf(h * root_half)
                vmem.slope[t, :, columns] = (share + h * jnp.exp(h * h * -0.5) * inverse_root_tau).astype(bf16)
                acts.append((h * share).astype(bf16))
            acc[...] += dot(beside(*acts), vmem.ff2[t])
            if self.keeping:
                self.slope_copy(t, False).start()
            return carry

        lax.fori_loop(0, tiles, tile_step, 0)

        def second_norm(index, carry):
            rows_ = strip(index, ROWS)
            two, two_inverse = row_norm(acc[rows_, :])
            self.value[rows_, :] = (two * vmem.second_gain[...] + vmem.second_shift[...]).astype(bf16)
            vmem.two[rows_, :] = two.astype(bf16)
            vmem.two_inverse[rows_, :] = jnp.broadcast_to(two_inverse, (ROWS, LANES))
            self.layer_copy(index).start()
            if self.keeping:
                self.two_copy(index).start()
            return carry

        lax.fori_loop(0, span // ROWS, second_norm, 0)
        self.keep("two_inverse")

    def finish_forward(self, *names):
        self.await_kept(False, *names)
        for index in range(self.span // ROWS):
            self.layer_copy(index).wait()
            if self.keeping:
                self.two_copy(index).wait()
        if self.keeping:
            for t in range(self.tiles):
                self.slope_copy(t, False).wait()

    def fetch_feed(self):
        for name in ("two", "two_inverse"):
            self.kept_copy(name, True).start()
        for t in range(self.tiles):
            self.slope_copy(t, True).start()

    def fetch_attend(self):
        for name in ("one", "one_inverse", "heads", "context", "marks"):
            self.kept_copy(name, True).start()

    def feed_backward(self):
        vmem, base, span = self.vmem, self.base, self.span
        width, tiles = self.width, self.tiles
        at_ff1 = 4 * width
        at_ff2 = at_ff1 + tiles * TILE
        at_second = at_ff2 + width
        totals, low = vmem.totals, vmem.low
        acc = self.some_rows(vmem.acc)
        self.await_kept(True, "two", "two_inverse")

        def second_back(index, carry):
            rows_ = strip(index, ROWS)
            upstream = vmem.up[rows_, :].astype(f32)
            grad = row_norm_back(upstream, vmem.two[rows_, :].astype(f32), vmem.two_inverse[rows_, :1], vmem.second_gain[...])
            low[rows_, :] = grad.astype(bf16)
            acc[rows_, :] = grad
            totals[:, at_second : at_second + width] += column_sum(upstream)
            totals[:, at_ff2 : at_ff2 + width] += column_sum(grad.astype(bf16).astype(f32))
            return carry

        lax.fori_loop(0, span // ROWS, second_back, 0)

        def tile_step(t, carry):
            if self.keeping:
                self.slope_copy(t, True).wait()
            grads, sums = [], []
            for c in range(TILE // BLOCK):
                columns = slice(c * BLOCK, (c + 1) * BLOCK)
                h = (dot_back(low[...], vmem.ff2[t, columns, :]) * vmem.slope[t, :, columns].astype(f32)).astype(bf16)
                sums.append(column_sum(h.astype(f32)))
                grads.append(h)
            totals[:, pl.ds(pl.multiple_of(at_ff1 + t * TILE, TILE), TILE)] += beside(*sums)
            acc[...] += dot_back(beside(*grads), vmem.ff1[t])
            return carry

        lax.fori_loop(0, tiles, tile_step, 0)

    def attend_backward(self):
        vmem, width, groups = self.vmem, self.width, self.groups
        rows = vmem.heads.shape[0]
        totals, acc = vmem.totals, vmem.acc
        at_out, at_first = 2 * width, 3 * width
        self.await_kept(True, "one", "one_inverse", "heads", "context", "marks")

        def first_back(index, carry):
            rows_ = strip(index, BLOCK)
            first_grad = acc[rows_, :]
            totals[:, at_first : at_first + width] += column_sum(first_grad)
            summed = row_norm_back(first_grad, vmem.one[rows_, :], vmem.one_inverse[rows_, :1], vmem.first_gain[...])
            acc[rows_, :] = summed
            attend_grad = summed.astype(bf16)
            totals[:, at_out : at_out + width] += column_sum(attend_grad.astype(f32))
            context_grad = dot_back(attend_grad, vmem.out[...]).astype(bf16)
            product = context_grad.astype(f32) * vmem.context[rows_, :].astype(f32)
            upper = product.astype(bf16)
            inner = dot(upper, pick) + dot((product - upper.astype(f32)).astype(bf16), pick)
            high, middle, rest = split_three(inner)
            place = lax.broadcasted_iota(jnp.int32, inner.shape, 1)
            vmem.grad_marks[rows_, :] = jnp.where(place < 16, high, jnp.where(place < 32, middle, rest)).astype(bf16)
            vmem.context[rows_, :] = context_grad
            return carry

        which = lax.broadcasted_iota(jnp.int32, (width, LANES), 0) // HEAD_DIM
        spot = lax.broadcasted_iota(jnp.int32, (width, LANES), 1)
        pick = jnp.where(((spot & 15) == which) & (spot < 48), 1.0, 0.0).astype(bf16)
        lax.fori_loop(0, rows // BLOCK, first_back, 0)
        lane = lax.broadcasted_iota(jnp.int32, (rows, LANES), 1)
        half = lane < HEAD_DIM
        zero = jnp.zeros((rows, LANES), bf16)
        query_mark = vmem.marks[...]
        key_mark = jnp.where(lane < 16, (1.0 - query_mark.astype(f32)) * masked_score, 0.0)
        head_lane = jnp.where((lane >= 16) & (lane < 64), lane & 15, -1)
        local_lane = jnp.where(lane < 48, lane & 15, -1)
        scale = HEAD_DIM**-0.5
        grad_mark = vmem.grad_marks[...]

        def head_step(step, carry):
            size = PAIRS * LANES
            spans = [pl.ds(pl.multiple_of(at * width + step * size, LANES), size) for at in range(3)]
            queries, all_keys, all_values = (vmem.heads[:, span] for span in spans)
            grads = vmem.context[:, strip(step, size)]
            query_grads, key_grads, value_grads = [], [], []
            for pair in range(PAIRS):
                chosen = slice(pair * LANES, (pair + 1) * LANES)
                query = queries[:, chosen] * jnp.asarray(scale, bf16)
                keys = all_keys[:, chosen]
                values = all_values[:, chosen]
                upper_grad = grads[:, chosen]
                query_turned = query.T
                grad_turned = upper_grad.T
                score_grads, keys_kept, key_turned, value_turned = [], [], [], []
                for side in range(2):
                    ours = half if side == 0 else ~half
                    mine = slice(side * HEAD_DIM, (side + 1) * HEAD_DIM)
                    head = step * 2 * PAIRS + pair * 2 + side
                    right = beside(keys, jnp.where(head_lane == head, -1.0, key_mark).astype(bf16))
                    probs = jnp.exp(dot_back(beside(jnp.where(ours, query, zero), query_mark), right))
                    right = beside(values, jnp.where(local_lane == head, -1.0, 0.0).astype(bf16))
                    score_grad = (probs * dot_back(beside(jnp.where(ours, upper_grad, zero), grad_mark), right)).astype(bf16)
                    value_turned.append(dot(grad_turned[mine], probs.astype(bf16)).astype(bf16))
                    key_turned.append(dot(query_turned[mine], score_grad).astype(bf16))
                    score_grads.append(score_grad)
                    keys_kept.append(jnp.where(ours, keys, zero))
                key_grads.append(above(*key_turned).T)
                value_grads.append(above(*value_turned).T)
                query_grads.append((dot(beside(*score_grads), above(*keys_kept)) * scale).astype(bf16))
            query_grad, key_grad, value_grad = beside(*query_grads), beside(*key_grads), beside(*value_grads)
            for span, grad in zip(spans, (query_grad, key_grad, value_grad)):
                vmem.heads[:, span] = grad
            totals[:, strip(step, size)] += column_sum(query_grad.astype(f32))
            totals[:, pl.ds(pl.multiple_of(width + step * size, LANES), size)] += column_sum(value_grad.astype(f32))
            return carry

        lax.fori_loop(0, width // (PAIRS * LANES), head_step, 0)
    def input_grad(self):
        vmem, base, span, part = self.vmem, self.base, self.span, self.part
        self.value = vmem.sent
        shift_by = base if vmem.acc.shape[0] != span else 0

        def input_step(index, carry):
            found = vmem.acc[pl.ds(shift_by + pl.multiple_of(index * BLOCK, BLOCK), BLOCK), :]
            rows_ = pl.ds(shift_by + pl.multiple_of(index * BLOCK, BLOCK), BLOCK)
            for g in range(self.groups):
                found = found + dot_back(vmem.heads[rows_, g * part : (g + 1) * part], vmem.qkv[g])
            vmem.sent[strip(index, BLOCK), :] = found.astype(bf16)
            self.grad_copy(index).start()
            return carry

        lax.fori_loop(0, span // BLOCK, input_step, 0)
        for index in range(span // BLOCK):
            self.grad_copy(index).wait()


def clear(ref):
    ref[...] = jnp.zeros_like(ref)


EVERY = False


def step_kernel(stage, slot, base, span, names, *refs):
    refs = dict(zip(names, refs))
    hbm = types.SimpleNamespace(**{name[4:]: ref for name, ref in refs.items() if name.startswith("hbm ")})
    vmem = types.SimpleNamespace(**{name[5:]: ref for name, ref in refs.items() if name.startswith("vmem ")})
    in_first = lax.axis_index("section") == 0
    working = jnp.logical_not(in_first) if stage in SECOND else in_first
    layer = Layer(hbm, vmem, refs["semaphores"], slot, base, span, stage != "turn")
    copies = layer.copies

    @pl.when(working)
    def _():
        if stage in ("open", "ahead", "enter", "turn"):
            layer.x_copy = None
            if stage in ("open", "ahead"):
                layer.x_copy = copies.start(hbm.tokens.at[slot, 0], vmem.x)
            elif hasattr(vmem, "x_low"):
                count = vmem.x_low.shape[0]
                vmem.x[:count, :] = vmem.x_low[...]
                vmem.x[count:, :] = vmem.x_high[...]
            if layer.loading:
                layer.start_weights()
            if stage == "turn":
                before = copies.start(hbm.totals, vmem.totals)
                up_copy = copies.start(hbm.cotangent.at[slot, 0], vmem.up)
            layer.attend_forward()
            later = []
            if stage == "open":
                rest = pl.ds(span, vmem.acc.shape[0] - span)
                later.append(copies.start(vmem.low.at[rest], hbm.more_low))
                later.append(copies.start(vmem.acc.at[rest], hbm.more_acc))
            layer.feed_forward()
            if stage != "turn":
                layer.finish_forward("heads", "context", "marks", "one", "one_inverse", "two_inverse")
            for copy in later:
                copy.wait()
        elif stage == "more":
            fetched = [copies.start(hbm.more_low, vmem.low), copies.start(hbm.more_acc, vmem.acc)]
            for copy in fetched:
                copy.wait()
            layer.feed_forward()
            layer.finish_forward("two_inverse")
        elif stage == "rest":
            fetched = [copies.start(hbm.tail_heads, vmem.heads), copies.start(hbm.tail_acc, vmem.acc)]
            for copy in fetched:
                copy.wait()
            layer.input_grad()
        if stage in ("leave", "turn", "back", "back part", "back whole"):
            if stage != "turn":
                before = None if slot == 0 else copies.start(hbm.totals, vmem.totals)
                up_copy = copies.start(hbm.cotangent.at[slot, 0], vmem.up) if stage == "leave" else None
                layer.fetch_feed()
                if stage == "back whole":
                    acc_copy = copies.start(hbm.acc_part, vmem.acc.at[pl.ds(0, base)])
                if stage != "back part":
                    layer.fetch_attend()
            if before is None:
                clear(vmem.totals)
            else:
                before.wait()
            if up_copy is not None:
                up_copy.wait()
            layer.feed_backward()
            if stage == "back whole":
                acc_copy.wait()
            if stage != "back part":
                layer.attend_backward()
            if stage == "turn":
                layer.finish_forward()
            after = [copies.start(vmem.totals, hbm.totals)]
            if stage == "back part":
                after.append(copies.start(vmem.acc, hbm.acc_part))
            else:
                if stage == "turn":
                    layer.base, layer.span = 0, vmem.sent.shape[0]
                    tail = pl.ds(layer.span, vmem.acc.shape[0] - layer.span)
                    after.append(copies.start(vmem.heads.at[tail], hbm.tail_heads))
                    after.append(copies.start(vmem.acc.at[tail], hbm.tail_acc))
                elif stage == "back whole":
                    layer.base, layer.span = 0, vmem.acc.shape[0]
                layer.input_grad()
            for copy in after:
                copy.wait()

    if layer.loading:
        @pl.when(jnp.logical_not(working))
        def _():
            layer.start_weights()
            layer.wait_weights()


FLOPS = 10**6
SECOND = ("enter", "leave", "turn", "rest")


def run(stage, slot, inputs, near, outputs, near_outputs, changed, rows, width, hidden, base=0, span=None):
    span = rows if span is None else span
    full, some = scratch_of(rows, width, hidden), scratch_of(span, width, hidden)
    feeding = ("slope", "two", "two_inverse")
    mixed = {name: some[name] if name in feeding else full[name] for name in full}
    if stage in ("open", "ahead", "enter"):
        scratch = {name: mixed[name] for name in mixed if name not in ("grad_marks", "totals")}
    elif stage == "more":
        scratch = {name: some[name] for name in ("acc", "low", *feeding)}
    elif stage == "rest":
        scratch = {name: some[name] for name in ("heads", "acc")}
    elif stage == "back part":
        scratch = {name: some[name] for name in ("acc", "low", "totals", *feeding)}
    else:
        scratch = dict(mixed, low=some["low"])
        if stage != "turn":
            del scratch["logsums"]
    if stage in ("open", "ahead", "enter"):
        scratch["x"] = ((rows, width), bf16)
    if stage in ("leave", "turn"):
        scratch["up"] = ((rows, width), bf16)
    if stage == "turn":
        scratch["value"] = ((rows, width), bf16)
    if stage != "back part":
        scratch["sent"] = ((rows, width), bf16)
    scratch = {name: shape for name, shape in scratch.items() if name not in near and name not in near_outputs}
    names = ["hbm " + name for name in inputs] + ["vmem " + name for name in near]
    names += ["hbm " + name + "_before" for name in changed]
    names += ["hbm " + name for name in outputs] + ["vmem " + name for name in near_outputs]
    names += ["hbm " + name for name in changed] + ["vmem " + name for name in scratch] + ["semaphores"]
    close = pl.BlockSpec(memory_space=pltpu.VMEM)
    specs = [pl.BlockSpec(memory_space=pltpu.SMEM if name == "lengths" else pl.ANY) for name in inputs]
    held = [pltpu.with_memory_space_constraint(item, pltpu.VMEM) for item in near.values()]
    first_changed, first_out = len(inputs) + len(near), len(outputs) + len(near_outputs)
    outs = pl.pallas_call(
        functools.partial(step_kernel, stage, slot, base, span, names),
        in_specs=specs + [close] * len(near) + any_space(len(changed)),
        out_specs=any_space(len(outputs)) + [close] * len(near_outputs) + any_space(len(changed)),
        out_shape=[jax.ShapeDtypeStruct(*shape) for shape in outputs.values()]
        + [pltpu.VMEM(*shape) for shape in near_outputs.values()]
        + [jax.ShapeDtypeStruct(item.shape, item.dtype) for item in changed.values()],
        input_output_aliases={first_changed + i: first_out + i for i in range(len(changed))},
        scratch_shapes=[pltpu.VMEM(*shape) for shape in scratch.values()] + [pltpu.SemaphoreType.DMA((96,))],
        compiler_params=pltpu.CompilerParams(vmem_limit_bytes=LIMITS.get(stage, LIMIT) * 2**20),
        cost_estimate=pl.CostEstimate(flops=FLOPS, bytes_accessed=2**16, transcendentals=0),
        name=f"{stage}_{slot}".replace(" ", "_"),
    )(*inputs.values(), *held, *changed.values())
    return dict(zip([*outputs, *near_outputs, *changed], outs))


def shift(value, axis, steps):
    count = lax.axis_size(axis)
    pairs = [(place, place + steps) for place in range(max(0, -steps), min(count, count - steps))]
    return lax.ppermute(value, axis, pairs)


def add_over(value, axis):
    count = lax.axis_size(axis)
    if count & (count - 1):
        return lax.psum(value, axis)

    def far(value, mask):
        return lax.ppermute(value, axis, [(place, place ^ mask) for place in range(count)])

    step = 1
    while step < count:
        if 2 * step < count:
            value = (value + far(value, step)) + (far(value, 2 * step) + far(value, 3 * step))
            step *= 4
        else:
            value = value + far(value, step)
            step *= 2
    return value


def body(tokens, doc_lengths, cotangent, *params):
    params = dict(zip(PARAMS, (item[0] if item.ndim == 3 else item for item in params)))
    micro, _, rows, width = tokens.shape
    hidden = params["ff1"].shape[1]
    scratch = scratch_of(rows, width, hidden)
    step = functools.partial(run, rows=rows, width=width, hidden=hidden)
    sheet = ((rows, width), bf16)
    sheets = ((micro, rows, width), bf16)
    kept_shapes = {"kept_" + name: ((micro,) + scratch[name][0], scratch[name][1]) for name in KEPT}
    lengths = dict(lengths=doc_lengths)
    resident = resident_of(width, hidden)
    half = rows // 2
    part, sums = ((half, width), bf16), ((1, 6 * width + hidden), f32)
    kept_names = [*kept_shapes, "layer"]

    def tails(*names):
        shapes = {"low": (width, bf16), "acc": (width, f32), "heads": (3 * width, bf16)}
        return {name: ((rows - half, shapes[name.split("_")[1]][0]), shapes[name.split("_")[1]][1]) for name in names}

    done = step(
        "open", 0, dict(lengths, tokens=tokens, **params), {}, dict(kept_shapes, layer=sheets, **tails("more_low", "more_acc")),
        dict(resident, sent=part), {}, span=half,
    )
    near = {name: done[name] for name in PARAMS}
    back = {name: near[name] for name in PARAMS[:6]}
    x_low = shift(done["sent"], "section", 1)
    done = step(
        "more", 0, {name: done[name] for name in ("more_low", "more_acc")}, near, {}, dict(sent=part),
        {name: done[name] for name in kept_names}, base=half, span=rows - half,
    )
    x_high = shift(done["sent"], "section", 1)
    x_low, layer = lax.optimization_barrier((x_low, done["layer"]))
    done = step(
        "ahead", 1, dict(lengths, tokens=tokens), near, {}, dict(sent=sheet),
        dict({name: done[name] for name in kept_names}, layer=layer),
    )
    x = shift(done["sent"], "section", 1)
    kept = {name: done[name] for name in kept_names}

    kept = step("enter", 0, lengths, dict(near, x_low=x_low, x_high=x_high), {}, {}, kept)
    stored = {name: kept[name] for name in kept_shapes}
    state = step("leave", 0, dict(stored, cotangent=cotangent), back, dict(grad=sheets, totals=sums), dict(sent=sheet), {})
    up = shift(state.pop("sent"), "section", -1)
    state = step(
        "turn", 1, dict(lengths, cotangent=cotangent), dict(near, x=x), tails("tail_heads", "tail_acc"), dict(sent=part),
        dict(state, layer=kept["layer"]),
    )
    layer_out = state["layer"]
    up_low = shift(state["sent"], "section", -1)
    totals = state["totals"]
    state = step(
        "rest", 1, {name: state[name] for name in ("tail_heads", "tail_acc")}, back, {}, dict(sent=part),
        dict(grad=state["grad"]), base=half, span=rows - half,
    )
    up_high = shift(state["sent"], "section", -1)
    state = step("back", 0, stored, dict(back, up=up), {}, {}, dict(grad=state["grad"], totals=totals))
    grad = state["grad"]
    state = step(
        "back part", 1, stored, dict(back, up=up_low), dict(acc_part=((half, width), f32)), {}, dict(totals=state["totals"]),
        span=half,
    )
    state = step(
        "back whole", 1, dict(stored, acc_part=state["acc_part"]), dict(back, up=up_high), {}, {},
        dict(grad=grad, totals=state["totals"]), base=half, span=rows - half,
    )
    totals = add_over(state["totals"], "dp")
    places = [0, 2 * width, 3 * width, 4 * width, 4 * width + hidden, 5 * width + hidden, 6 * width + hidden]
    return (layer_out[None, :, None], state["grad"][None, :, None]) + tuple(
        totals[:, low:high] for low, high in zip(places[:-1], places[1:])
    )


def solution(mesh):
    in_specs = (
        P(None, "dp", None, None), P(None, "dp", None), P(None, "dp", None, None),
        P("section", None, None), P("section", None, None), P("section", None, None), P("section", None, None),
    ) + (P("section", None),) * 8
    out_specs = (P("section", None, "dp", None, None),) * 2 + (P("section", None),) * 6
    return jax.shard_map(body, mesh=mesh, in_specs=in_specs, out_specs=out_specs, check_vma=False)
```

```python
import functools
import math
import types
import jax
import jax.numpy as jnp
from jax import lax
from jax.experimental import pallas as pl
from jax.experimental.pallas import tpu as pltpu
from jax.sharding import PartitionSpec as P

HEAD_DIM = 64
LANES = 128
GROUP = 256
TILE = 1024
BLOCK = 256
ROWS = 128
PAIRS = 4
LIMITS = {}
LIMIT = 35
epsilon = 1e-05
masked_score = -1000000000.0
root_half = 0.7071067811865476
inverse_root_tau = 0.3989422804014327
f32 = jnp.float32
bf16 = jnp.bfloat16


def dot(left, right):
    return jnp.dot(left, right, preferred_element_type=f32)


def dot_back(left, right):
    return lax.dot_general(left, right, (((1,), (1,)), ((), ())), preferred_element_type=f32)


def beside(*parts):
    return jnp.concatenate(parts, axis=1)


def above(*parts):
    return jnp.concatenate(parts, axis=0)


def column_sum(value):
    return jnp.sum(value, axis=0, keepdims=True)


def row_norm(summed):
    middle = jnp.mean(summed, axis=-1, keepdims=True)
    centered = summed - middle
    inverse = lax.rsqrt(jnp.mean(centered * centered, axis=-1, keepdims=True) + epsilon)
    return centered * inverse, inverse


def row_norm_back(upstream, normed, inverse, gain):
    scaled = upstream * gain
    centered = scaled - jnp.mean(scaled, axis=-1, keepdims=True)
    return inverse * (centered - normed * jnp.mean(scaled * normed, axis=-1, keepdims=True))


def split_three(value):
    high = value.astype(bf16).astype(f32)
    rest = value - high
    middle = rest.astype(bf16).astype(f32)
    return high, middle, rest - middle


def spread(value):
    lane = lax.broadcasted_iota(jnp.int32, value.shape, 1)
    high, middle, low = split_three(value)
    return jnp.where(lane < 16, high, jnp.where(lane < 32, middle, low)).astype(bf16)


def strip(index, size):
    return pl.ds(pl.multiple_of(index * size, size), size)


class Copies:
    def __init__(self, semaphores):
        self.semaphores = semaphores
        self.used = 0

    def take(self, count=1):
        self.used += count
        return self.used - count

    def make(self, source, target, place=None):
        place = self.take() if place is None else place
        return pltpu.make_async_copy(source, target, self.semaphores.at[place])

    def start(self, source, target):
        return self.start_at(source, target, self.take())

    def start_at(self, source, target, place):
        copy = self.make(source, target, place)
        copy.start()
        return copy


def any_space(count):
    return [pl.BlockSpec(memory_space=pl.ANY)] * count


PARAMS = (
    "qkv", "out", "ff1", "ff2", "first_gain", "second_gain", "qv_bias", "out_bias", "first_shift", "ff1_bias", "ff2_bias",
    "second_shift",
)
KEPT = ("heads", "context", "shares", "weights", "one", "one_inverse", "slope", "two", "two_inverse")


def resident_of(width, hidden):
    groups, tiles = width // GROUP, hidden // TILE
    shapes = {
        "qkv": ((groups, width, 3 * width // groups), bf16),
        "out": ((width, width), bf16),
        "ff1": ((tiles, width, TILE), bf16),
        "ff2": ((tiles, TILE, width), bf16),
    }
    lengths = {"qv_bias": 3 * width, "ff1_bias": hidden}
    return shapes | {name: ((1, lengths.get(name, width)), f32) for name in PARAMS[4:]}


def scratch_of(rows, width, hidden):
    tiles = hidden // TILE
    return {
        "acc": ((rows, width), f32),
        "low": ((rows, width), bf16),
        "heads": ((rows, 3 * width), bf16),
        "context": ((rows, width), bf16),
        "shares": ((rows, LANES), f32),
        "weights": ((width // HEAD_DIM, rows, rows), bf16),
        "one": ((rows, width), f32),
        "one_inverse": ((rows, LANES), f32),
        "slope": ((tiles, rows, TILE), bf16),
        "two": ((rows, width), bf16),
        "two_inverse": ((rows, LANES), f32),
        "grad_marks": ((rows, LANES), bf16),
        "totals": ((1, 6 * width + hidden), f32),
    }


class Layer:
    def __init__(self, hbm, vmem, semaphores, slot, base, span, keeping):
        self.hbm, self.vmem = hbm, vmem
        self.slot, self.base, self.span = slot, base, span
        self.keeping = keeping
        self.value = vmem.value if hasattr(vmem, "value") else getattr(vmem, "sent", None)
        self.copies = Copies(semaphores)
        self.groups, self.width, self.part = vmem.qkv.shape
        self.tiles = vmem.ff1.shape[0] if hasattr(vmem, "ff1") else 0
        self.qkv_place = self.copies.take(self.groups)
        self.out_place = self.copies.take()
        self.ff_place = self.copies.take(2 * self.tiles)
        self.small_place = self.copies.take(9)
        self.loading = hasattr(hbm, "qkv")
        self.kept_place = self.copies.take(len(KEPT))
        self.slope_place = self.copies.take(self.tiles)
        self.row_place = self.copies.take(2 * (span // ROWS))

    def qkv_copy(self, g):
        part = self.vmem.qkv.shape[2]
        return self.copies.make(self.hbm.qkv.at[:, strip(g, part)], self.vmem.qkv.at[g], self.qkv_place + g)

    def out_copy(self):
        return self.copies.make(self.hbm.out, self.vmem.out, self.out_place)

    def ff1_copy(self, t):
        return self.copies.make(self.hbm.ff1.at[:, strip(t, TILE)], self.vmem.ff1.at[t], self.ff_place + 2 * t)

    def ff2_copy(self, t):
        return self.copies.make(self.hbm.ff2.at[strip(t, TILE)], self.vmem.ff2.at[t], self.ff_place + 2 * t + 1)

    def small_copies(self):
        copies = []
        for name in PARAMS[4:]:
            source, target = getattr(self.hbm, name), getattr(self.vmem, name)
            if name == "qv_bias":
                copies.append((source.at[:, : self.width], target.at[:, : self.width]))
                copies.append((source.at[:, self.width :], target.at[:, 2 * self.width :]))
            else:
                copies.append((source, target))
        return [self.copies.make(*pair, self.small_place + index) for index, pair in enumerate(copies)]

    def start_weights(self):
        for g in range(self.groups):
            self.qkv_copy(g).start()
            if g == 0:
                for copy in self.small_copies():
                    copy.start()
        self.out_copy().start()
        for t in range(self.tiles):
            self.ff1_copy(t).start()
            self.ff2_copy(t).start()
        self.vmem.qv_bias[:, self.width : 2 * self.width] = jnp.zeros((1, self.width), f32)

    def wait_qkv(self, g):
        if self.loading:
            self.qkv_copy(g).wait()

    def wait_out(self):
        if self.loading:
            self.out_copy().wait()

    def wait_feed(self, t):
        if self.loading:
            self.ff1_copy(t).wait()
            self.ff2_copy(t).wait()

    def wait_small(self):
        if self.loading:
            for copy in self.small_copies():
                copy.wait()

    def wait_weights(self):
        self.wait_small()
        self.wait_out()
        for g in range(self.groups):
            self.wait_qkv(g)
        for t in range(self.tiles):
            self.wait_feed(t)

    def kept_copy(self, name, back):
        there, here = getattr(self.hbm, "kept_" + name).at[self.slot], getattr(self.vmem, name)
        if here.shape[0] == self.span:
            there = there.at[pl.ds(self.base, self.span)]
        place = self.kept_place + KEPT.index(name)
        return self.copies.make(there, here, place) if back else self.copies.make(here, there, place)

    def slope_copy(self, t, back):
        there, here = self.hbm.kept_slope.at[self.slot, t, pl.ds(self.base, self.span)], self.vmem.slope.at[t]
        return self.copies.make(there, here, self.slope_place + t) if back else self.copies.make(here, there, self.slope_place + t)

    def row_copy(self, name, target, index, size, part):
        here = (self.value if name == "sent" else getattr(self.vmem, name)).at[strip(index, size)]
        there = getattr(self.hbm, target).at[self.slot, pl.ds(self.base + pl.multiple_of(index * size, size), size)]
        return self.copies.make(here, there, self.row_place + 2 * index + part)

    def layer_copy(self, index):
        return self.row_copy("sent", "layer", index, ROWS, 0)

    def two_copy(self, index):
        return self.row_copy("two", "kept_two", index, ROWS, 1)

    def grad_copy(self, index):
        return self.row_copy("sent", "grad", index, BLOCK, 0)

    def keep(self, *names):
        if self.keeping:
            for name in names:
                self.kept_copy(name, False).start()

    def await_kept(self, back, *names):
        if self.keeping:
            for name in names:
                self.kept_copy(name, back).wait()

    def some_rows(self, ref):
        return ref if ref.shape[0] == self.span else ref.at[pl.ds(self.base, self.span)]

    def attend_forward(self):
        hbm, vmem, slot = self.hbm, self.vmem, self.slot
        width, groups, part = self.width, self.groups, self.part
        rows = vmem.heads.shape[0]
        segments = hbm.lengths.shape[2]

        def own_marks(start, count):
            place = start + lax.broadcasted_iota(jnp.int32, (count, LANES), 0)
            label = jnp.zeros((count, LANES), jnp.int32)
            end = jnp.int32(0)
            for index in range(segments):
                end = end + hbm.lengths[slot, 0, index]
                label = label + jnp.where(place >= end, 1, 0)
            lane = lax.broadcasted_iota(jnp.int32, (count, LANES), 1)
            return jnp.where(lane == label, 1.0, 0.0), lane

        own, lane = own_marks(0, rows)
        key_mark = jnp.where(lane < segments, (1.0 - own) * masked_score, 0.0).astype(bf16)
        query_mark = own.astype(bf16)
        clear(vmem.shares)
        half = lane < HEAD_DIM
        zero = jnp.zeros((rows, LANES), bf16)
        ones = jnp.ones((rows, LANES), bf16)
        head_lane = jnp.where(lane < 48, lane & 15, -1)
        self.wait_small()
        if self.x_copy is not None:
            self.x_copy.wait()

        def project(g, carry):
            self.wait_qkv(g)
            columns = strip(g, part)
            vmem.heads[:, columns] = (dot(vmem.x[...], vmem.qkv[g]) + vmem.qv_bias[:, columns]).astype(bf16)
            return carry

        lax.fori_loop(0, groups, project, 0)
        self.keep("heads")

        def head_step(step, carry):
            count = 2 * PAIRS
            queries, keys, values = (
                vmem.heads[:, pl.ds(pl.multiple_of(at * width + step * PAIRS * LANES, LANES), PAIRS * LANES)] for at in range(3)
            )
            mixes = []

            def score(local):
                pair, side = divmod(local, 2)
                chosen = slice(pair * LANES, (pair + 1) * LANES)
                scaled = queries[:, chosen] * jnp.asarray(HEAD_DIM**-0.5, bf16)
                left = jnp.where(half if side == 0 else ~half, scaled, zero)
                return dot_back(beside(left, query_mark), beside(keys[:, chosen], key_mark))

            scores = score(0)
            for local in range(count):
                following = score(local + 1) if local + 1 < count else None
                chosen = slice(local // 2 * LANES, (local // 2 + 1) * LANES)
                top = jnp.max(scores, axis=-1, keepdims=True)
                weights = jnp.exp(scores - top).astype(bf16)
                vmem.weights[step * count + local] = weights
                mixes.append(dot(weights, beside(values[:, chosen], ones)))
                scores = following
            keep = vmem.shares[...]
            parts = []
            for local in range(count):
                share = 1.0 / mixes[local][:, LANES:]
                parts.append(mixes[local][:, :LANES] * share)
                keep = jnp.where(head_lane == step * count + local, share, keep)
            vmem.shares[...] = keep
            mixed = beside(*[jnp.where(half, parts[2 * p], parts[2 * p + 1]) for p in range(PAIRS)])
            vmem.context[:, strip(step, PAIRS * LANES)] = mixed.astype(bf16)
            return carry

        lax.fori_loop(0, width // (PAIRS * LANES), head_step, 0)
        self.keep("context", "shares", "weights")
        self.wait_out()

        def first_norm(index, carry):
            rows_ = strip(index, BLOCK)
            summed = vmem.x[rows_, :].astype(f32) + vmem.out_bias[...] + dot(vmem.context[rows_, :], vmem.out[...])
            one, one_inverse = row_norm(summed)
            vmem.one[rows_, :] = one
            vmem.one_inverse[rows_, :] = jnp.broadcast_to(one_inverse, (one.shape[0], LANES))
            value = one * vmem.first_gain[...] + vmem.first_shift[...]
            vmem.low[rows_, :] = value.astype(bf16)
            vmem.acc[rows_, :] = value + vmem.ff2_bias[...]
            return carry

        lax.fori_loop(0, rows // BLOCK, first_norm, 0)
        self.keep("one", "one_inverse")

    def feed_forward(self):
        vmem, span, tiles = self.vmem, self.span, self.tiles
        low, acc = self.some_rows(vmem.low), self.some_rows(vmem.acc)

        def tile_step(t, carry):
            self.wait_feed(t)
            bias = vmem.ff1_bias[:, strip(t, TILE)]
            acts = []
            for c in range(TILE // BLOCK):
                columns = slice(c * BLOCK, (c + 1) * BLOCK)
                h = dot(low[...], vmem.ff1[t, :, columns]) + bias[:, columns]
                share = 0.5 + 0.5 * lax.erf(h * root_half)
                vmem.slope[t, :, columns] = (share + h * jnp.exp(h * h * -0.5) * inverse_root_tau).astype(bf16)
                acts.append((h * share).astype(bf16))
            acc[...] += dot(beside(*acts), vmem.ff2[t])
            if self.keeping:
                self.slope_copy(t, False).start()
            return carry

        lax.fori_loop(0, tiles, tile_step, 0)

        def second_norm(index, carry):
            rows_ = strip(index, ROWS)
            two, two_inverse = row_norm(acc[rows_, :])
            self.value[rows_, :] = (two * vmem.second_gain[...] + vmem.second_shift[...]).astype(bf16)
            vmem.two[rows_, :] = two.astype(bf16)
            vmem.two_inverse[rows_, :] = jnp.broadcast_to(two_inverse, (ROWS, LANES))
            self.layer_copy(index).start()
            if self.keeping:
                self.two_copy(index).start()
            return carry

        lax.fori_loop(0, span // ROWS, second_norm, 0)
        self.keep("two_inverse")

    def finish_forward(self, *names):
        self.await_kept(False, *names)
        for index in range(self.span // ROWS):
            self.layer_copy(index).wait()
            if self.keeping:
                self.two_copy(index).wait()
        if self.keeping:
            for t in range(self.tiles):
                self.slope_copy(t, False).wait()

    def fetch_feed(self):
        for name in ("two", "two_inverse"):
            self.kept_copy(name, True).start()
        for t in range(self.tiles):
            self.slope_copy(t, True).start()

    def fetch_attend(self):
        for name in ("one", "one_inverse", "context", "shares", "heads", "weights"):
            self.kept_copy(name, True).start()

    def feed_backward(self):
        vmem, base, span = self.vmem, self.base, self.span
        width, tiles = self.width, self.tiles
        at_ff1 = 4 * width
        at_ff2 = at_ff1 + tiles * TILE
        at_second = at_ff2 + width
        totals, low = vmem.totals, vmem.low
        acc = self.some_rows(vmem.acc)
        self.await_kept(True, "two", "two_inverse")

        def second_back(index, carry):
            rows_ = strip(index, ROWS)
            upstream = vmem.up[rows_, :].astype(f32)
            grad = row_norm_back(upstream, vmem.two[rows_, :].astype(f32), vmem.two_inverse[rows_, :1], vmem.second_gain[...])
            low[rows_, :] = grad.astype(bf16)
            acc[rows_, :] = grad
            totals[:, at_second : at_second + width] += column_sum(upstream)
            totals[:, at_ff2 : at_ff2 + width] += column_sum(grad.astype(bf16).astype(f32))
            return carry

        lax.fori_loop(0, span // ROWS, second_back, 0)

        def tile_step(t, carry):
            if self.keeping:
                self.slope_copy(t, True).wait()
            grads, sums = [], []
            for c in range(TILE // BLOCK):
                columns = slice(c * BLOCK, (c + 1) * BLOCK)
                h = (dot_back(low[...], vmem.ff2[t, columns, :]) * vmem.slope[t, :, columns].astype(f32)).astype(bf16)
                sums.append(column_sum(h.astype(f32)))
                grads.append(h)
            totals[:, pl.ds(pl.multiple_of(at_ff1 + t * TILE, TILE), TILE)] += beside(*sums)
            acc[...] += dot_back(beside(*grads), vmem.ff1[t])
            return carry

        lax.fori_loop(0, tiles, tile_step, 0)

    def attend_backward(self):
        vmem, width, groups = self.vmem, self.width, self.groups
        rows = vmem.heads.shape[0]
        totals, acc = vmem.totals, vmem.acc
        at_out, at_first = 2 * width, 3 * width
        self.await_kept(True, "one", "one_inverse", "context", "shares")

        def first_back(index, carry):
            rows_ = strip(index, BLOCK)
            first_grad = acc[rows_, :]
            totals[:, at_first : at_first + width] += column_sum(first_grad)
            summed = row_norm_back(first_grad, vmem.one[rows_, :], vmem.one_inverse[rows_, :1], vmem.first_gain[...])
            acc[rows_, :] = summed
            attend_grad = summed.astype(bf16)
            totals[:, at_out : at_out + width] += column_sum(attend_grad.astype(f32))
            shares = spread(vmem.shares[rows_, :])
            context_grad = (dot_back(attend_grad, vmem.out[...]) * dot_back(shares, pick)).astype(bf16)
            product = context_grad.astype(f32) * vmem.context[rows_, :].astype(f32)
            upper = product.astype(bf16)
            inner = dot(upper, pick) + dot((product - upper.astype(f32)).astype(bf16), pick)
            vmem.grad_marks[rows_, :] = spread(inner)
            vmem.context[rows_, :] = context_grad
            return carry

        which = lax.broadcasted_iota(jnp.int32, (width, LANES), 0) // HEAD_DIM
        spot = lax.broadcasted_iota(jnp.int32, (width, LANES), 1)
        pick = jnp.where(((spot & 15) == which) & (spot < 48), 1.0, 0.0).astype(bf16)
        lax.fori_loop(0, rows // BLOCK, first_back, 0)
        lane = lax.broadcasted_iota(jnp.int32, (rows, LANES), 1)
        half = lane < HEAD_DIM
        zero = jnp.zeros((rows, LANES), bf16)
        local_lane = jnp.where(lane < 48, lane & 15, -1)
        self.await_kept(True, "heads", "weights")
        scale = HEAD_DIM**-0.5
        grad_mark = vmem.grad_marks[...]

        def head_step(step, carry):
            size = PAIRS * LANES
            spans = [pl.ds(pl.multiple_of(at * width + step * size, LANES), size) for at in range(3)]
            queries, all_keys, all_values = (vmem.heads[:, span] for span in spans)
            grads = vmem.context[:, strip(step, size)]
            query_grads, key_grads, value_grads = [], [], []
            for pair in range(PAIRS):
                chosen = slice(pair * LANES, (pair + 1) * LANES)
                query = queries[:, chosen] * jnp.asarray(scale, bf16)
                keys = all_keys[:, chosen]
                values = all_values[:, chosen]
                upper_grad = grads[:, chosen]
                query_turned = query.T
                grad_turned = upper_grad.T
                score_grads, keys_kept, key_turned, value_turned = [], [], [], []
                for side in range(2):
                    ours = half if side == 0 else ~half
                    mine = slice(side * HEAD_DIM, (side + 1) * HEAD_DIM)
                    head = step * 2 * PAIRS + pair * 2 + side
                    weights = vmem.weights[head]
                    right = beside(values, jnp.where(local_lane == head, -1.0, 0.0).astype(bf16))
                    score_grad = (weights.astype(f32) * dot_back(beside(jnp.where(ours, upper_grad, zero), grad_mark), right)).astype(bf16)
                    value_turned.append(dot(grad_turned[mine], weights).astype(bf16))
                    key_turned.append(dot(query_turned[mine], score_grad).astype(bf16))
                    score_grads.append(score_grad)
                    keys_kept.append(jnp.where(ours, keys, zero))
                key_grads.append(above(*key_turned).T)
                value_grads.append(above(*value_turned).T)
                query_grads.append((dot(beside(*score_grads), above(*keys_kept)) * scale).astype(bf16))
            query_grad, key_grad, value_grad = beside(*query_grads), beside(*key_grads), beside(*value_grads)
            for span, grad in zip(spans, (query_grad, key_grad, value_grad)):
                vmem.heads[:, span] = grad
            totals[:, strip(step, size)] += column_sum(query_grad.astype(f32))
            totals[:, pl.ds(pl.multiple_of(width + step * size, LANES), size)] += column_sum(value_grad.astype(f32))
            return carry

        lax.fori_loop(0, width // (PAIRS * LANES), head_step, 0)
    def input_grad(self):
        vmem, base, span, part = self.vmem, self.base, self.span, self.part
        self.value = vmem.sent
        shift_by = base if vmem.acc.shape[0] != span else 0

        def input_step(index, carry):
            found = vmem.acc[pl.ds(shift_by + pl.multiple_of(index * BLOCK, BLOCK), BLOCK), :]
            rows_ = pl.ds(shift_by + pl.multiple_of(index * BLOCK, BLOCK), BLOCK)
            for g in range(self.groups):
                found = found + dot_back(vmem.heads[rows_, g * part : (g + 1) * part], vmem.qkv[g])
            vmem.sent[strip(index, BLOCK), :] = found.astype(bf16)
            self.grad_copy(index).start()
            return carry

        lax.fori_loop(0, span // BLOCK, input_step, 0)
        for index in range(span // BLOCK):
            self.grad_copy(index).wait()


def clear(ref):
    ref[...] = jnp.zeros_like(ref)


EVERY = False


def step_kernel(stage, slot, base, span, names, *refs):
    refs = dict(zip(names, refs))
    hbm = types.SimpleNamespace(**{name[4:]: ref for name, ref in refs.items() if name.startswith("hbm ")})
    vmem = types.SimpleNamespace(**{name[5:]: ref for name, ref in refs.items() if name.startswith("vmem ")})
    in_first = lax.axis_index("section") == 0
    working = jnp.logical_not(in_first) if stage in SECOND else in_first
    layer = Layer(hbm, vmem, refs["semaphores"], slot, base, span, stage != "turn")
    copies = layer.copies

    @pl.when(working)
    def _():
        if stage in ("open", "ahead", "enter", "turn"):
            layer.x_copy = None
            if stage in ("open", "ahead"):
                layer.x_copy = copies.start(hbm.tokens.at[slot, 0], vmem.x)
            elif hasattr(vmem, "x_low"):
                count = vmem.x_low.shape[0]
                vmem.x[:count, :] = vmem.x_low[...]
                vmem.x[count:, :] = vmem.x_high[...]
            if layer.loading:
                layer.start_weights()
            if stage == "turn":
                before = copies.start(hbm.totals, vmem.totals)
                up_copy = copies.start(hbm.cotangent.at[slot, 0], vmem.up)
            layer.attend_forward()
            later = []
            if stage == "open":
                rest = pl.ds(span, vmem.acc.shape[0] - span)
                later.append(copies.start(vmem.low.at[rest], hbm.more_low))
                later.append(copies.start(vmem.acc.at[rest], hbm.more_acc))
            layer.feed_forward()
            if stage != "turn":
                layer.finish_forward("heads", "context", "shares", "weights", "one", "one_inverse", "two_inverse")
            for copy in later:
                copy.wait()
        elif stage == "more":
            fetched = [copies.start(hbm.more_low, vmem.low), copies.start(hbm.more_acc, vmem.acc)]
            for copy in fetched:
                copy.wait()
            layer.feed_forward()
            layer.finish_forward("two_inverse")
        elif stage == "rest":
            fetched = [copies.start(hbm.tail_heads, vmem.heads), copies.start(hbm.tail_acc, vmem.acc)]
            for copy in fetched:
                copy.wait()
            layer.input_grad()
        if stage in ("leave", "turn", "back", "back part", "back whole"):
            if stage != "turn":
                before = None if slot == 0 else copies.start(hbm.totals, vmem.totals)
                up_copy = copies.start(hbm.cotangent.at[slot, 0], vmem.up) if stage == "leave" else None
                layer.fetch_feed()
                if stage == "back whole":
                    acc_copy = copies.start(hbm.acc_part, vmem.acc.at[pl.ds(0, base)])
                if stage != "back part":
                    layer.fetch_attend()
            if before is None:
                clear(vmem.totals)
            else:
                before.wait()
            if up_copy is not None:
                up_copy.wait()
            layer.feed_backward()
            if stage == "back whole":
                acc_copy.wait()
            if stage != "back part":
                layer.attend_backward()
            if stage == "turn":
                layer.finish_forward()
            after = [copies.start(vmem.totals, hbm.totals)]
            if stage == "back part":
                after.append(copies.start(vmem.acc, hbm.acc_part))
            else:
                if stage == "turn":
                    layer.base, layer.span = 0, vmem.sent.shape[0]
                    tail = pl.ds(layer.span, vmem.acc.shape[0] - layer.span)
                    after.append(copies.start(vmem.heads.at[tail], hbm.tail_heads))
                    after.append(copies.start(vmem.acc.at[tail], hbm.tail_acc))
                elif stage == "back whole":
                    layer.base, layer.span = 0, vmem.acc.shape[0]
                layer.input_grad()
            for copy in after:
                copy.wait()

    if layer.loading:
        @pl.when(jnp.logical_not(working))
        def _():
            layer.start_weights()
            layer.wait_weights()


FLOPS = 10**6
SECOND = ("enter", "leave", "turn", "rest")


def run(stage, slot, inputs, near, outputs, near_outputs, changed, rows, width, hidden, base=0, span=None):
    span = rows if span is None else span
    full, some = scratch_of(rows, width, hidden), scratch_of(span, width, hidden)
    feeding = ("slope", "two", "two_inverse")
    mixed = {name: some[name] if name in feeding else full[name] for name in full}
    if stage in ("open", "ahead", "enter"):
        scratch = {name: mixed[name] for name in mixed if name not in ("grad_marks", "totals")}
    elif stage == "more":
        scratch = {name: some[name] for name in ("acc", "low", *feeding)}
    elif stage == "rest":
        scratch = {name: some[name] for name in ("heads", "acc")}
    elif stage == "back part":
        scratch = {name: some[name] for name in ("acc", "low", "totals", *feeding)}
    else:
        scratch = dict(mixed, low=some["low"])
    if stage in ("open", "ahead", "enter"):
        scratch["x"] = ((rows, width), bf16)
    if stage in ("leave", "turn"):
        scratch["up"] = ((rows, width), bf16)
    if stage == "turn":
        scratch["value"] = ((rows, width), bf16)
    if stage != "back part":
        scratch["sent"] = ((rows, width), bf16)
    scratch = {name: shape for name, shape in scratch.items() if name not in near and name not in near_outputs}
    names = ["hbm " + name for name in inputs] + ["vmem " + name for name in near]
    names += ["hbm " + name + "_before" for name in changed]
    names += ["hbm " + name for name in outputs] + ["vmem " + name for name in near_outputs]
    names += ["hbm " + name for name in changed] + ["vmem " + name for name in scratch] + ["semaphores"]
    close = pl.BlockSpec(memory_space=pltpu.VMEM)
    specs = [pl.BlockSpec(memory_space=pltpu.SMEM if name == "lengths" else pl.ANY) for name in inputs]
    held = [pltpu.with_memory_space_constraint(item, pltpu.VMEM) for item in near.values()]
    first_changed, first_out = len(inputs) + len(near), len(outputs) + len(near_outputs)
    outs = pl.pallas_call(
        functools.partial(step_kernel, stage, slot, base, span, names),
        in_specs=specs + [close] * len(near) + any_space(len(changed)),
        out_specs=any_space(len(outputs)) + [close] * len(near_outputs) + any_space(len(changed)),
        out_shape=[jax.ShapeDtypeStruct(*shape) for shape in outputs.values()]
        + [pltpu.VMEM(*shape) for shape in near_outputs.values()]
        + [jax.ShapeDtypeStruct(item.shape, item.dtype) for item in changed.values()],
        input_output_aliases={first_changed + i: first_out + i for i in range(len(changed))},
        scratch_shapes=[pltpu.VMEM(*shape) for shape in scratch.values()] + [pltpu.SemaphoreType.DMA((96,))],
        compiler_params=pltpu.CompilerParams(vmem_limit_bytes=LIMITS.get(stage, LIMIT) * 2**20),
        cost_estimate=pl.CostEstimate(flops=FLOPS, bytes_accessed=2**16, transcendentals=0),
        name=f"{stage}_{slot}".replace(" ", "_"),
    )(*inputs.values(), *held, *changed.values())
    return dict(zip([*outputs, *near_outputs, *changed], outs))


def shift(value, axis, steps):
    count = lax.axis_size(axis)
    pairs = [(place, place + steps) for place in range(max(0, -steps), min(count, count - steps))]
    return lax.ppermute(value, axis, pairs)


def add_over(value, axis):
    count = lax.axis_size(axis)
    if count & (count - 1):
        return lax.psum(value, axis)

    def far(value, mask):
        return lax.ppermute(value, axis, [(place, place ^ mask) for place in range(count)])

    step = 1
    while step < count:
        if 2 * step < count:
            value = (value + far(value, step)) + (far(value, 2 * step) + far(value, 3 * step))
            step *= 4
        else:
            value = value + far(value, step)
            step *= 2
    return value


def body(tokens, doc_lengths, cotangent, *params):
    params = dict(zip(PARAMS, (item[0] if item.ndim == 3 else item for item in params)))
    micro, _, rows, width = tokens.shape
    hidden = params["ff1"].shape[1]
    scratch = scratch_of(rows, width, hidden)
    step = functools.partial(run, rows=rows, width=width, hidden=hidden)
    sheet = ((rows, width), bf16)
    sheets = ((micro, rows, width), bf16)
    kept_shapes = {"kept_" + name: ((micro,) + scratch[name][0], scratch[name][1]) for name in KEPT}
    lengths = dict(lengths=doc_lengths)
    resident = resident_of(width, hidden)
    half = rows // 2
    part, sums = ((half, width), bf16), ((1, 6 * width + hidden), f32)
    kept_names = [*kept_shapes, "layer"]

    def tails(*names):
        shapes = {"low": (width, bf16), "acc": (width, f32), "heads": (3 * width, bf16)}
        return {name: ((rows - half, shapes[name.split("_")[1]][0]), shapes[name.split("_")[1]][1]) for name in names}

    done = step(
        "open", 0, dict(lengths, tokens=tokens, **params), {}, dict(kept_shapes, layer=sheets, **tails("more_low", "more_acc")),
        dict(resident, sent=part), {}, span=half,
    )
    near = {name: done[name] for name in PARAMS}
    back = {name: near[name] for name in PARAMS[:6]}
    x_low = shift(done["sent"], "section", 1)
    done = step(
        "more", 0, {name: done[name] for name in ("more_low", "more_acc")}, near, {}, dict(sent=part),
        {name: done[name] for name in kept_names}, base=half, span=rows - half,
    )
    x_high = shift(done["sent"], "section", 1)
    x_low, layer = lax.optimization_barrier((x_low, done["layer"]))
    done = step(
        "ahead", 1, dict(lengths, tokens=tokens), near, {}, dict(sent=sheet),
        dict({name: done[name] for name in kept_names}, layer=layer),
    )
    x = shift(done["sent"], "section", 1)
    kept = {name: done[name] for name in kept_names}

    kept = step("enter", 0, lengths, dict(near, x_low=x_low, x_high=x_high), {}, {}, kept)
    stored = {name: kept[name] for name in kept_shapes}
    state = step("leave", 0, dict(stored, cotangent=cotangent), back, dict(grad=sheets, totals=sums), dict(sent=sheet), {})
    up = shift(state.pop("sent"), "section", -1)
    state = step(
        "turn", 1, dict(lengths, cotangent=cotangent), dict(near, x=x), tails("tail_heads", "tail_acc"), dict(sent=part),
        dict(state, layer=kept["layer"]),
    )
    layer_out = state["layer"]
    up_low = shift(state["sent"], "section", -1)
    totals = state["totals"]
    state = step(
        "rest", 1, {name: state[name] for name in ("tail_heads", "tail_acc")}, back, {}, dict(sent=part),
        dict(grad=state["grad"]), base=half, span=rows - half,
    )
    up_high = shift(state["sent"], "section", -1)
    state = step("back", 0, stored, dict(back, up=up), {}, {}, dict(grad=state["grad"], totals=totals))
    grad = state["grad"]
    state = step(
        "back part", 1, stored, dict(back, up=up_low), dict(acc_part=((half, width), f32)), {}, dict(totals=state["totals"]),
        span=half,
    )
    state = step(
        "back whole", 1, dict(stored, acc_part=state["acc_part"]), dict(back, up=up_high), {}, {},
        dict(grad=grad, totals=state["totals"]), base=half, span=rows - half,
    )
    totals = add_over(state["totals"], "dp")
    places = [0, 2 * width, 3 * width, 4 * width, 4 * width + hidden, 5 * width + hidden, 6 * width + hidden]
    return (layer_out[None, :, None], state["grad"][None, :, None]) + tuple(
        totals[:, low:high] for low, high in zip(places[:-1], places[1:])
    )


def solution(mesh):
    in_specs = (
        P(None, "dp", None, None), P(None, "dp", None), P(None, "dp", None, None),
        P("section", None, None), P("section", None, None), P("section", None, None), P("section", None, None),
    ) + (P("section", None),) * 8
    out_specs = (P("section", None, "dp", None, None),) * 2 + (P("section", None),) * 6
    return jax.shard_map(body, mesh=mesh, in_specs=in_specs, out_specs=out_specs, check_vma=False)
```

```python
import functools
import math
import types
import jax
import jax.numpy as jnp
from jax import lax
from jax.experimental import pallas as pl
from jax.experimental.pallas import tpu as pltpu
from jax.sharding import PartitionSpec as P

HEAD_DIM = 64
LANES = 128
GROUP = 256
TILE = 2048
BLOCK = 256
ROWS = 128
PAIRS = 4
LIMITS = {}
TURN = 1
LIMIT = 35
epsilon = 1e-05
masked_score = -1000000000.0
root_half = 0.7071067811865476
inverse_root_tau = 0.3989422804014327
f32 = jnp.float32
bf16 = jnp.bfloat16


def dot(left, right):
    return jnp.dot(left, right, preferred_element_type=f32)


def dot_back(left, right):
    return lax.dot_general(left, right, (((1,), (1,)), ((), ())), preferred_element_type=f32)


def beside(*parts):
    return jnp.concatenate(parts, axis=1)


def above(*parts):
    return jnp.concatenate(parts, axis=0)


def column_sum(value):
    return jnp.sum(value, axis=0, keepdims=True)


def row_norm(summed):
    middle = jnp.mean(summed, axis=-1, keepdims=True)
    centered = summed - middle
    inverse = lax.rsqrt(jnp.mean(centered * centered, axis=-1, keepdims=True) + epsilon)
    return centered * inverse, inverse


def row_norm_back(upstream, normed, inverse, gain):
    scaled = upstream * gain
    centered = scaled - jnp.mean(scaled, axis=-1, keepdims=True)
    return inverse * (centered - normed * jnp.mean(scaled * normed, axis=-1, keepdims=True))


def split_three(value):
    high = value.astype(bf16).astype(f32)
    rest = value - high
    middle = rest.astype(bf16).astype(f32)
    return high, middle, rest - middle


def spread(value):
    lane = lax.broadcasted_iota(jnp.int32, value.shape, 1)
    high, middle, low = split_three(value)
    return jnp.where(lane < 16, high, jnp.where(lane < 32, middle, low)).astype(bf16)


def strip(index, size):
    return pl.ds(pl.multiple_of(index * size, size), size)


class Copies:
    def __init__(self, semaphores):
        self.semaphores = semaphores
        self.used = 0

    def take(self, count=1):
        self.used += count
        return self.used - count

    def make(self, source, target, place=None):
        place = self.take() if place is None else place
        return pltpu.make_async_copy(source, target, self.semaphores.at[place])

    def start(self, source, target):
        return self.start_at(source, target, self.take())

    def start_at(self, source, target, place):
        copy = self.make(source, target, place)
        copy.start()
        return copy


def any_space(count):
    return [pl.BlockSpec(memory_space=pl.ANY)] * count


PARAMS = (
    "qkv", "out", "ff1", "ff2", "first_gain", "second_gain", "qv_bias", "out_bias", "first_shift", "ff1_bias", "ff2_bias",
    "second_shift",
)
KEPT = ("heads", "context", "shares", "weights", "one", "one_inverse", "slope", "two", "two_inverse")


def resident_of(width, hidden):
    groups, tiles = width // GROUP, hidden // TILE
    shapes = {
        "qkv": ((groups, width, 3 * width // groups), bf16),
        "out": ((width, width), bf16),
        "ff1": ((tiles, width, TILE), bf16),
        "ff2": ((tiles, TILE, width), bf16),
    }
    lengths = {"qv_bias": 3 * width, "ff1_bias": hidden}
    return shapes | {name: ((1, lengths.get(name, width)), f32) for name in PARAMS[4:]}


def scratch_of(rows, width, hidden):
    tiles = hidden // TILE
    return {
        "acc": ((rows, width), f32),
        "low": ((rows, width), bf16),
        "heads": ((rows, 3 * width), bf16),
        "context": ((rows, width), bf16),
        "shares": ((rows, LANES), f32),
        "weights": ((width // HEAD_DIM, rows, rows), bf16),
        "one": ((rows, width), f32),
        "one_inverse": ((rows, LANES), f32),
        "slope": ((tiles, rows, TILE), bf16),
        "two": ((rows, width), bf16),
        "two_inverse": ((rows, LANES), f32),
        "grad_marks": ((rows, LANES), bf16),
        "totals": ((1, 6 * width + hidden), f32),
    }


class Layer:
    def __init__(self, hbm, vmem, semaphores, slot, base, span, keeping):
        self.hbm, self.vmem = hbm, vmem
        self.slot, self.base, self.span = slot, base, span
        self.keeping = keeping
        self.value = vmem.value if hasattr(vmem, "value") else getattr(vmem, "sent", None)
        self.copies = Copies(semaphores)
        self.groups, self.width, self.part = vmem.qkv.shape
        self.tiles = vmem.ff1.shape[0] if hasattr(vmem, "ff1") else 0
        self.qkv_place = self.copies.take(self.groups)
        self.out_place = self.copies.take()
        self.ff_place = self.copies.take(2 * self.tiles)
        self.small_place = self.copies.take(9)
        self.loading = hasattr(hbm, "qkv")
        self.kept_place = self.copies.take(len(KEPT))
        self.slope_place = self.copies.take(self.tiles)
        self.row_place = self.copies.take(2 * (span // ROWS))

    def qkv_copy(self, g):
        part = self.vmem.qkv.shape[2]
        return self.copies.make(self.hbm.qkv.at[:, strip(g, part)], self.vmem.qkv.at[g], self.qkv_place + g)

    def out_copy(self):
        return self.copies.make(self.hbm.out, self.vmem.out, self.out_place)

    def ff1_copy(self, t):
        return self.copies.make(self.hbm.ff1.at[:, strip(t, TILE)], self.vmem.ff1.at[t], self.ff_place + 2 * t)

    def ff2_copy(self, t):
        return self.copies.make(self.hbm.ff2.at[strip(t, TILE)], self.vmem.ff2.at[t], self.ff_place + 2 * t + 1)

    def small_copies(self):
        copies = []
        for name in PARAMS[4:]:
            source, target = getattr(self.hbm, name), getattr(self.vmem, name)
            if name == "qv_bias":
                copies.append((source.at[:, : self.width], target.at[:, : self.width]))
                copies.append((source.at[:, self.width :], target.at[:, 2 * self.width :]))
            else:
                copies.append((source, target))
        return [self.copies.make(*pair, self.small_place + index) for index, pair in enumerate(copies)]

    def start_weights(self):
        for g in range(self.groups):
            self.qkv_copy(g).start()
            if g == 0:
                for copy in self.small_copies():
                    copy.start()
        self.out_copy().start()
        for t in range(self.tiles):
            self.ff1_copy(t).start()
            self.ff2_copy(t).start()
        self.vmem.qv_bias[:, self.width : 2 * self.width] = jnp.zeros((1, self.width), f32)

    def wait_qkv(self, g):
        if self.loading:
            self.qkv_copy(g).wait()

    def wait_out(self):
        if self.loading:
            self.out_copy().wait()

    def wait_feed(self, t):
        if self.loading:
            self.ff1_copy(t).wait()
            self.ff2_copy(t).wait()

    def wait_small(self):
        if self.loading:
            for copy in self.small_copies():
                copy.wait()

    def wait_weights(self):
        self.wait_small()
        self.wait_out()
        for g in range(self.groups):
            self.wait_qkv(g)
        for t in range(self.tiles):
            self.wait_feed(t)

    def kept_copy(self, name, back):
        there, here = getattr(self.hbm, "kept_" + name).at[self.slot], getattr(self.vmem, name)
        if here.shape[0] == self.span:
            there = there.at[pl.ds(self.base, self.span)]
        place = self.kept_place + KEPT.index(name)
        return self.copies.make(there, here, place) if back else self.copies.make(here, there, place)

    def slope_copy(self, t, back):
        there, here = self.hbm.kept_slope.at[self.slot, t, pl.ds(self.base, self.span)], self.vmem.slope.at[t]
        return self.copies.make(there, here, self.slope_place + t) if back else self.copies.make(here, there, self.slope_place + t)

    def row_copy(self, name, target, index, size, part):
        here = (self.value if name == "sent" else getattr(self.vmem, name)).at[strip(index, size)]
        there = getattr(self.hbm, target).at[self.slot, pl.ds(self.base + pl.multiple_of(index * size, size), size)]
        return self.copies.make(here, there, self.row_place + 2 * index + part)

    def layer_copy(self, index):
        return self.row_copy("sent", "layer", index, ROWS, 0)

    def two_copy(self, index):
        return self.row_copy("two", "kept_two", index, ROWS, 1)

    def grad_copy(self, index):
        return self.row_copy("sent", "grad", index, BLOCK, 0)

    def keep(self, *names):
        if self.keeping:
            for name in names:
                self.kept_copy(name, False).start()

    def await_kept(self, back, *names):
        if self.keeping:
            for name in names:
                self.kept_copy(name, back).wait()

    def some_rows(self, ref):
        return ref if ref.shape[0] == self.span else ref.at[pl.ds(self.base, self.span)]

    def attend_forward(self):
        hbm, vmem, slot = self.hbm, self.vmem, self.slot
        width, groups, part = self.width, self.groups, self.part
        rows = vmem.heads.shape[0]
        segments = hbm.lengths.shape[2]

        def own_marks(start, count):
            place = start + lax.broadcasted_iota(jnp.int32, (count, LANES), 0)
            label = jnp.zeros((count, LANES), jnp.int32)
            end = jnp.int32(0)
            for index in range(segments):
                end = end + hbm.lengths[slot, 0, index]
                label = label + jnp.where(place >= end, 1, 0)
            lane = lax.broadcasted_iota(jnp.int32, (count, LANES), 1)
            return jnp.where(lane == label, 1.0, 0.0), lane

        own, lane = own_marks(0, rows)
        key_mark = jnp.where(lane < segments, (1.0 - own) * masked_score, 0.0).astype(bf16)
        query_mark = own.astype(bf16)
        clear(vmem.shares)
        half = lane < HEAD_DIM
        zero = jnp.zeros((rows, LANES), bf16)
        ones = jnp.ones((rows, LANES), bf16)
        head_lane = jnp.where(lane < 48, lane & 15, -1)
        self.wait_small()
        if self.x_copy is not None:
            self.x_copy.wait()

        def project(g, carry):
            self.wait_qkv(g)
            columns = strip(g, part)
            vmem.heads[:, columns] = (dot(vmem.x[...], vmem.qkv[g]) + vmem.qv_bias[:, columns]).astype(bf16)
            return carry

        lax.fori_loop(0, groups, project, 0)
        self.keep("heads")

        def head_step(step, carry):
            count = 2 * PAIRS
            queries, keys, values = (
                vmem.heads[:, pl.ds(pl.multiple_of(at * width + step * PAIRS * LANES, LANES), PAIRS * LANES)] for at in range(3)
            )
            mixes = []

            def score(local):
                pair, side = divmod(local, 2)
                chosen = slice(pair * LANES, (pair + 1) * LANES)
                scaled = queries[:, chosen] * jnp.asarray(HEAD_DIM**-0.5, bf16)
                left = jnp.where(half if side == 0 else ~half, scaled, zero)
                return dot_back(beside(left, query_mark), beside(keys[:, chosen], key_mark))

            scores = score(0)
            for local in range(count):
                following = score(local + 1) if local + 1 < count else None
                chosen = slice(local // 2 * LANES, (local // 2 + 1) * LANES)
                top = jnp.max(scores, axis=-1, keepdims=True)
                weights = jnp.exp(scores - top).astype(bf16)
                vmem.weights[step * count + local] = weights
                mixes.append(dot(weights, beside(values[:, chosen], ones)))
                scores = following
            keep = vmem.shares[...]
            parts = []
            for local in range(count):
                share = 1.0 / mixes[local][:, LANES:]
                parts.append(mixes[local][:, :LANES] * share)
                keep = jnp.where(head_lane == step * count + local, share, keep)
            vmem.shares[...] = keep
            mixed = beside(*[jnp.where(half, parts[2 * p], parts[2 * p + 1]) for p in range(PAIRS)])
            vmem.context[:, strip(step, PAIRS * LANES)] = mixed.astype(bf16)
            return carry

        lax.fori_loop(0, width // (PAIRS * LANES), head_step, 0)
        self.keep("context", "shares", "weights")
        self.wait_out()

        def first_norm(index, carry):
            rows_ = strip(index, BLOCK)
            summed = vmem.x[rows_, :].astype(f32) + vmem.out_bias[...] + dot(vmem.context[rows_, :], vmem.out[...])
            one, one_inverse = row_norm(summed)
            vmem.one[rows_, :] = one
            vmem.one_inverse[rows_, :] = jnp.broadcast_to(one_inverse, (one.shape[0], LANES))
            value = one * vmem.first_gain[...] + vmem.first_shift[...]
            vmem.low[rows_, :] = value.astype(bf16)
            vmem.acc[rows_, :] = value + vmem.ff2_bias[...]
            return carry

        lax.fori_loop(0, rows // BLOCK, first_norm, 0)
        self.keep("one", "one_inverse")

    def feed_forward(self):
        vmem, span, tiles = self.vmem, self.span, self.tiles
        low, acc = self.some_rows(vmem.low), self.some_rows(vmem.acc)

        def tile_step(t, carry):
            self.wait_feed(t)
            bias = vmem.ff1_bias[:, strip(t, TILE)]
            acts = []
            for c in range(TILE // BLOCK):
                columns = slice(c * BLOCK, (c + 1) * BLOCK)
                h = dot(low[...], vmem.ff1[t, :, columns]) + bias[:, columns]
                share = 0.5 + 0.5 * lax.erf(h * root_half)
                vmem.slope[t, :, columns] = (share + h * jnp.exp(h * h * -0.5) * inverse_root_tau).astype(bf16)
                acts.append((h * share).astype(bf16))
            acc[...] += dot(beside(*acts), vmem.ff2[t])
            if self.keeping:
                self.slope_copy(t, False).start()
            return carry

        lax.fori_loop(0, tiles, tile_step, 0)

        def second_norm(index, carry):
            rows_ = strip(index, ROWS)
            two, two_inverse = row_norm(acc[rows_, :])
            self.value[rows_, :] = (two * vmem.second_gain[...] + vmem.second_shift[...]).astype(bf16)
            vmem.two[rows_, :] = two.astype(bf16)
            vmem.two_inverse[rows_, :] = jnp.broadcast_to(two_inverse, (ROWS, LANES))
            self.layer_copy(index).start()
            if self.keeping:
                self.two_copy(index).start()
            return carry

        lax.fori_loop(0, span // ROWS, second_norm, 0)
        self.keep("two_inverse")

    def finish_forward(self, *names):
        self.await_kept(False, *names)
        for index in range(self.span // ROWS):
            self.layer_copy(index).wait()
            if self.keeping:
                self.two_copy(index).wait()
        if self.keeping:
            for t in range(self.tiles):
                self.slope_copy(t, False).wait()

    def fetch_feed(self):
        for name in ("two", "two_inverse"):
            self.kept_copy(name, True).start()
        for t in range(self.tiles):
            self.slope_copy(t, True).start()

    def fetch_attend(self):
        for name in ("one", "one_inverse", "context", "shares", "heads", "weights"):
            self.kept_copy(name, True).start()

    def feed_backward(self):
        vmem, base, span = self.vmem, self.base, self.span
        width, tiles = self.width, self.tiles
        at_ff1 = 4 * width
        at_ff2 = at_ff1 + tiles * TILE
        at_second = at_ff2 + width
        totals, low = vmem.totals, vmem.low
        acc = self.some_rows(vmem.acc)
        self.await_kept(True, "two", "two_inverse")

        def second_back(index, carry):
            rows_ = strip(index, ROWS)
            upstream = vmem.up[rows_, :].astype(f32)
            grad = row_norm_back(upstream, vmem.two[rows_, :].astype(f32), vmem.two_inverse[rows_, :1], vmem.second_gain[...])
            low[rows_, :] = grad.astype(bf16)
            acc[rows_, :] = grad
            totals[:, at_second : at_second + width] += column_sum(upstream)
            totals[:, at_ff2 : at_ff2 + width] += column_sum(grad.astype(bf16).astype(f32))
            return carry

        lax.fori_loop(0, span // ROWS, second_back, 0)

        def tile_step(t, carry):
            if self.keeping:
                self.slope_copy(t, True).wait()
            grads, sums = [], []
            for c in range(TILE // BLOCK):
                columns = slice(c * BLOCK, (c + 1) * BLOCK)
                h = (dot_back(low[...], vmem.ff2[t, columns, :]) * vmem.slope[t, :, columns].astype(f32)).astype(bf16)
                sums.append(column_sum(h.astype(f32)))
                grads.append(h)
            totals[:, pl.ds(pl.multiple_of(at_ff1 + t * TILE, TILE), TILE)] += beside(*sums)
            acc[...] += dot_back(beside(*grads), vmem.ff1[t])
            return carry

        lax.fori_loop(0, tiles, tile_step, 0)

    def attend_backward(self):
        vmem, width, groups = self.vmem, self.width, self.groups
        rows = vmem.heads.shape[0]
        totals, acc = vmem.totals, vmem.acc
        at_out, at_first = 2 * width, 3 * width
        self.await_kept(True, "one", "one_inverse", "context", "shares")

        def first_back(index, carry):
            rows_ = strip(index, BLOCK)
            first_grad = acc[rows_, :]
            totals[:, at_first : at_first + width] += column_sum(first_grad)
            summed = row_norm_back(first_grad, vmem.one[rows_, :], vmem.one_inverse[rows_, :1], vmem.first_gain[...])
            acc[rows_, :] = summed
            attend_grad = summed.astype(bf16)
            totals[:, at_out : at_out + width] += column_sum(attend_grad.astype(f32))
            shares = spread(vmem.shares[rows_, :])
            context_grad = (dot_back(attend_grad, vmem.out[...]) * dot_back(shares, pick)).astype(bf16)
            product = context_grad.astype(f32) * vmem.context[rows_, :].astype(f32)
            upper = product.astype(bf16)
            inner = dot(upper, pick) + dot((product - upper.astype(f32)).astype(bf16), pick)
            vmem.grad_marks[rows_, :] = spread(inner)
            vmem.context[rows_, :] = context_grad
            return carry

        which = lax.broadcasted_iota(jnp.int32, (width, LANES), 0) // HEAD_DIM
        spot = lax.broadcasted_iota(jnp.int32, (width, LANES), 1)
        pick = jnp.where(((spot & 15) == which) & (spot < 48), 1.0, 0.0).astype(bf16)
        lax.fori_loop(0, rows // BLOCK, first_back, 0)
        lane = lax.broadcasted_iota(jnp.int32, (rows, LANES), 1)
        half = lane < HEAD_DIM
        zero = jnp.zeros((rows, LANES), bf16)
        local_lane = jnp.where(lane < 48, lane & 15, -1)
        self.await_kept(True, "heads", "weights")
        scale = HEAD_DIM**-0.5
        grad_mark = vmem.grad_marks[...]

        def head_step(step, carry):
            size = PAIRS * LANES
            spans = [pl.ds(pl.multiple_of(at * width + step * size, LANES), size) for at in range(3)]
            queries, all_keys, all_values = (vmem.heads[:, span] for span in spans)
            grads = vmem.context[:, strip(step, size)]
            query_grads, key_grads, value_grads = [], [], []
            for pair in range(PAIRS):
                chosen = slice(pair * LANES, (pair + 1) * LANES)
                query = queries[:, chosen] * jnp.asarray(scale, bf16)
                keys = all_keys[:, chosen]
                values = all_values[:, chosen]
                upper_grad = grads[:, chosen]
                query_turned = query.T
                grad_turned = upper_grad.T
                score_grads, keys_kept, key_turned, value_turned = [], [], [], []
                for side in range(2):
                    ours = half if side == 0 else ~half
                    mine = slice(side * HEAD_DIM, (side + 1) * HEAD_DIM)
                    head = step * 2 * PAIRS + pair * 2 + side
                    weights = vmem.weights[head]
                    right = beside(values, jnp.where(local_lane == head, -1.0, 0.0).astype(bf16))
                    score_grad = (weights.astype(f32) * dot_back(beside(jnp.where(ours, upper_grad, zero), grad_mark), right)).astype(bf16)
                    value_turned.append(dot(grad_turned[mine], weights).astype(bf16))
                    key_turned.append(dot(query_turned[mine], score_grad).astype(bf16))
                    score_grads.append(score_grad)
                    keys_kept.append(jnp.where(ours, keys, zero))
                key_grads.append(above(*key_turned).T)
                value_grads.append(above(*value_turned).T)
                query_grads.append((dot(beside(*score_grads), above(*keys_kept)) * scale).astype(bf16))
            query_grad, key_grad, value_grad = beside(*query_grads), beside(*key_grads), beside(*value_grads)
            for span, grad in zip(spans, (query_grad, key_grad, value_grad)):
                vmem.heads[:, span] = grad
            totals[:, strip(step, size)] += column_sum(query_grad.astype(f32))
            totals[:, pl.ds(pl.multiple_of(width + step * size, LANES), size)] += column_sum(value_grad.astype(f32))
            return carry

        lax.fori_loop(0, width // (PAIRS * LANES), head_step, 0)
    def input_grad(self):
        vmem, base, span, part = self.vmem, self.base, self.span, self.part
        self.value = vmem.sent
        shift_by = base if vmem.acc.shape[0] != span else 0

        def input_step(index, carry):
            found = vmem.acc[pl.ds(shift_by + pl.multiple_of(index * BLOCK, BLOCK), BLOCK), :]
            rows_ = pl.ds(shift_by + pl.multiple_of(index * BLOCK, BLOCK), BLOCK)
            for g in range(self.groups):
                found = found + dot_back(vmem.heads[rows_, g * part : (g + 1) * part], vmem.qkv[g])
            vmem.sent[strip(index, BLOCK), :] = found.astype(bf16)
            self.grad_copy(index).start()
            return carry

        lax.fori_loop(0, span // BLOCK, input_step, 0)
        for index in range(span // BLOCK):
            self.grad_copy(index).wait()


def clear(ref):
    ref[...] = jnp.zeros_like(ref)


EVERY = False


def step_kernel(stage, slot, base, span, names, *refs):
    refs = dict(zip(names, refs))
    hbm = types.SimpleNamespace(**{name[4:]: ref for name, ref in refs.items() if name.startswith("hbm ")})
    vmem = types.SimpleNamespace(**{name[5:]: ref for name, ref in refs.items() if name.startswith("vmem ")})
    in_first = lax.axis_index("section") == 0
    working = jnp.logical_not(in_first) if stage in SECOND else in_first
    layer = Layer(hbm, vmem, refs["semaphores"], slot, base, span, stage != "turn")
    copies = layer.copies

    @pl.when(working)
    def _():
        if stage in ("open", "ahead", "enter", "turn"):
            layer.x_copy = None
            if stage in ("open", "ahead"):
                layer.x_copy = copies.start(hbm.tokens.at[slot, 0], vmem.x)
            elif hasattr(vmem, "x_low"):
                count = vmem.x_low.shape[0]
                vmem.x[:count, :] = vmem.x_low[...]
                vmem.x[count:, :] = vmem.x_high[...]
            if layer.loading:
                layer.start_weights()
            if stage == "turn":
                before = None if slot == 0 else copies.start(hbm.totals, vmem.totals)
                up_copy = copies.start(hbm.cotangent.at[slot, 0], vmem.up)
            layer.attend_forward()
            later = []
            if stage == "open":
                rest = pl.ds(span, vmem.acc.shape[0] - span)
                later.append(copies.start(vmem.low.at[rest], hbm.more_low))
                later.append(copies.start(vmem.acc.at[rest], hbm.more_acc))
            layer.feed_forward()
            if stage != "turn":
                layer.finish_forward("heads", "context", "shares", "weights", "one", "one_inverse", "two_inverse")
            for copy in later:
                copy.wait()
        elif stage == "more":
            fetched = [copies.start(hbm.more_low, vmem.low), copies.start(hbm.more_acc, vmem.acc)]
            for copy in fetched:
                copy.wait()
            layer.feed_forward()
            layer.finish_forward("two_inverse")
        elif stage == "rest":
            fetched = [copies.start(hbm.tail_heads, vmem.heads), copies.start(hbm.tail_acc, vmem.acc)]
            for copy in fetched:
                copy.wait()
            layer.input_grad()
        if stage in ("leave", "turn", "back", "back part", "back whole"):
            if stage != "turn":
                before = None if slot == 0 else copies.start(hbm.totals, vmem.totals)
                up_copy = copies.start(hbm.cotangent.at[slot, 0], vmem.up) if stage == "leave" else None
                layer.fetch_feed()
                if stage == "back whole":
                    acc_copy = copies.start(hbm.acc_part, vmem.acc.at[pl.ds(0, base)])
                if stage != "back part":
                    layer.fetch_attend()
            if before is None:
                clear(vmem.totals)
            else:
                before.wait()
            if up_copy is not None:
                up_copy.wait()
            layer.feed_backward()
            if stage == "back whole":
                acc_copy.wait()
            if stage != "back part":
                layer.attend_backward()
            if stage == "turn":
                layer.finish_forward()
            after = [copies.start(vmem.totals, hbm.totals)]
            if stage == "back part":
                after.append(copies.start(vmem.acc, hbm.acc_part))
            else:
                if stage == "turn" and vmem.sent.shape[0] < vmem.acc.shape[0]:
                    layer.base, layer.span = 0, vmem.sent.shape[0]
                    tail = pl.ds(layer.span, vmem.acc.shape[0] - layer.span)
                    after.append(copies.start(vmem.heads.at[tail], hbm.tail_heads))
                    after.append(copies.start(vmem.acc.at[tail], hbm.tail_acc))
                elif stage == "back whole":
                    layer.base, layer.span = 0, vmem.acc.shape[0]
                layer.input_grad()
            for copy in after:
                copy.wait()

    if layer.loading:
        @pl.when(jnp.logical_not(working))
        def _():
            layer.start_weights()
            layer.wait_weights()


FLOPS = 10**6
SECOND = ("enter", "leave", "turn", "rest")


def run(stage, slot, inputs, near, outputs, near_outputs, changed, rows, width, hidden, base=0, span=None):
    span = rows if span is None else span
    full, some = scratch_of(rows, width, hidden), scratch_of(span, width, hidden)
    feeding = ("slope", "two", "two_inverse")
    mixed = {name: some[name] if name in feeding else full[name] for name in full}
    if stage in ("open", "ahead", "enter"):
        scratch = {name: mixed[name] for name in mixed if name not in ("grad_marks", "totals")}
    elif stage == "more":
        scratch = {name: some[name] for name in ("acc", "low", *feeding)}
    elif stage == "rest":
        scratch = {name: some[name] for name in ("heads", "acc")}
    elif stage == "back part":
        scratch = {name: some[name] for name in ("acc", "low", "totals", *feeding)}
    else:
        scratch = dict(mixed, low=some["low"])
    if stage in ("open", "ahead", "enter", "turn"):
        scratch["x"] = ((rows, width), bf16)
    if stage in ("leave", "turn"):
        scratch["up"] = ((rows, width), bf16)
    if stage == "turn":
        scratch["value"] = ((rows, width), bf16)
    if stage != "back part":
        scratch["sent"] = ((rows, width), bf16)
    scratch = {name: shape for name, shape in scratch.items() if name not in near and name not in near_outputs}
    names = ["hbm " + name for name in inputs] + ["vmem " + name for name in near]
    names += ["hbm " + name + "_before" for name in changed]
    names += ["hbm " + name for name in outputs] + ["vmem " + name for name in near_outputs]
    names += ["hbm " + name for name in changed] + ["vmem " + name for name in scratch] + ["semaphores"]
    close = pl.BlockSpec(memory_space=pltpu.VMEM)
    specs = [pl.BlockSpec(memory_space=pltpu.SMEM if name == "lengths" else pl.ANY) for name in inputs]
    held = [pltpu.with_memory_space_constraint(item, pltpu.VMEM) for item in near.values()]
    first_changed, first_out = len(inputs) + len(near), len(outputs) + len(near_outputs)
    outs = pl.pallas_call(
        functools.partial(step_kernel, stage, slot, base, span, names),
        in_specs=specs + [close] * len(near) + any_space(len(changed)),
        out_specs=any_space(len(outputs)) + [close] * len(near_outputs) + any_space(len(changed)),
        out_shape=[jax.ShapeDtypeStruct(*shape) for shape in outputs.values()]
        + [pltpu.VMEM(*shape) for shape in near_outputs.values()]
        + [jax.ShapeDtypeStruct(item.shape, item.dtype) for item in changed.values()],
        input_output_aliases={first_changed + i: first_out + i for i in range(len(changed))},
        scratch_shapes=[pltpu.VMEM(*shape) for shape in scratch.values()] + [pltpu.SemaphoreType.DMA((96,))],
        compiler_params=pltpu.CompilerParams(vmem_limit_bytes=LIMITS.get(stage, LIMIT) * 2**20),
        cost_estimate=pl.CostEstimate(flops=FLOPS, bytes_accessed=2**16, transcendentals=0),
        name=f"{stage}_{slot}".replace(" ", "_"),
    )(*inputs.values(), *held, *changed.values())
    return dict(zip([*outputs, *near_outputs, *changed], outs))


def shift(value, axis, steps):
    count = lax.axis_size(axis)
    pairs = [(place, place + steps) for place in range(max(0, -steps), min(count, count - steps))]
    return lax.ppermute(value, axis, pairs)


def add_over(value, axis):
    count = lax.axis_size(axis)
    if count & (count - 1):
        return [lax.psum(value, axis)]

    def far(value, mask):
        return lax.ppermute(value, axis, [(place, place ^ mask) for place in range(count)])

    step = 1
    while 4 * step < count:
        value = (value + far(value, step)) + (far(value, 2 * step) + far(value, 3 * step))
        step *= 4
    if 2 * step < count:
        return [value, far(value, step), far(value, 2 * step), far(value, 3 * step)]
    return [value, far(value, step)] if step < count else [value]


def sum_parts(values, sizes):
    def kernel(*refs):
        parts = [ref[...] for ref in refs[: len(values)]]
        while len(parts) > 1:
            parts = [one + two for one, two in zip(parts[::2], parts[1::2])]
        at = 0
        for ref in refs[len(values) :]:
            ref[...] = parts[0][:, at : at + ref.shape[1]]
            at += ref.shape[1]

    return pl.pallas_call(kernel, out_shape=[jax.ShapeDtypeStruct((1, size), f32) for size in sizes], name="sums")(*values)


def body(tokens, doc_lengths, cotangent, *params):
    params = dict(zip(PARAMS, (item[0] if item.ndim == 3 else item for item in params)))
    micro, _, rows, width = tokens.shape
    hidden = params["ff1"].shape[1]
    scratch = scratch_of(rows, width, hidden)
    step = functools.partial(run, rows=rows, width=width, hidden=hidden)
    sheet = ((rows, width), bf16)
    sheets = ((micro, rows, width), bf16)
    kept_shapes = {"kept_" + name: ((micro,) + scratch[name][0], scratch[name][1]) for name in KEPT}
    lengths = dict(lengths=doc_lengths)
    resident = resident_of(width, hidden)
    half = rows // 2
    part, sums = ((half, width), bf16), ((1, 6 * width + hidden), f32)
    kept_names = [*kept_shapes, "layer"]

    def tails(*names):
        shapes = {"low": (width, bf16), "acc": (width, f32), "heads": (3 * width, bf16)}
        return {name: ((rows - half, shapes[name.split("_")[1]][0]), shapes[name.split("_")[1]][1]) for name in names}

    done = step(
        "open", 0, dict(lengths, tokens=tokens, **params), {}, dict(kept_shapes, layer=sheets, **tails("more_low", "more_acc")),
        dict(resident, sent=part), {}, span=half,
    )
    near = {name: done[name] for name in PARAMS}
    back = {name: near[name] for name in PARAMS[:6]}
    x_low = shift(done["sent"], "section", 1)
    done = step(
        "more", 0, {name: done[name] for name in ("more_low", "more_acc")}, near, {}, dict(sent=part),
        {name: done[name] for name in kept_names}, base=half, span=rows - half,
    )
    x_high = shift(done["sent"], "section", 1)
    x_low, layer = lax.optimization_barrier((x_low, done["layer"]))
    done = step(
        "ahead", 1, dict(lengths, tokens=tokens), near, {}, dict(sent=sheet),
        dict({name: done[name] for name in kept_names}, layer=layer),
    )
    x = shift(done["sent"], "section", 1)
    kept = {name: done[name] for name in kept_names}

    stored = {name: kept[name] for name in kept_shapes}
    if TURN:
        state = step(
            "turn", 0, dict(lengths, cotangent=cotangent), dict(near, x_low=x_low, x_high=x_high), dict(grad=sheets, totals=sums),
            dict(sent=sheet), dict(layer=kept["layer"]),
        )
        layer_out = state.pop("layer")
    else:
        kept = step("enter", 0, lengths, dict(near, x_low=x_low, x_high=x_high), {}, {}, kept)
        layer_out = kept["layer"]
        stored = {name: kept[name] for name in kept_shapes}
        state = step("leave", 0, dict(stored, cotangent=cotangent), back, dict(grad=sheets, totals=sums), dict(sent=sheet), {})
    up = shift(state.pop("sent"), "section", -1)
    state = step(
        "turn", 1, dict(lengths, cotangent=cotangent), dict(near, x=x), tails("tail_heads", "tail_acc"), dict(sent=part),
        dict(state, layer=layer_out),
    )
    layer_out = state["layer"]
    up_low = shift(state["sent"], "section", -1)
    totals = state["totals"]
    state = step(
        "rest", 1, {name: state[name] for name in ("tail_heads", "tail_acc")}, back, {}, dict(sent=part),
        dict(grad=state["grad"]), base=half, span=rows - half,
    )
    up_high = shift(state["sent"], "section", -1)
    state = step("back", 0, stored, dict(back, up=up), {}, {}, dict(grad=state["grad"], totals=totals))
    grad = state["grad"]
    state = step(
        "back part", 1, stored, dict(back, up=up_low), dict(acc_part=((half, width), f32)), {}, dict(totals=state["totals"]),
        span=half,
    )
    state = step(
        "back whole", 1, dict(stored, acc_part=state["acc_part"]), dict(back, up=up_high), {}, {},
        dict(grad=grad, totals=state["totals"]), base=half, span=rows - half,
    )
    totals = sum_parts(add_over(state["totals"], "dp"), [2 * width, width, width, hidden, width, width])
    return (layer_out[None, :, None], state["grad"][None, :, None], *totals)


def solution(mesh):
    in_specs = (
        P(None, "dp", None, None), P(None, "dp", None), P(None, "dp", None, None),
        P("section", None, None), P("section", None, None), P("section", None, None), P("section", None, None),
    ) + (P("section", None),) * 8
    out_specs = (P("section", None, "dp", None, None),) * 2 + (P("section", None),) * 6
    return jax.shard_map(body, mesh=mesh, in_specs=in_specs, out_specs=out_specs, check_vma=False)
```

```python
import functools
import math
import types
import jax
import jax.numpy as jnp
from jax import lax
from jax.experimental import pallas as pl
from jax.experimental.pallas import tpu as pltpu
from jax.sharding import PartitionSpec as P

HEAD_DIM = 64
LANES = 128
GROUP = 256
TILE = 2048
BLOCK = 256
ROWS = 128
PAIRS = 4
LIMITS = {}
LIMIT = 35
epsilon = 1e-05
masked_score = -1000000000.0
root_half = 0.7071067811865476
inverse_root_tau = 0.3989422804014327
f32 = jnp.float32
bf16 = jnp.bfloat16


def dot(left, right):
    return jnp.dot(left, right, preferred_element_type=f32)


def dot_back(left, right):
    return lax.dot_general(left, right, (((1,), (1,)), ((), ())), preferred_element_type=f32)


def beside(*parts):
    return jnp.concatenate(parts, axis=1)


def above(*parts):
    return jnp.concatenate(parts, axis=0)


def column_sum(value):
    return jnp.sum(value, axis=0, keepdims=True)


def row_norm(summed):
    middle = jnp.mean(summed, axis=-1, keepdims=True)
    centered = summed - middle
    inverse = lax.rsqrt(jnp.mean(centered * centered, axis=-1, keepdims=True) + epsilon)
    return centered * inverse, inverse


def row_norm_back(upstream, normed, inverse, gain):
    scaled = upstream * gain
    centered = scaled - jnp.mean(scaled, axis=-1, keepdims=True)
    return inverse * (centered - normed * jnp.mean(scaled * normed, axis=-1, keepdims=True))


def split_three(value):
    high = value.astype(bf16).astype(f32)
    rest = value - high
    middle = rest.astype(bf16).astype(f32)
    return high, middle, rest - middle


def spread(value):
    lane = lax.broadcasted_iota(jnp.int32, value.shape, 1)
    high, middle, low = split_three(value)
    return jnp.where(lane < 16, high, jnp.where(lane < 32, middle, low)).astype(bf16)


def strip(index, size):
    return pl.ds(pl.multiple_of(index * size, size), size)


class Copies:
    def __init__(self, semaphores):
        self.semaphores = semaphores
        self.used = 0

    def take(self, count=1):
        self.used += count
        return self.used - count

    def make(self, source, target, place=None):
        place = self.take() if place is None else place
        return pltpu.make_async_copy(source, target, self.semaphores.at[place])

    def start(self, source, target):
        return self.start_at(source, target, self.take())

    def start_at(self, source, target, place):
        copy = self.make(source, target, place)
        copy.start()
        return copy


def any_space(count):
    return [pl.BlockSpec(memory_space=pl.ANY)] * count


PARAMS = (
    "qkv", "out", "ff1", "ff2", "first_gain", "second_gain", "qv_bias", "out_bias", "first_shift", "ff1_bias", "ff2_bias",
    "second_shift",
)
KEPT = ("heads", "context", "shares", "weights", "one", "one_inverse", "slope", "two", "two_inverse")


def resident_of(width, hidden):
    groups, tiles = width // GROUP, hidden // TILE
    shapes = {
        "qkv": ((groups, width, 3 * width // groups), bf16),
        "out": ((width, width), bf16),
        "ff1": ((tiles, width, TILE), bf16),
        "ff2": ((tiles, TILE, width), bf16),
    }
    lengths = {"qv_bias": 3 * width, "ff1_bias": hidden}
    return shapes | {name: ((1, lengths.get(name, width)), f32) for name in PARAMS[4:]}


def scratch_of(rows, width, hidden):
    tiles = hidden // TILE
    return {
        "acc": ((rows, width), f32),
        "low": ((rows, width), bf16),
        "heads": ((rows, 3 * width), bf16),
        "context": ((rows, width), bf16),
        "shares": ((rows, LANES), f32),
        "weights": ((width // HEAD_DIM, rows, rows), bf16),
        "one": ((rows, width), f32),
        "one_inverse": ((rows, LANES), f32),
        "slope": ((tiles, rows, TILE), bf16),
        "two": ((rows, width), bf16),
        "two_inverse": ((rows, LANES), f32),
        "grad_marks": ((rows, LANES), bf16),
        "totals": ((1, 6 * width + hidden), f32),
    }


class Layer:
    def __init__(self, hbm, vmem, semaphores, slot, base, span, keeping):
        self.hbm, self.vmem = hbm, vmem
        self.slot, self.base, self.span = slot, base, span
        self.keeping = keeping
        self.value = vmem.value if hasattr(vmem, "value") else getattr(vmem, "sent", None)
        self.copies = Copies(semaphores)
        self.groups, self.width, self.part = vmem.qkv.shape
        self.tiles = vmem.ff1.shape[0] if hasattr(vmem, "ff1") else 0
        self.qkv_place = self.copies.take(self.groups)
        self.out_place = self.copies.take()
        self.ff_place = self.copies.take(2 * self.tiles)
        self.small_place = self.copies.take(9)
        self.loading = hasattr(hbm, "qkv")
        self.kept_place = self.copies.take(len(KEPT))
        self.slope_place = self.copies.take(self.tiles)
        self.row_place = self.copies.take(2 * (span // ROWS))

    def qkv_copy(self, g):
        part = self.vmem.qkv.shape[2]
        return self.copies.make(self.hbm.qkv.at[:, strip(g, part)], self.vmem.qkv.at[g], self.qkv_place + g)

    def out_copy(self):
        return self.copies.make(self.hbm.out, self.vmem.out, self.out_place)

    def ff1_copy(self, t):
        return self.copies.make(self.hbm.ff1.at[:, strip(t, TILE)], self.vmem.ff1.at[t], self.ff_place + 2 * t)

    def ff2_copy(self, t):
        return self.copies.make(self.hbm.ff2.at[strip(t, TILE)], self.vmem.ff2.at[t], self.ff_place + 2 * t + 1)

    def small_copies(self):
        copies = []
        for name in PARAMS[4:]:
            source, target = getattr(self.hbm, name), getattr(self.vmem, name)
            if name == "qv_bias":
                copies.append((source.at[:, : self.width], target.at[:, : self.width]))
                copies.append((source.at[:, self.width :], target.at[:, 2 * self.width :]))
            else:
                copies.append((source, target))
        return [self.copies.make(*pair, self.small_place + index) for index, pair in enumerate(copies)]

    def start_weights(self):
        for g in range(self.groups):
            self.qkv_copy(g).start()
            if g == 0:
                for copy in self.small_copies():
                    copy.start()
        self.out_copy().start()
        for t in range(self.tiles):
            self.ff1_copy(t).start()
            self.ff2_copy(t).start()
        self.vmem.qv_bias[:, self.width : 2 * self.width] = jnp.zeros((1, self.width), f32)

    def wait_qkv(self, g):
        if self.loading:
            self.qkv_copy(g).wait()

    def wait_out(self):
        if self.loading:
            self.out_copy().wait()

    def wait_feed(self, t):
        if self.loading:
            self.ff1_copy(t).wait()
            self.ff2_copy(t).wait()

    def wait_small(self):
        if self.loading:
            for copy in self.small_copies():
                copy.wait()

    def wait_weights(self):
        self.wait_small()
        self.wait_out()
        for g in range(self.groups):
            self.wait_qkv(g)
        for t in range(self.tiles):
            self.wait_feed(t)

    def kept_copy(self, name, back):
        there, here = getattr(self.hbm, "kept_" + name).at[self.slot], getattr(self.vmem, name)
        if here.shape[0] == self.span:
            there = there.at[pl.ds(self.base, self.span)]
        place = self.kept_place + KEPT.index(name)
        return self.copies.make(there, here, place) if back else self.copies.make(here, there, place)

    def slope_copy(self, t, back):
        there, here = self.hbm.kept_slope.at[self.slot, t, pl.ds(self.base, self.span)], self.vmem.slope.at[t]
        return self.copies.make(there, here, self.slope_place + t) if back else self.copies.make(here, there, self.slope_place + t)

    def row_copy(self, name, target, index, size, part):
        here = (self.value if name == "sent" else getattr(self.vmem, name)).at[strip(index, size)]
        there = getattr(self.hbm, target).at[self.slot, pl.ds(self.base + pl.multiple_of(index * size, size), size)]
        return self.copies.make(here, there, self.row_place + 2 * index + part)

    def layer_copy(self, index):
        return self.row_copy("sent", "layer", index, ROWS, 0)

    def two_copy(self, index):
        return self.row_copy("two", "kept_two", index, ROWS, 1)

    def grad_copy(self, index):
        return self.row_copy("sent", "grad", index, BLOCK, 0)

    def keep(self, *names):
        if self.keeping:
            for name in names:
                self.kept_copy(name, False).start()

    def await_kept(self, back, *names):
        if self.keeping:
            for name in names:
                self.kept_copy(name, back).wait()

    def some_rows(self, ref):
        return ref if ref.shape[0] == self.span else ref.at[pl.ds(self.base, self.span)]

    def attend_forward(self):
        hbm, vmem, slot = self.hbm, self.vmem, self.slot
        width, groups, part = self.width, self.groups, self.part
        rows = vmem.heads.shape[0]
        segments = hbm.lengths.shape[2]
        lengths_copy = self.copies.start(hbm.lengths, vmem.lengths)

        def own_marks(start, count):
            place = start + lax.broadcasted_iota(jnp.int32, (count, LANES), 0)
            label = jnp.zeros((count, LANES), jnp.int32)
            end = jnp.int32(0)
            for index in range(segments):
                end = end + vmem.lengths[slot, 0, index]
                label = label + jnp.where(place >= end, 1, 0)
            lane = lax.broadcasted_iota(jnp.int32, (count, LANES), 1)
            return jnp.where(lane == label, 1.0, 0.0), lane

        self.wait_small()
        if self.x_copy is not None:
            self.x_copy.wait()

        def project(g, carry):
            self.wait_qkv(g)
            columns = strip(g, part)
            vmem.heads[:, columns] = (dot(vmem.x[...], vmem.qkv[g]) + vmem.qv_bias[:, columns]).astype(bf16)
            return carry

        lax.fori_loop(0, groups, project, 0)
        self.keep("heads")
        lengths_copy.wait()
        own, lane = own_marks(0, rows)
        key_mark = jnp.where(lane < segments, (1.0 - own) * masked_score, 0.0).astype(bf16)
        query_mark = own.astype(bf16)
        clear(vmem.shares)
        half = lane < HEAD_DIM
        zero = jnp.zeros((rows, LANES), bf16)
        ones = jnp.ones((rows, LANES), bf16)
        head_lane = jnp.where(lane < 48, lane & 15, -1)

        def head_step(step, carry):
            count = 2 * PAIRS
            queries, keys, values = (
                vmem.heads[:, pl.ds(pl.multiple_of(at * width + step * PAIRS * LANES, LANES), PAIRS * LANES)] for at in range(3)
            )
            mixes = []

            def score(local):
                pair, side = divmod(local, 2)
                chosen = slice(pair * LANES, (pair + 1) * LANES)
                scaled = queries[:, chosen] * jnp.asarray(HEAD_DIM**-0.5, bf16)
                left = jnp.where(half if side == 0 else ~half, scaled, zero)
                return dot_back(beside(left, query_mark), beside(keys[:, chosen], key_mark))

            scores = score(0)
            for local in range(count):
                following = score(local + 1) if local + 1 < count else None
                chosen = slice(local // 2 * LANES, (local // 2 + 1) * LANES)
                top = jnp.max(scores, axis=-1, keepdims=True)
                weights = jnp.exp(scores - top).astype(bf16)
                vmem.weights[step * count + local] = weights
                mixes.append(dot(weights, beside(values[:, chosen], ones)))
                scores = following
            keep = vmem.shares[...]
            parts = []
            for local in range(count):
                share = 1.0 / mixes[local][:, LANES:]
                parts.append(mixes[local][:, :LANES] * share)
                keep = jnp.where(head_lane == step * count + local, share, keep)
            vmem.shares[...] = keep
            mixed = beside(*[jnp.where(half, parts[2 * p], parts[2 * p + 1]) for p in range(PAIRS)])
            vmem.context[:, strip(step, PAIRS * LANES)] = mixed.astype(bf16)
            return carry

        lax.fori_loop(0, width // (PAIRS * LANES), head_step, 0)
        self.keep("context", "shares", "weights")
        self.wait_out()

        def first_norm(index, carry):
            rows_ = strip(index, BLOCK)
            summed = vmem.x[rows_, :].astype(f32) + vmem.out_bias[...] + dot(vmem.context[rows_, :], vmem.out[...])
            one, one_inverse = row_norm(summed)
            vmem.one[rows_, :] = one
            vmem.one_inverse[rows_, :] = jnp.broadcast_to(one_inverse, (one.shape[0], LANES))
            value = one * vmem.first_gain[...] + vmem.first_shift[...]
            vmem.low[rows_, :] = value.astype(bf16)
            vmem.acc[rows_, :] = value + vmem.ff2_bias[...]
            return carry

        lax.fori_loop(0, rows // BLOCK, first_norm, 0)
        self.keep("one", "one_inverse")

    def feed_forward(self):
        vmem, span, tiles = self.vmem, self.span, self.tiles
        low, acc = self.some_rows(vmem.low), self.some_rows(vmem.acc)

        def tile_step(t, carry):
            self.wait_feed(t)
            bias = vmem.ff1_bias[:, strip(t, TILE)]
            acts = []
            for c in range(TILE // BLOCK):
                columns = slice(c * BLOCK, (c + 1) * BLOCK)
                h = dot(low[...], vmem.ff1[t, :, columns]) + bias[:, columns]
                share = 0.5 + 0.5 * lax.erf(h * root_half)
                vmem.slope[t, :, columns] = (share + h * jnp.exp(h * h * -0.5) * inverse_root_tau).astype(bf16)
                acts.append((h * share).astype(bf16))
            acc[...] += dot(beside(*acts), vmem.ff2[t])
            if self.keeping:
                self.slope_copy(t, False).start()
            return carry

        lax.fori_loop(0, tiles, tile_step, 0)

        def second_norm(index, carry):
            rows_ = strip(index, ROWS)
            two, two_inverse = row_norm(acc[rows_, :])
            self.value[rows_, :] = (two * vmem.second_gain[...] + vmem.second_shift[...]).astype(bf16)
            vmem.two[rows_, :] = two.astype(bf16)
            vmem.two_inverse[rows_, :] = jnp.broadcast_to(two_inverse, (ROWS, LANES))
            self.layer_copy(index).start()
            if self.keeping:
                self.two_copy(index).start()
            return carry

        lax.fori_loop(0, span // ROWS, second_norm, 0)
        self.keep("two_inverse")

    def finish_forward(self, *names):
        self.await_kept(False, *names)
        for index in range(self.span // ROWS):
            self.layer_copy(index).wait()
            if self.keeping:
                self.two_copy(index).wait()
        if self.keeping:
            for t in range(self.tiles):
                self.slope_copy(t, False).wait()

    def fetch_feed(self):
        for name in ("two", "two_inverse"):
            self.kept_copy(name, True).start()
        for t in range(self.tiles):
            self.slope_copy(t, True).start()

    def fetch_attend(self):
        for name in ("one", "one_inverse", "context", "shares", "heads", "weights"):
            self.kept_copy(name, True).start()

    def feed_backward(self):
        vmem, base, span = self.vmem, self.base, self.span
        width, tiles = self.width, self.tiles
        at_ff1 = 4 * width
        at_ff2 = at_ff1 + tiles * TILE
        at_second = at_ff2 + width
        totals, low = vmem.totals, vmem.low
        acc = self.some_rows(vmem.acc)
        self.await_kept(True, "two", "two_inverse")

        def second_back(index, carry):
            rows_ = strip(index, ROWS)
            upstream = vmem.up[rows_, :].astype(f32)
            grad = row_norm_back(upstream, vmem.two[rows_, :].astype(f32), vmem.two_inverse[rows_, :1], vmem.second_gain[...])
            low[rows_, :] = grad.astype(bf16)
            acc[rows_, :] = grad
            totals[:, at_second : at_second + width] += column_sum(upstream)
            totals[:, at_ff2 : at_ff2 + width] += column_sum(grad.astype(bf16).astype(f32))
            return carry

        lax.fori_loop(0, span // ROWS, second_back, 0)

        def tile_step(t, carry):
            if self.keeping:
                self.slope_copy(t, True).wait()
            grads, sums = [], []
            for c in range(TILE // BLOCK):
                columns = slice(c * BLOCK, (c + 1) * BLOCK)
                h = (dot_back(low[...], vmem.ff2[t, columns, :]) * vmem.slope[t, :, columns].astype(f32)).astype(bf16)
                sums.append(column_sum(h.astype(f32)))
                grads.append(h)
            totals[:, pl.ds(pl.multiple_of(at_ff1 + t * TILE, TILE), TILE)] += beside(*sums)
            acc[...] += dot_back(beside(*grads), vmem.ff1[t])
            return carry

        lax.fori_loop(0, tiles, tile_step, 0)

    def attend_backward(self):
        vmem, width, groups = self.vmem, self.width, self.groups
        rows = vmem.heads.shape[0]
        totals, acc = vmem.totals, vmem.acc
        at_out, at_first = 2 * width, 3 * width
        self.await_kept(True, "one", "one_inverse", "context", "shares")

        def first_back(index, carry):
            rows_ = strip(index, BLOCK)
            first_grad = acc[rows_, :]
            totals[:, at_first : at_first + width] += column_sum(first_grad)
            summed = row_norm_back(first_grad, vmem.one[rows_, :], vmem.one_inverse[rows_, :1], vmem.first_gain[...])
            acc[rows_, :] = summed
            attend_grad = summed.astype(bf16)
            totals[:, at_out : at_out + width] += column_sum(attend_grad.astype(f32))
            shares = spread(vmem.shares[rows_, :])
            context_grad = (dot_back(attend_grad, vmem.out[...]) * dot_back(shares, pick)).astype(bf16)
            product = context_grad.astype(f32) * vmem.context[rows_, :].astype(f32)
            upper = product.astype(bf16)
            inner = dot(upper, pick) + dot((product - upper.astype(f32)).astype(bf16), pick)
            vmem.grad_marks[rows_, :] = spread(inner)
            vmem.context[rows_, :] = context_grad
            return carry

        which = lax.broadcasted_iota(jnp.int32, (width, LANES), 0) // HEAD_DIM
        spot = lax.broadcasted_iota(jnp.int32, (width, LANES), 1)
        pick = jnp.where(((spot & 15) == which) & (spot < 48), 1.0, 0.0).astype(bf16)
        lax.fori_loop(0, rows // BLOCK, first_back, 0)
        lane = lax.broadcasted_iota(jnp.int32, (rows, LANES), 1)
        half = lane < HEAD_DIM
        zero = jnp.zeros((rows, LANES), bf16)
        local_lane = jnp.where(lane < 48, lane & 15, -1)
        self.await_kept(True, "heads", "weights")
        scale = HEAD_DIM**-0.5
        grad_mark = vmem.grad_marks[...]

        def head_step(step, carry):
            size = PAIRS * LANES
            spans = [pl.ds(pl.multiple_of(at * width + step * size, LANES), size) for at in range(3)]
            queries, all_keys, all_values = (vmem.heads[:, span] for span in spans)
            grads = vmem.context[:, strip(step, size)]
            query_grads, key_grads, value_grads = [], [], []
            for pair in range(PAIRS):
                chosen = slice(pair * LANES, (pair + 1) * LANES)
                query = queries[:, chosen] * jnp.asarray(scale, bf16)
                keys = all_keys[:, chosen]
                values = all_values[:, chosen]
                upper_grad = grads[:, chosen]
                query_turned = query.T
                grad_turned = upper_grad.T
                score_grads, keys_kept, key_turned, value_turned = [], [], [], []
                for side in range(2):
                    ours = half if side == 0 else ~half
                    mine = slice(side * HEAD_DIM, (side + 1) * HEAD_DIM)
                    head = step * 2 * PAIRS + pair * 2 + side
                    weights = vmem.weights[head]
                    right = beside(values, jnp.where(local_lane == head, -1.0, 0.0).astype(bf16))
                    score_grad = (weights.astype(f32) * dot_back(beside(jnp.where(ours, upper_grad, zero), grad_mark), right)).astype(bf16)
                    value_turned.append(dot(grad_turned[mine], weights).astype(bf16))
                    key_turned.append(dot(query_turned[mine], score_grad).astype(bf16))
                    score_grads.append(score_grad)
                    keys_kept.append(jnp.where(ours, keys, zero))
                key_grads.append(above(*key_turned).T)
                value_grads.append(above(*value_turned).T)
                query_grads.append((dot(beside(*score_grads), above(*keys_kept)) * scale).astype(bf16))
            query_grad, key_grad, value_grad = beside(*query_grads), beside(*key_grads), beside(*value_grads)
            for span, grad in zip(spans, (query_grad, key_grad, value_grad)):
                vmem.heads[:, span] = grad
            totals[:, strip(step, size)] += column_sum(query_grad.astype(f32))
            totals[:, pl.ds(pl.multiple_of(width + step * size, LANES), size)] += column_sum(value_grad.astype(f32))
            return carry

        lax.fori_loop(0, width // (PAIRS * LANES), head_step, 0)
    def input_grad(self, storing):
        vmem, base, span, part = self.vmem, self.base, self.span, self.part
        self.value = vmem.sent
        shift_by = base if vmem.acc.shape[0] != span else 0

        def input_step(index, carry):
            found = vmem.acc[pl.ds(shift_by + pl.multiple_of(index * BLOCK, BLOCK), BLOCK), :]
            rows_ = pl.ds(shift_by + pl.multiple_of(index * BLOCK, BLOCK), BLOCK)
            for g in range(self.groups):
                found = found + dot_back(vmem.heads[rows_, g * part : (g + 1) * part], vmem.qkv[g])
            vmem.sent[strip(index, BLOCK), :] = found.astype(bf16)
            if storing:
                self.grad_copy(index).start()
            return carry

        lax.fori_loop(0, span // BLOCK, input_step, 0)
        if storing:
            for index in range(span // BLOCK):
                self.grad_copy(index).wait()


def clear(ref):
    ref[...] = jnp.zeros_like(ref)


EVERY = False


def step_kernel(stage, slot, base, span, names, *refs):
    refs = dict(zip(names, refs))
    hbm = types.SimpleNamespace(**{name[4:]: ref for name, ref in refs.items() if name.startswith("hbm ")})
    vmem = types.SimpleNamespace(**{name[5:]: ref for name, ref in refs.items() if name.startswith("vmem ")})
    in_first = lax.axis_index("section") == 0
    working = jnp.logical_not(in_first) if stage in SECOND else in_first
    layer = Layer(hbm, vmem, refs["semaphores"], slot, base, span, stage != "turn")
    copies = layer.copies

    @pl.when(working)
    def _():
        earlier = []
        if hasattr(vmem, "sent_before"):
            place = pl.ds(0, vmem.sent_before.shape[0])
            earlier.append(copies.start(vmem.sent_before, hbm.grad.at[slot if stage == "rest" else slot - 1, place]))
        if stage in ("open", "ahead", "enter", "turn"):
            layer.x_copy = None
            if stage in ("open", "ahead"):
                layer.x_copy = copies.start(hbm.tokens.at[slot, 0], vmem.x)
            elif hasattr(vmem, "x_low"):
                count = vmem.x_low.shape[0]
                vmem.x[:count, :] = vmem.x_low[...]
                vmem.x[count:, :] = vmem.x_high[...]
            if layer.loading:
                layer.start_weights()
            if stage == "turn":
                before = None if slot == 0 else copies.start(hbm.totals, vmem.totals)
                up_copy = copies.start(hbm.cotangent.at[slot, 0], vmem.up)
            layer.attend_forward()
            later = []
            if stage == "open":
                rest = pl.ds(span, vmem.acc.shape[0] - span)
                later.append(copies.start(vmem.low.at[rest], hbm.more_low))
                later.append(copies.start(vmem.acc.at[rest], hbm.more_acc))
            layer.feed_forward()
            if stage != "turn":
                layer.finish_forward("heads", "context", "shares", "weights", "one", "one_inverse", "two_inverse")
            for copy in later:
                copy.wait()
        elif stage == "more":
            fetched = [copies.start(hbm.more_low, vmem.low), copies.start(hbm.more_acc, vmem.acc)]
            for copy in fetched:
                copy.wait()
            layer.feed_forward()
            layer.finish_forward("two_inverse")
        elif stage == "rest":
            fetched = [copies.start(hbm.tail_heads, vmem.heads), copies.start(hbm.tail_acc, vmem.acc)]
            for copy in fetched:
                copy.wait()
            layer.input_grad(True)
        if stage in ("leave", "turn", "back", "back part", "back whole"):
            if stage != "turn":
                before = None if slot == 0 else copies.start(hbm.totals, vmem.totals)
                up_copy = copies.start(hbm.cotangent.at[slot, 0], vmem.up) if stage == "leave" else None
                layer.fetch_feed()
                if stage == "back whole":
                    acc_copy = copies.start(hbm.acc_part, vmem.acc.at[pl.ds(0, base)])
                if stage != "back part":
                    layer.fetch_attend()
            if before is None:
                clear(vmem.totals)
            else:
                before.wait()
            if up_copy is not None:
                up_copy.wait()
            layer.feed_backward()
            if stage == "back whole":
                acc_copy.wait()
            if stage != "back part":
                layer.attend_backward()
            if stage == "turn":
                layer.finish_forward()
            after = [copies.start(vmem.totals, hbm.totals)]
            if stage == "back part":
                after.append(copies.start(vmem.acc, hbm.acc_part))
            else:
                if stage == "turn" and vmem.sent.shape[0] < vmem.acc.shape[0]:
                    layer.base, layer.span = 0, vmem.sent.shape[0]
                    tail = pl.ds(layer.span, vmem.acc.shape[0] - layer.span)
                    after.append(copies.start(vmem.heads.at[tail], hbm.tail_heads))
                    after.append(copies.start(vmem.acc.at[tail], hbm.tail_acc))
                elif stage == "back whole":
                    layer.base, layer.span = 0, vmem.acc.shape[0]
                layer.input_grad(stage != "turn")
            for copy in after:
                copy.wait()
        for copy in earlier:
            copy.wait()

    if layer.loading:
        @pl.when(jnp.logical_not(working))
        def _():
            layer.start_weights()
            layer.wait_weights()


FLOPS = 10**6
SECOND = ("enter", "leave", "turn", "rest")


def run(stage, slot, inputs, near, outputs, near_outputs, changed, rows, width, hidden, base=0, span=None):
    span = rows if span is None else span
    full, some = scratch_of(rows, width, hidden), scratch_of(span, width, hidden)
    feeding = ("slope", "two", "two_inverse")
    mixed = {name: some[name] if name in feeding else full[name] for name in full}
    if stage in ("open", "ahead", "enter"):
        scratch = {name: mixed[name] for name in mixed if name not in ("grad_marks", "totals")}
    elif stage == "more":
        scratch = {name: some[name] for name in ("acc", "low", *feeding)}
    elif stage == "rest":
        scratch = {name: some[name] for name in ("heads", "acc")}
    elif stage == "back part":
        scratch = {name: some[name] for name in ("acc", "low", "totals", *feeding)}
    else:
        scratch = dict(mixed, low=some["low"])
    if stage in ("open", "ahead", "enter", "turn"):
        scratch["x"] = ((rows, width), bf16)
    if "lengths" in inputs:
        scratch["lengths"] = (inputs["lengths"].shape, jnp.int32)
    if stage in ("leave", "turn"):
        scratch["up"] = ((rows, width), bf16)
    if stage == "turn":
        scratch["value"] = ((rows, width), bf16)
    if stage != "back part":
        scratch["sent"] = ((rows, width), bf16)
    scratch = {name: shape for name, shape in scratch.items() if name not in near and name not in near_outputs}
    names = ["hbm " + name for name in inputs] + ["vmem " + name for name in near]
    names += ["hbm " + name + "_before" for name in changed]
    names += ["hbm " + name for name in outputs] + ["vmem " + name for name in near_outputs]
    names += ["hbm " + name for name in changed] + ["vmem " + name for name in scratch] + ["semaphores"]
    close = pl.BlockSpec(memory_space=pltpu.VMEM)
    specs = any_space(len(inputs))
    held = [pltpu.with_memory_space_constraint(item, pltpu.VMEM) for item in near.values()]
    first_changed, first_out = len(inputs) + len(near), len(outputs) + len(near_outputs)
    outs = pl.pallas_call(
        functools.partial(step_kernel, stage, slot, base, span, names),
        in_specs=specs + [close] * len(near) + any_space(len(changed)),
        out_specs=any_space(len(outputs)) + [close] * len(near_outputs) + any_space(len(changed)),
        out_shape=[jax.ShapeDtypeStruct(*shape) for shape in outputs.values()]
        + [pltpu.VMEM(*shape) for shape in near_outputs.values()]
        + [jax.ShapeDtypeStruct(item.shape, item.dtype) for item in changed.values()],
        input_output_aliases={first_changed + i: first_out + i for i in range(len(changed))},
        scratch_shapes=[(pltpu.SMEM if name == "lengths" else pltpu.VMEM)(*shape) for name, shape in scratch.items()] + [pltpu.SemaphoreType.DMA((96,))],
        compiler_params=pltpu.CompilerParams(vmem_limit_bytes=LIMITS.get(stage, LIMIT) * 2**20),
        cost_estimate=pl.CostEstimate(flops=FLOPS, bytes_accessed=2**16, transcendentals=0),
        name=f"{stage}_{slot}".replace(" ", "_"),
    )(*inputs.values(), *held, *changed.values())
    return dict(zip([*outputs, *near_outputs, *changed], outs))


def shift(value, axis, steps):
    count = lax.axis_size(axis)
    pairs = [(place, place + steps) for place in range(max(0, -steps), min(count, count - steps))]
    return lax.ppermute(value, axis, pairs)


def add_over(value, axis):
    count = lax.axis_size(axis)
    if count & (count - 1):
        return [lax.psum(value, axis)]

    def far(value, mask):
        return lax.ppermute(value, axis, [(place, place ^ mask) for place in range(count)])

    step = 1
    while 4 * step < count:
        value = (value + far(value, step)) + (far(value, 2 * step) + far(value, 3 * step))
        step *= 4
    if 2 * step < count:
        return [value, far(value, step), far(value, 2 * step), far(value, 3 * step)]
    return [value, far(value, step)] if step < count else [value]


def sum_parts(values, sizes):
    def kernel(*refs):
        parts = [ref[...] for ref in refs[: len(values)]]
        while len(parts) > 1:
            parts = [one + two for one, two in zip(parts[::2], parts[1::2])]
        at = 0
        for ref in refs[len(values) :]:
            ref[...] = parts[0][:, at : at + ref.shape[1]]
            at += ref.shape[1]

    return pl.pallas_call(kernel, out_shape=[jax.ShapeDtypeStruct((1, size), f32) for size in sizes], name="sums")(*values)


def body(tokens, doc_lengths, cotangent, *params):
    params = dict(zip(PARAMS, (item[0] if item.ndim == 3 else item for item in params)))
    micro, _, rows, width = tokens.shape
    hidden = params["ff1"].shape[1]
    scratch = scratch_of(rows, width, hidden)
    step = functools.partial(run, rows=rows, width=width, hidden=hidden)
    sheet = ((rows, width), bf16)
    sheets = ((micro, rows, width), bf16)
    kept_shapes = {"kept_" + name: ((micro,) + scratch[name][0], scratch[name][1]) for name in KEPT}
    lengths = dict(lengths=doc_lengths)
    resident = resident_of(width, hidden)
    half = rows // 2
    part, sums = ((half, width), bf16), ((1, 6 * width + hidden), f32)
    kept_names = [*kept_shapes, "layer"]

    def tails(*names):
        shapes = {"low": (width, bf16), "acc": (width, f32), "heads": (3 * width, bf16)}
        return {name: ((rows - half, shapes[name.split("_")[1]][0]), shapes[name.split("_")[1]][1]) for name in names}

    done = step(
        "open", 0, dict(lengths, tokens=tokens, **params), {}, dict(kept_shapes, layer=sheets, **tails("more_low", "more_acc")),
        dict(resident, sent=part), {}, span=half,
    )
    near = {name: done[name] for name in PARAMS}
    back = {name: near[name] for name in PARAMS[:6]}
    x_low = shift(done["sent"], "section", 1)
    done = step(
        "more", 0, {name: done[name] for name in ("more_low", "more_acc")}, near, {}, dict(sent=part),
        {name: done[name] for name in kept_names}, base=half, span=rows - half,
    )
    x_high = shift(done["sent"], "section", 1)
    x_low, layer = lax.optimization_barrier((x_low, done["layer"]))
    done = step(
        "ahead", 1, dict(lengths, tokens=tokens), near, {}, dict(sent=sheet),
        dict({name: done[name] for name in kept_names}, layer=layer),
    )
    x = shift(done["sent"], "section", 1)
    kept = {name: done[name] for name in kept_names}

    stored = {name: kept[name] for name in kept_shapes}
    state = step(
        "turn", 0, dict(lengths, cotangent=cotangent), dict(near, x_low=x_low, x_high=x_high), dict(grad=sheets, totals=sums),
        dict(sent=sheet), dict(layer=kept["layer"]),
    )
    layer_out = state.pop("layer")
    first_sent = state["sent"]
    up = shift(state.pop("sent"), "section", -1)
    state = step(
        "turn", 1, dict(lengths, cotangent=cotangent), dict(near, x=x, sent_before=first_sent), tails("tail_heads", "tail_acc"),
        dict(sent=part),
        dict(state, layer=layer_out),
    )
    layer_out = state["layer"]
    up_low = shift(state["sent"], "section", -1)
    totals = state["totals"]
    state = step(
        "rest", 1, {name: state[name] for name in ("tail_heads", "tail_acc")}, dict(back, sent_before=state["sent"]), {}, dict(sent=part),
        dict(grad=state["grad"]), base=half, span=rows - half,
    )
    up_high = shift(state["sent"], "section", -1)
    state = step("back", 0, stored, dict(back, up=up), {}, {}, dict(grad=state["grad"], totals=totals))
    grad = state["grad"]
    state = step(
        "back part", 1, stored, dict(back, up=up_low), dict(acc_part=((half, width), f32)), {}, dict(totals=state["totals"]),
        span=half,
    )
    state = step(
        "back whole", 1, dict(stored, acc_part=state["acc_part"]), dict(back, up=up_high), {}, {},
        dict(grad=grad, totals=state["totals"]), base=half, span=rows - half,
    )
    totals = sum_parts(add_over(state["totals"], "dp"), [2 * width, width, width, hidden, width, width])
    return (layer_out[None, :, None], state["grad"][None, :, None], *totals)


def solution(mesh):
    in_specs = (
        P(None, "dp", None, None), P(None, "dp", None), P(None, "dp", None, None),
        P("section", None, None), P("section", None, None), P("section", None, None), P("section", None, None),
    ) + (P("section", None),) * 8
    out_specs = (P("section", None, "dp", None, None),) * 2 + (P("section", None),) * 6
    return jax.shard_map(body, mesh=mesh, in_specs=in_specs, out_specs=out_specs, check_vma=False)
```
